32 devices in a mesh: dp: 4 (over z), tensor: 4 (over y, x), shard: 2 (over core).
Axes of the slice: x: 2, y: 2, z: 4, core: 2. Of those that a mesh axis runs over, the one named last changes fastest.
Arguments:
- tokens: bfloat16 [8192, 768], P(('dp', 'shard')), may hold values from -6 to 6
- segment_ids: int32 [8, 1024], P(('dp', 'shard')), may hold values from 0 to 7, never falling along the last dimension, each value on 1 to 800 neighbouring positions
- buckets: int32 [2047], replicated, may hold values from 0 to 31, as said below
- routes: int32 [8192], P(('dp', 'shard')), may hold values from 0 to 3, as said below
- kept: int32 [8192], P(('dp', 'shard')), may hold values from 0 to 1, as said below
- slots: int32 [8192], P(('dp', 'shard')), may hold values from 0 to 319, as said below
- cotangent: bfloat16 [8192, 768], P(('dp', 'shard')), may hold values from -6 to 6
- norm_one: bfloat16 [768], P('shard'), may hold values from 0.25 to 1.75
- norm_two: bfloat16 [768], P('shard'), may hold values from 0.25 to 1.75
- qkv_weight: bfloat16 [768, 3, 768], P('shard', None, 'tensor'), may hold values from -0.21875 to 0.21875
- out_weight: bfloat16 [768, 768], P('tensor', 'shard'), may hold values from -0.875 to 0.875
- bias_table: bfloat16 [12, 32], P('tensor', 'shard'), may hold values from -4 to 4
- router_weight: bfloat16 [768, 4], P('shard'), may hold values from -0.15625 to 0.15625
- expert_in: bfloat16 [4, 768, 3072], P('dp', 'shard', 'tensor'), may hold values from -0.21875 to 0.21875
- expert_out: bfloat16 [4, 3072, 768], P('dp', 'tensor', 'shard'), may hold values from -0.4375 to 0.4375
Outputs:
- output: bfloat16 [8192, 768], P(('dp', 'shard'))
- grad_tokens: float32 [8192, 768], P(('dp', 'shard'))
- grad_norm_one: float32 [768], P('shard')
- grad_norm_two: float32 [768], P('shard')
- grad_qkv: float32 [768, 3, 768], P('shard', None, 'tensor')
- grad_out_weight: float32 [768, 768], P('tensor', 'shard')
- grad_table: float32 [12, 32], P('tensor', 'shard')
- grad_router: float32 [768, 4], P('shard')
- grad_expert_in: float32 [4, 768, 3072], P('dp', 'shard', 'tensor')
- grad_expert_out: float32 [4, 3072, 768], P('dp', 'tensor', 'shard')
The draws below stay inside these ranges and needn't reach their ends.
Inputs may be any that keep to these rules, and one draw needn't show every extreme that they name: `buckets`: bucket of offset d stored at index d + 1023: offset 0 has bucket 0; on each side the bucket does not fall as |d| grows, and 16 is added where d > 0. `routes`: in every device block of 1024 tokens some expert is named by more than 320 tokens. kept[t] is 1 exactly when fewer than 320 earlier tokens of the same device block have the same route. `slots`: for a kept token, the number of earlier tokens of its device block with the same route; 319 for a dropped token.
All inputs are finite; a program needn't handle non-finite values.
Results may differ from the reference program's by a relative error of at most 0.013.
Values may be sent and summed in bfloat16 or wider, within the bound.
No kernel may reach another device: no remote copies, remote signals or barrier semaphores. Data moves between devices by JAX's collectives and lax.ppermute only.
A program may use at most 128 MiB of HBM per device.

```python
import math
import jax
import jax.numpy as jnp
import numpy as np
from jax import lax

D = 768
H = 12
DH = 64
FF = 3072
NB = 32
LEN = 1024
TOK_DEV = 1024
NSEQ = 8
TOKENS = 8192
EXPERTS = 4
CAP = 320


def routing_tables(key):
    first = jax.random.randint(jax.random.fold_in(key, 11), (TOKENS,), 0, EXPERTS)
    second = jax.random.randint(jax.random.fold_in(key, 12), (TOKENS,), 0, EXPERTS)
    order = jax.random.permutation(jax.random.fold_in(key, 13), EXPERTS).astype(jnp.int32)
    place = jnp.arange(TOKENS) % TOK_DEV
    ranked = jnp.where(place <= CAP, 0, jnp.minimum(first, second))
    route = jnp.take(order, ranked).astype(jnp.int32)
    hits = (route.reshape(-1, TOK_DEV)[:, :, None] == jnp.arange(EXPERTS)[None, None, :]).astype(jnp.int32)
    before = jnp.cumsum(hits, axis=1) - hits
    rank = jnp.sum(before * hits, axis=2).reshape(TOKENS)
    keep_flag = (rank < CAP).astype(jnp.int32)
    slot_index = jnp.where(rank < CAP, rank, CAP - 1).astype(jnp.int32)
    return (route, keep_flag, slot_index)


def draw_routes(key, part):
    return routing_tables(key)[0]


def draw_kept(key, part):
    return routing_tables(key)[1]


def draw_slots(key, part):
    return routing_tables(key)[2]


def draw_buckets(key, part):
    key = jax.random.fold_in(key, 21)
    half_count = NB // 2
    exact_count = half_count // 2
    widest = (LEN - 1 - exact_count) // (half_count - exact_count - 1)
    increments = jax.random.randint(key, (half_count - exact_count - 1,), 1, widest + 1)
    edges = exact_count + jnp.cumsum(increments)
    offset = jnp.arange(2 * LEN - 1) - (LEN - 1)
    distance = jnp.abs(offset)
    far_bucket = exact_count + jnp.sum((distance[:, None] >= edges[None, :]).astype(jnp.int32), axis=1)
    near_bucket = jnp.where(distance < exact_count, distance, far_bucket)
    return (near_bucket + jnp.where(offset > 0, half_count, 0)).astype(jnp.int32)


def levels(key, extent, split, least, high):
    loudness = 1.0
    for dim, blocks in split:
        draws = jax.random.uniform(jax.random.fold_in(jax.random.fold_in(key, 6), dim), (blocks,), jnp.float32, least / len(split), high / len(split))
        loudness = loudness * jnp.repeat(jnp.exp(draws), extent[dim] // blocks).reshape((-1,) + (1,) * (len(extent) - 1 - dim))
    return loudness


def length_profile(number_of, total, bound, slope):
    portions = [(1 << 20) // math.isqrt(rank ** slope) + 1 for rank in range(2, number_of + 1)]
    surplus, given = total - bound - (number_of - 1), [1] * (number_of - 1)
    while surplus > 0:
        candidates = [i for i in range(number_of - 1) if given[i] < bound]
        mass, left = sum([portions[i] for i in candidates]), surplus
        for i in candidates:
            more = min(bound - given[i], max(1, left * portions[i] // mass), surplus)
            given[i] = given[i] + more
            surplus = surplus - more
    return np.array([bound] + given)


def uneven_parts(key, count, total, reach, slope):
    if count == 2:
        one = jax.random.randint(key, (), max(1, total - reach), min(reach, total - 1) + 1)
        return jnp.stack([one, total - one])
    sizes = jnp.asarray(length_profile(count, total, reach, slope), jnp.int32)
    twos = (count - 1) // 2
    donor, receiver = sizes[1:1 + 2 * twos:2], sizes[2:2 + 2 * twos:2]
    margin = jnp.minimum(donor - 1, reach - receiver)
    shifted = jax.random.randint(jax.random.fold_in(key, 1), (twos,), 0, 1 << 20) % (margin + 1)
    sizes = sizes.at[1:1 + 2 * twos:2].set(donor - shifted).at[2:2 + 2 * twos:2].set(receiver + shifted)
    return sizes[jax.random.permutation(jax.random.fold_in(key, 2), count)]


def bell_draw(own_key, shape, scale, limit, cuts=(), dtype=jnp.bfloat16):
    entries = scale * jax.random.normal(own_key, shape, jnp.float32)
    if cuts:
        entries = entries * levels(own_key, shape, cuts, -0.22, 0.18)
    return jnp.clip(entries, -limit, limit).astype(dtype)


def setup_inputs(seed: int = 0) -> dict:
    arg_keys = jax.random.split(jax.random.key(seed), 16)
    return {
        "tokens": bell_draw(arg_keys[0], (TOKENS, D), 1.0, 6.0, ((0, 8),)),
        "segment_ids": jax.vmap(lambda own: jnp.searchsorted(jnp.cumsum(uneven_parts(own, max(2, LEN // 128), LEN, LEN * 25 // 32, 1)), jnp.arange(LEN), side="right"))(jax.random.split(arg_keys[1], NSEQ)).reshape((NSEQ, LEN)).astype(jnp.int32),
        "buckets": draw_buckets(jax.random.fold_in(arg_keys[15], 71), 0),
        "routes": draw_routes(jax.random.fold_in(arg_keys[15], 71), 0),
        "kept": draw_kept(jax.random.fold_in(arg_keys[15], 71), 0),
        "slots": draw_slots(jax.random.fold_in(arg_keys[15], 71), 0),
        "cotangent": bell_draw(arg_keys[6], (TOKENS, D), 1.0, 6.0, ((0, 8),)),
        "norm_one": jnp.clip(1.0 + 0.15 * jax.random.normal(arg_keys[7], (D,), jnp.float32), 0.25, 1.75).astype(jnp.bfloat16),
        "norm_two": jnp.clip(1.0 + 0.15 * jax.random.normal(arg_keys[8], (D,), jnp.float32), 0.25, 1.75).astype(jnp.bfloat16),
        "qkv_weight": bell_draw(arg_keys[9], (D, 3, D), D ** -0.5, 0.21875, ((0, 2), (2, 4))),
        "out_weight": bell_draw(arg_keys[10], (D, D), (D // 16) ** -0.5, 0.875, ((0, 4), (1, 2))),
        "bias_table": bell_draw(arg_keys[11], (H, NB), 1.0, 4.0, ((0, 4), (1, 2))),
        "router_weight": bell_draw(arg_keys[12], (D, EXPERTS), (2 * D) ** -0.5, 0.15625, ((0, 2),)),
        "expert_in": bell_draw(arg_keys[13], (EXPERTS, D, FF), D ** -0.5, 0.21875, ((0, 4), (1, 2), (2, 4))),
        "expert_out": bell_draw(arg_keys[14], (EXPERTS, FF, D), (max(1, FF // (EXPERTS * EXPERTS))) ** -0.5, 0.4375, ((0, 4), (1, 4), (2, 2))),
    }


EPS = 1e-06
HIGH = lax.Precision.HIGHEST

@jax.custom_vjp
def low(v):
    return lax.optimization_barrier(v.astype(jnp.bfloat16)).astype(jnp.float32)

@jax.custom_vjp
def low_back(v):
    return v

def low_keep(v):
    return (low(v), None)

def low_pass(kept, grad):
    return (grad,)

def back_keep(v):
    return (v, None)

def back_low(kept, grad):
    return (low(grad),)
low.defvjp(low_keep, low_pass)
low_back.defvjp(back_keep, back_low)

def attend(seq_block, doc_ids, rel_bias):
    queries = seq_block[:, 0]
    key_rows = seq_block[:, 1]
    value_rows = seq_block[:, 2]
    scores = low_back(0.125 * jnp.einsum('qhd,khd->hqk', queries, key_rows, precision=HIGH) + rel_bias)
    same = doc_ids[:, None] == doc_ids[None, :]
    scores = jnp.where(same[None], scores, -1e+30)
    row_max = lax.optimization_barrier(jnp.max(scores, axis=2, keepdims=True))
    exp_scores = jnp.exp(scores - row_max)
    attn_probs = exp_scores / lax.optimization_barrier(jnp.sum(exp_scores, axis=2, keepdims=True))
    return jnp.einsum('hqk,khd->qhd', low(attn_probs), value_rows, precision=HIGH)

def expert_ffn(rows_in, weight_in, weight_out):
    pre_act = low_back(jnp.dot(rows_in, weight_in, precision=HIGH))
    hidden = low(jax.nn.gelu(pre_act))
    return low_back(low(jnp.dot(hidden, weight_out, precision=HIGH)))

def forward(inputs, gain_one, gain_two, qkv_mat, out_mat, bias_mat, router_mat, in_mats, out_mats, segment_ids, buckets, routes, kept, slots):
    inv_one = lax.rsqrt(lax.optimization_barrier(jnp.mean(inputs * inputs, axis=1, keepdims=True)) + EPS)
    normed_one = low(inputs * inv_one * gain_one)
    projected = low_back(low(jnp.einsum('td,dkc->tkc', normed_one, qkv_mat, precision=HIGH)))
    projected = projected.reshape(NSEQ, LEN, 3, H, DH)
    onehot = (buckets[:, None] == jnp.arange(NB)[None, :]).astype(jnp.float32)
    relative = jnp.dot(bias_mat, onehot.T, precision=HIGH)
    offsets = (jnp.arange(LEN)[None, :] - jnp.arange(LEN)[:, None] + (LEN - 1)).astype(jnp.int32)
    rel_bias = jnp.take(relative, offsets, axis=1)
    attended = lax.map(jax.checkpoint(lambda pair: attend(pair[0], pair[1], rel_bias)), (projected, segment_ids))
    attended = low_back(low(attended.reshape(TOKENS, D)))
    mixed = low_back(jnp.dot(attended, out_mat, precision=HIGH))
    residual = inputs + mixed
    inv_two = lax.rsqrt(lax.optimization_barrier(jnp.mean(residual * residual, axis=1, keepdims=True)) + EPS)
    normed_two = low(residual * inv_two * gain_two)
    logits = low_back(jnp.dot(normed_two, router_mat, precision=HIGH))
    exp_logits = jnp.exp(logits - lax.optimization_barrier(jnp.max(logits, axis=1, keepdims=True)))
    router_probs = exp_logits / lax.optimization_barrier(jnp.sum(exp_logits, axis=1, keepdims=True))
    chosen = (routes[:, None] == jnp.arange(EXPERTS)[None, :]).astype(jnp.float32)
    gate = lax.optimization_barrier(jnp.sum(router_probs * chosen, axis=1))
    block_count = TOKENS // TOK_DEV
    slot_total = block_count * EXPERTS * CAP
    owner = (jnp.arange(TOKENS) // TOK_DEV).astype(jnp.int32)
    target = jnp.where(kept > 0, (owner * EXPERTS + routes) * CAP + slots, slot_total).astype(jnp.int32)
    buffer = jnp.zeros((slot_total, D), jnp.float32).at[target].set(normed_two, mode='drop')
    buffer = low_back(buffer)
    grouped = buffer.reshape(block_count, EXPERTS, CAP, D).transpose(1, 0, 2, 3).reshape(EXPERTS, block_count * CAP, D)
    results = lax.map(jax.checkpoint(lambda trio: expert_ffn(trio[0], trio[1], trio[2])), (grouped, in_mats, out_mats))
    results = results.reshape(EXPERTS, block_count, CAP, D).transpose(1, 0, 2, 3).reshape(slot_total, D)
    picked = jnp.take(results, jnp.minimum(target, slot_total - 1), axis=0)
    return residual + (kept.astype(jnp.float32) * gate)[:, None] * picked

def reference(tokens, segment_ids, buckets, routes, kept, slots, cotangent, norm_one, norm_two, qkv_weight, out_weight, bias_table, router_weight, expert_in, expert_out):

    def layer(inputs, gain_one, gain_two, qkv_mat, out_mat, bias_mat, router_mat, in_mats, out_mats):
        return forward(inputs, gain_one, gain_two, qkv_mat, out_mat, bias_mat, router_mat, in_mats, out_mats, segment_ids, buckets, routes, kept, slots)
    final, pullback = jax.vjp(layer, tokens.astype(jnp.float32), norm_one.astype(jnp.float32), norm_two.astype(jnp.float32), qkv_weight.astype(jnp.float32), out_weight.astype(jnp.float32), bias_table.astype(jnp.float32), router_weight.astype(jnp.float32), expert_in.astype(jnp.float32), expert_out.astype(jnp.float32))
    grads = pullback(cotangent.astype(jnp.float32))
    return (final.astype(jnp.bfloat16), grads[0], grads[1], grads[2], grads[3], grads[4], grads[5], grads[6], grads[7], grads[8])
```

```python
import functools

import jax
import jax.numpy as jnp
from jax import lax
from jax.experimental import pallas as pl
from jax.experimental.pallas import tpu as pltpu
from jax.sharding import PartitionSpec as P

DH = 64
EPS = 1e-06
NEG = -1e30
HIGH = lax.Precision.HIGHEST
BQ = 128
F32 = jnp.float32
BF16 = jnp.bfloat16


def contract(left, right, left_dim, right_dim):
    return lax.dot_general(
        left, right, (((left_dim,), (right_dim,)), ((), ())), preferred_element_type=F32
    )


def partner(value, axis, step):
    size = lax.axis_size(axis)
    return lax.ppermute(value, axis, [(i, i ^ step) for i in range(size)])


def swap_chunks(chunks, axis):
    return [chunks[0]] + [partner(c, axis, k) for k, c in enumerate(chunks) if k]


def gather_pieces(value, axis):
    return swap_chunks([value] * lax.axis_size(axis), axis)


def shear_table(rel_ref, table_ref, heads, span):
    for h in range(heads):
        row = jnp.broadcast_to(rel_ref[h : h + 1, :], (BQ, span))
        table_ref[h] = pltpu.roll(row, span - (BQ - 1), 1, stride=1, stride_axis=0)


def attend_fwd_kernel(qkv_ref, rel_ref, doc_row_ref, doc_col_ref, out_ref, lse_ref, table_ref, *, heads):
    length = qkv_ref.shape[0]
    blocks = length // BQ
    width = heads * DH
    step = pl.program_id(0)

    @pl.when(step == 0)
    def _():
        shear_table(rel_ref, table_ref, heads, table_ref.shape[2])

    row0 = pl.multiple_of(step * BQ, BQ)
    col0 = pl.multiple_of((blocks - 1 - step) * BQ, BQ)
    same = doc_col_ref[...] == doc_row_ref[...]
    outs, stats = [], []
    for h in range(heads):
        q = qkv_ref[pl.ds(row0, BQ), h * DH : (h + 1) * DH] * 0.125
        k = qkv_ref[:, width + h * DH : width + (h + 1) * DH]
        v = qkv_ref[:, 2 * width + h * DH : 2 * width + (h + 1) * DH]
        s = contract(q, k, 1, 1) + table_ref[h, :, pl.ds(col0, length)]
        s = jnp.where(same, s, NEG)
        top = jnp.max(s, axis=1, keepdims=True)
        e = jnp.exp(s - top)
        total = jnp.sum(e, axis=1, keepdims=True)
        o = contract(e.astype(BF16), v, 1, 0)
        outs.append(o * (1.0 / total))
        stats.append(top + jnp.log(total))
    out_ref[...] = jnp.concatenate(outs, axis=1).astype(BF16)
    lse_ref[...] = jnp.concatenate(stats, axis=1)


def attend_bwd_kernel(
    qkv_ref, rel_ref, doc_row_ref, doc_col_ref, lse_ref, grad_ref,
    dq_ref, dk_ref, dv_ref, drel_ref, table_ref, acc_ref, dk_acc, dv_acc, *, heads,
):
    length = qkv_ref.shape[0]
    blocks = length // BQ
    width = heads * DH
    span = table_ref.shape[2]
    step = pl.program_id(0)

    @pl.when(step == 0)
    def _():
        shear_table(rel_ref, table_ref, heads, span)
        acc_ref[...] = jnp.zeros(acc_ref.shape, F32)
        dk_acc[...] = jnp.zeros(dk_acc.shape, F32)
        dv_acc[...] = jnp.zeros(dv_acc.shape, F32)

    row0 = pl.multiple_of(step * BQ, BQ)
    col0 = pl.multiple_of((blocks - 1 - step) * BQ, BQ)
    same = doc_col_ref[...] == doc_row_ref[...]
    dqs = []
    for h in range(heads):
        q = qkv_ref[pl.ds(row0, BQ), h * DH : (h + 1) * DH] * 0.125
        k = qkv_ref[:, width + h * DH : width + (h + 1) * DH]
        v = qkv_ref[:, 2 * width + h * DH : 2 * width + (h + 1) * DH]
        g = grad_ref[:, h * DH : (h + 1) * DH]
        s = contract(q, k, 1, 1) + table_ref[h, :, pl.ds(col0, length)]
        s = jnp.where(same, s, NEG)
        p = jnp.exp(s - lse_ref[:, h : h + 1])
        dp = contract(g, v, 1, 1)
        inner = jnp.sum(p * dp, axis=1, keepdims=True)
        ds = p * (dp - inner)
        dsb = ds.astype(BF16)
        acc_ref[h, :, pl.ds(col0, length)] += ds
        dqs.append(0.125 * contract(dsb, k, 1, 0))
        dk_acc[h * DH : (h + 1) * DH, :] += contract(q, dsb, 0, 0)
        dv_acc[h * DH : (h + 1) * DH, :] += contract(g, p.astype(BF16), 0, 0)
    dq_ref[...] = jnp.concatenate(dqs, axis=1).astype(BF16)

    @pl.when(step == blocks - 1)
    def _():
        dk_ref[...] = dk_acc[...].astype(BF16)
        dv_ref[...] = dv_acc[...].astype(BF16)
        for h in range(heads):
            rows = acc_ref[h]
            half = BQ // 2
            while half >= 1:
                rows = pltpu.roll(rows[:half], half, 1) + rows[half:]
                half //= 2
            drel_ref[h : h + 1, :] = rows


def attend_specs(length, heads, span):
    whole = lambda shape: pl.BlockSpec(shape, lambda i: (0, 0))
    return [
        whole((length, 3 * heads * DH)),
        whole((8, span)),
        whole((1, length)),
        pl.BlockSpec((BQ, 1), lambda i: (i, 0)),
    ]


def attend_fwd(projected, rel, doc_row, doc_col, heads):
    length = projected.shape[0]
    span = rel.shape[1]
    return pl.pallas_call(
        functools.partial(attend_fwd_kernel, heads=heads),
        grid=(length // BQ,),
        in_specs=attend_specs(length, heads, span),
        out_specs=[
            pl.BlockSpec((BQ, heads * DH), lambda i: (i, 0)),
            pl.BlockSpec((BQ, heads), lambda i: (i, 0)),
        ],
        out_shape=[
            jax.ShapeDtypeStruct((length, heads * DH), BF16),
            jax.ShapeDtypeStruct((length, heads), F32),
        ],
        scratch_shapes=[pltpu.VMEM((heads, BQ, span), F32)],
        compiler_params=pltpu.CompilerParams(vmem_limit_bytes=48 * 1024 * 1024),
        name="attend_fwd",
    )(projected, rel, doc_row, doc_col)


def attend_bwd(projected, rel, doc_row, doc_col, lse, grad, heads):
    length = projected.shape[0]
    span = rel.shape[1]
    width = heads * DH
    return pl.pallas_call(
        functools.partial(attend_bwd_kernel, heads=heads),
        grid=(length // BQ,),
        in_specs=attend_specs(length, heads, span)
        + [
            pl.BlockSpec((BQ, heads), lambda i: (i, 0)),
            pl.BlockSpec((BQ, width), lambda i: (i, 0)),
        ],
        out_specs=[
            pl.BlockSpec((BQ, width), lambda i: (i, 0)),
            pl.BlockSpec((width, length), lambda i: (0, 0)),
            pl.BlockSpec((width, length), lambda i: (0, 0)),
            pl.BlockSpec((8, span), lambda i: (0, 0)),
        ],
        out_shape=[
            jax.ShapeDtypeStruct((length, width), BF16),
            jax.ShapeDtypeStruct((width, length), BF16),
            jax.ShapeDtypeStruct((width, length), BF16),
            jax.ShapeDtypeStruct((8, span), F32),
        ],
        scratch_shapes=[
            pltpu.VMEM((heads, BQ, span), F32),
            pltpu.VMEM((heads, BQ, span), F32),
            pltpu.VMEM((width, length), F32),
            pltpu.VMEM((width, length), F32),
        ],
        compiler_params=pltpu.CompilerParams(vmem_limit_bytes=48 * 1024 * 1024),
        name="attend_bwd",
    )(projected, rel, doc_row, doc_col, lse, grad)


def gelu_pair(pre):
    root = 0.7978845608028654
    cubic = 0.044715
    square = pre * pre
    th = jnp.tanh(root * pre * (1.0 + cubic * square))
    value = 0.5 * pre * (1.0 + th)
    slope = 0.5 * (1.0 + th) + 0.5 * pre * (1.0 - th * th) * root * (1.0 + 3.0 * cubic * square)
    return value, slope


def halves(value, dim):
    extent = value.shape[dim] // 2
    me = lax.axis_index("shard")
    own = lax.dynamic_slice_in_dim(value, me * extent, extent, dim)
    other = lax.dynamic_slice_in_dim(value, (1 - me) * extent, extent, dim)
    return other, own


def pair_scatter(value, dim):
    other, own = halves(value, dim)
    return own + partner(other.astype(BF16), "shard", 1).astype(F32)


def chunk_of(value, axis, step):
    size = lax.axis_size(axis)
    extent = value.shape[0] // size
    return lax.dynamic_slice_in_dim(value, (lax.axis_index(axis) ^ step) * extent, extent, 0)


def scatter_sum(value, axis):
    size = lax.axis_size(axis)
    total = chunk_of(value, axis, 0)
    for k in range(1, size):
        total = total + partner(chunk_of(value, axis, k).astype(BF16), axis, k).astype(F32)
    return total


def join_chunks(value, axis):
    size = lax.axis_size(axis)
    pieces = gather_pieces(value, axis)
    extent = value.shape[0]
    out = jnp.zeros((size * extent,) + value.shape[1:], value.dtype)
    me = lax.axis_index(axis)
    for k in range(size):
        out = lax.dynamic_update_slice_in_dim(out, pieces[k], (me ^ k) * extent, 0)
    return out


def total_over(value, axis):
    for piece in gather_pieces(value, axis)[1:]:
        value = value + piece
    return value


def body(
    tokens, segment_ids, buckets, routes, kept, slots, cotangent, norm_one, norm_two,
    qkv_weight, out_weight, bias_table, router_weight, expert_in, expert_out,
):
    n_t = lax.axis_size("tensor")
    n_d = lax.axis_size("dp")
    me_t = lax.axis_index("tensor")
    me_d = lax.axis_index("dp")
    me_s = lax.axis_index("shard")
    length, width = tokens.shape
    heads = qkv_weight.shape[2] // DH
    own = heads * DH
    n_e = router_weight.shape[1]
    n_b = 2 * bias_table.shape[1]
    capacity = 5 * length // (4 * n_d)
    quarter = capacity // n_t
    rows_q = n_d * quarter
    rows_all = n_t * rows_q

    half = norm_one.shape[0]
    packed = jnp.concatenate(
        [norm_one, norm_two, router_weight.T.reshape(-1), bias_table.reshape(-1)]
    )
    packed = lax.all_gather(packed, "shard", axis=0, tiled=False)
    gain_one = packed[:, :half].reshape(1, width).astype(F32)
    gain_two = packed[:, half : 2 * half].reshape(1, width).astype(F32)
    router = (
        packed[:, 2 * half : (2 + n_e) * half].reshape(2, n_e, half).transpose(1, 0, 2).reshape(n_e, width)
    )
    table = (
        packed[:, (2 + n_e) * half :].reshape(2, heads, n_b // 2).transpose(1, 0, 2).reshape(heads, n_b)
    )
    qkv_full = lax.all_gather(qkv_weight.reshape(half, 3 * own), "shard", axis=0, tiled=True)
    out_own = lax.all_gather(out_weight, "shard", axis=1, tiled=True)
    in_own = lax.all_gather(expert_in[0], "shard", axis=0, tiled=True)
    outw_own = lax.all_gather(expert_out[0], "shard", axis=1, tiled=True)
    out_rel = jnp.concatenate(gather_pieces(out_own, "tensor"), axis=0)

    place = ((slots // quarter) ^ me_t) * rows_q + (routes ^ me_d) * quarter + slots % quarter
    place = jnp.where(kept > 0, place, -1)
    pick = (place[None, :] == jnp.arange(rows_all, dtype=jnp.int32)[:, None]).astype(BF16)
    dropped = (kept == 0)[:, None]

    g_slots = contract(pick, cotangent, 1, 0).astype(BF16).reshape(n_t, n_d, quarter, width)
    g_own = g_slots[0].reshape(rows_q, width)
    g_rows = jnp.stack(
        swap_chunks([g_slots[:, k] for k in range(n_d)], "dp"), axis=1
    ).reshape(rows_all, width)

    inputs = tokens.astype(F32)
    inv_one = lax.rsqrt(jnp.mean(inputs * inputs, axis=1, keepdims=True) + EPS)
    normed_one = (inputs * inv_one * gain_one).astype(BF16)
    projected = contract(normed_one, qkv_full, 1, 0).astype(BF16)
    span = 2 * length
    onehot = (
        jnp.pad(buckets, (0, span - buckets.shape[0]), constant_values=-1)[None, :]
        == jnp.arange(n_b, dtype=jnp.int32)[:, None]
    )
    rel = jnp.pad(contract(table, onehot.astype(BF16), 1, 0), ((0, 8 - heads), (0, 0)))
    doc_row = segment_ids.reshape(1, length)
    doc_col = segment_ids.reshape(length, 1)
    attended, lse = attend_fwd(projected, rel, doc_row, doc_col, heads)

    att_slots = contract(pick, attended, 1, 0).astype(BF16).reshape(n_t, rows_q, own)
    att_rows = jnp.concatenate(swap_chunks([att_slots[k] for k in range(n_t)], "tensor"), axis=1)
    x_rows = contract(pick[:rows_q], tokens, 1, 0)
    resid_rows = x_rows + contract(att_rows, out_rel, 1, 0)
    inv_two = lax.rsqrt(jnp.mean(resid_rows * resid_rows, axis=1, keepdims=True) + EPS)
    unit_two = resid_rows * inv_two
    normed_two = (unit_two * gain_two).astype(BF16)

    sent = normed_two.reshape(n_d, quarter, width)
    arrived = jnp.concatenate(swap_chunks([sent[k] for k in range(n_d)], "dp"), axis=0)
    rows = jnp.concatenate(gather_pieces(arrived, "tensor"), axis=0)

    logits = contract(rows, router, 1, 1)
    exp_logits = jnp.exp(logits - jnp.max(logits, axis=1, keepdims=True))
    probs = exp_logits / jnp.sum(exp_logits, axis=1, keepdims=True)
    chosen = (jnp.arange(n_e, dtype=jnp.int32)[None, :] == me_d).astype(F32)
    gate = jnp.sum(probs * chosen, axis=1, keepdims=True)
    pre = contract(rows, in_own, 1, 0)
    value, slope = gelu_pair(pre)
    hidden = value.astype(BF16)
    grad_raw = contract(g_rows, outw_own, 1, 1)
    grad_pre = (gate * grad_raw * slope).astype(BF16)
    grad_gate = jnp.sum(hidden.astype(F32) * grad_raw, axis=1, keepdims=True)
    grad_logits = (grad_gate * probs * (chosen - gate)).astype(BF16)
    grad_rows = contract(grad_pre, in_own, 1, 1) + contract(grad_logits, router, 1, 0)
    back = swap_chunks(
        [grad_rows[k * rows_q : (k + 1) * rows_q].astype(BF16) for k in range(n_t)], "tensor"
    )
    grad_arrived = grad_rows[:rows_q]
    for piece in back[1:]:
        grad_arrived = grad_arrived + piece.astype(F32)
    grad_arrived = grad_arrived.astype(BF16).reshape(n_d, quarter, width)
    grad_two = jnp.concatenate(
        swap_chunks([grad_arrived[k] for k in range(n_d)], "dp"), axis=0
    ).astype(F32)

    gain_two_part = jnp.sum(grad_two * unit_two, axis=0)
    scaled_two = grad_two * gain_two
    grad_resid = g_own.astype(F32) + inv_two * (
        scaled_two - unit_two * jnp.mean(scaled_two * unit_two, axis=1, keepdims=True)
    )
    grad_mixed = grad_resid.astype(BF16)
    grad_att = contract(grad_mixed, out_rel, 1, 1).astype(BF16)
    grad_att_slots = jnp.concatenate(
        swap_chunks([grad_att[:, k * own : (k + 1) * own] for k in range(n_t)], "tensor"), axis=0
    )
    drop_att = jnp.where(dropped, contract(cotangent, out_own, 1, 1), 0.0)
    grad_attended = (contract(pick, grad_att_slots, 0, 0) + drop_att).astype(BF16)

    grad_q, grad_kt, grad_vt, drel = attend_bwd(
        projected, rel, doc_row, doc_col, lse, grad_attended, heads
    )
    w_q, w_k, w_v = (qkv_full[:, i * own : (i + 1) * own] for i in range(3))
    grad_one = contract(grad_q, w_q, 1, 1) + contract(grad_kt, w_k, 0, 1) + contract(grad_vt, w_v, 0, 1)
    unit_one = inputs * inv_one
    gain_one_part = jnp.sum(grad_one * unit_one, axis=0)
    grad_one_q = scatter_sum(grad_one, "tensor")
    unit_q = chunk_of(unit_one, "tensor", 0)
    inv_q = chunk_of(inv_one, "tensor", 0)
    scaled_one = grad_one_q * gain_one
    delta = inv_q * (scaled_one - unit_q * jnp.mean(scaled_one * unit_q, axis=1, keepdims=True))
    delta_all = join_chunks(delta.astype(BF16), "tensor")

    mixed_slots = jnp.concatenate(gather_pieces(grad_mixed, "tensor"), axis=0)
    mixed_tok = jnp.where(dropped, cotangent, contract(pick, mixed_slots, 0, 0).astype(BF16))
    grad_tokens = mixed_tok.astype(F32) + delta_all.astype(F32)
    grad_out = pair_scatter(contract(attended, mixed_tok, 0, 0), 1)
    grad_out = join_chunks(scatter_sum(grad_out, "dp").astype(BF16), "dp").astype(F32)
    grad_qkv = jnp.concatenate(
        [contract(normed_one, grad_q, 0, 0), contract(normed_one, grad_kt, 0, 1), contract(normed_one, grad_vt, 0, 1)],
        axis=1,
    )
    grad_qkv = pair_scatter(grad_qkv, 0)
    grad_qkv = join_chunks(scatter_sum(grad_qkv, "dp").astype(BF16), "dp").astype(F32)

    scaled_res = (gate * contract(hidden, outw_own, 1, 0)).reshape(n_t, rows_q, width)
    res_pieces = swap_chunks([scaled_res[k].astype(BF16) for k in range(n_t)], "tensor")
    res = scaled_res[0]
    for piece in res_pieces[1:]:
        res = res + piece.astype(F32)
    res = res.astype(BF16).reshape(n_d, quarter, width)
    res = jnp.concatenate(swap_chunks([res[k] for k in range(n_d)], "dp"), axis=0)
    res_slots = jnp.concatenate(gather_pieces(res, "tensor"), axis=0)
    att_all = jnp.concatenate(gather_pieces(attended, "tensor"), axis=1)
    residual = inputs + contract(att_all, out_rel, 1, 0)
    output = (residual + contract(pick, res_slots, 0, 0)).astype(BF16)

    slot_grad = (gate * g_rows.astype(F32)).astype(BF16)
    grad_outw = pair_scatter(contract(hidden, slot_grad, 0, 0), 1)[None]
    grad_inw = pair_scatter(contract(rows, grad_pre, 0, 0), 0)[None]

    grad_router = contract(grad_logits, rows, 0, 0)
    grad_table = jnp.dot(drel[:heads], onehot.astype(F32).T, precision=HIGH)
    small = jnp.concatenate([gain_one_part[None], gain_two_part[None], grad_router], axis=0)
    small = total_over(total_over(total_over(small, "shard"), "dp"), "tensor")
    small = lax.dynamic_slice_in_dim(small, me_s * half, half, 1)
    grad_table = total_over(total_over(grad_table, "shard"), "dp")
    grad_table = lax.dynamic_slice_in_dim(grad_table, me_s * (n_b // 2), n_b // 2, 1)
    return (
        output,
        grad_tokens,
        small[0],
        small[1],
        grad_qkv.reshape(half, 3, own),
        grad_out,
        grad_table,
        small[2:].T,
        grad_inw,
        grad_outw,
    )


def solution(mesh):
    placed = (
        P(("dp", "shard"), None),
        P(("dp", "shard"), None),
        P(),
        P(("dp", "shard")),
        P(("dp", "shard")),
        P(("dp", "shard")),
        P(("dp", "shard"), None),
        P("shard"),
        P("shard"),
        P("shard", None, "tensor"),
        P("tensor", "shard"),
        P("tensor", "shard"),
        P("shard", None),
        P("dp", "shard", "tensor"),
        P("dp", "tensor", "shard"),
    )
    return jax.shard_map(
        body,
        mesh=mesh,
        in_specs=placed,
        out_specs=(
            P(("dp", "shard"), None),
            P(("dp", "shard"), None),
            P("shard"),
            P("shard"),
            P("shard", None, "tensor"),
            P("tensor", "shard"),
            P("tensor", "shard"),
            P("shard", None),
            P("dp", "shard", "tensor"),
            P("dp", "tensor", "shard"),
        ),
        check_vma=False,
    )
```

```python
import functools

import jax
import jax.numpy as jnp
from jax import lax
from jax.experimental import pallas as pl
from jax.experimental.pallas import tpu as pltpu
from jax.sharding import PartitionSpec as P

DH = 64
EPS = 1e-06
NEG = -1e30
HIGH = lax.Precision.HIGHEST
BQ = 128
F32 = jnp.float32
BF16 = jnp.bfloat16


def contract(left, right, left_dim, right_dim):
    return lax.dot_general(
        left, right, (((left_dim,), (right_dim,)), ((), ())), preferred_element_type=F32
    )


def partner(value, axis, step):
    size = lax.axis_size(axis)
    return lax.ppermute(value, axis, [(i, i ^ step) for i in range(size)])


def swap_chunks(chunks, axis):
    return [chunks[0]] + [partner(c, axis, k) for k, c in enumerate(chunks) if k]


def gather_pieces(value, axis):
    return swap_chunks([value] * lax.axis_size(axis), axis)


def pick_rows(place_row, start, rows):
    at = lax.broadcasted_iota(jnp.int32, (rows, place_row.shape[1]), 0) + start
    return (at == place_row).astype(F32).astype(BF16)


def pick_cols(place_col, start, rows):
    at = lax.broadcasted_iota(jnp.int32, (place_col.shape[0], rows), 1) + start
    return (at == place_col).astype(F32).astype(BF16)


def shear_table(rel_ref, table_ref, heads, span):
    for h in range(heads):
        row = jnp.broadcast_to(rel_ref[h : h + 1, :], (BQ, span))
        table_ref[h] = pltpu.roll(row, span - (BQ - 1), 1, stride=1, stride_axis=0)


def attend_fwd_kernel(
    qkv_ref, rel_ref, doc_row_ref, doc_col_ref, place_ref, out_ref, lse_ref, *rest, heads
):
    slot_refs, table_ref = rest[:-1], rest[-1]
    length = qkv_ref.shape[0]
    blocks = length // BQ
    width = heads * DH
    step = pl.program_id(0)

    @pl.when(step == 0)
    def _():
        shear_table(rel_ref, table_ref, heads, table_ref.shape[2])

    row0 = pl.multiple_of(step * BQ, BQ)
    col0 = pl.multiple_of((blocks - 1 - step) * BQ, BQ)
    same = doc_col_ref[...] == doc_row_ref[...]
    outs, stats = [], []
    for h in range(heads):
        q = qkv_ref[pl.ds(row0, BQ), h * DH : (h + 1) * DH] * 0.125
        k = qkv_ref[:, width + h * DH : width + (h + 1) * DH]
        v = qkv_ref[:, 2 * width + h * DH : 2 * width + (h + 1) * DH]
        s = contract(q, k, 1, 1) + table_ref[h, :, pl.ds(col0, length)]
        s = jnp.where(same, s, NEG)
        top = jnp.max(s, axis=1, keepdims=True)
        e = jnp.exp(s - top)
        total = jnp.sum(e, axis=1, keepdims=True)
        o = contract(e.astype(BF16), v, 1, 0)
        outs.append(o * (1.0 / total))
        stats.append(top + jnp.log(total))
    out_ref[pl.ds(row0, BQ), :] = jnp.concatenate(outs, axis=1).astype(BF16)
    lse_ref[...] = jnp.concatenate(stats, axis=1)

    @pl.when(step == blocks - 1)
    def _():
        place = place_ref[...]
        for n, ref in enumerate(slot_refs):
            ref[...] = contract(pick_rows(place, n * ref.shape[0], ref.shape[0]), out_ref[...], 1, 0).astype(BF16)


def attend_bwd_kernel(
    qkv_ref, rel_ref, doc_row_ref, doc_col_ref, lse_ref, place_ref, drop_ref, *rest, heads,
):
    slot_refs = rest[:-9]
    dq_ref, dk_ref, dv_ref, drel_ref, table_ref, acc_ref, dk_acc, dv_acc, grad_ref = rest[-9:]
    length = qkv_ref.shape[0]
    blocks = length // BQ
    width = heads * DH
    span = table_ref.shape[2]
    step = pl.program_id(0)

    @pl.when(step == 0)
    def _():
        shear_table(rel_ref, table_ref, heads, span)
        acc_ref[...] = jnp.zeros(acc_ref.shape, F32)
        dk_acc[...] = jnp.zeros(dk_acc.shape, F32)
        dv_acc[...] = jnp.zeros(dv_acc.shape, F32)
        grad = drop_ref[...].astype(F32)
        for n, ref in enumerate(slot_refs):
            grad = grad + contract(pick_cols(place_ref[...], n * ref.shape[0], ref.shape[0]), ref[...], 1, 0)
        grad_ref[...] = grad.astype(BF16)

    row0 = pl.multiple_of(step * BQ, BQ)
    col0 = pl.multiple_of((blocks - 1 - step) * BQ, BQ)
    same = doc_col_ref[...] == doc_row_ref[...]
    dqs = []
    for h in range(heads):
        q = qkv_ref[pl.ds(row0, BQ), h * DH : (h + 1) * DH] * 0.125
        k = qkv_ref[:, width + h * DH : width + (h + 1) * DH]
        v = qkv_ref[:, 2 * width + h * DH : 2 * width + (h + 1) * DH]
        g = grad_ref[pl.ds(row0, BQ), h * DH : (h + 1) * DH]
        s = contract(q, k, 1, 1) + table_ref[h, :, pl.ds(col0, length)]
        s = jnp.where(same, s, NEG)
        p = jnp.exp(s - lse_ref[:, h : h + 1])
        dp = contract(g, v, 1, 1)
        inner = jnp.sum(p * dp, axis=1, keepdims=True)
        ds = p * (dp - inner)
        dsb = ds.astype(BF16)
        acc_ref[h, :, pl.ds(col0, length)] += ds
        dqs.append(0.125 * contract(dsb, k, 1, 0))
        dk_acc[h * DH : (h + 1) * DH, :] += contract(q, dsb, 0, 0)
        dv_acc[h * DH : (h + 1) * DH, :] += contract(g, p.astype(BF16), 0, 0)
    dq_ref[...] = jnp.concatenate(dqs, axis=1).astype(BF16)

    @pl.when(step == blocks - 1)
    def _():
        dk_ref[...] = dk_acc[...].astype(BF16)
        dv_ref[...] = dv_acc[...].astype(BF16)
        for h in range(heads):
            rows = acc_ref[h]
            half = BQ // 2
            while half >= 1:
                rows = pltpu.roll(rows[:half], half, 1) + rows[half:]
                half //= 2
            drel_ref[h : h + 1, :] = rows


def whole(shape):
    return pl.BlockSpec(shape, lambda *i: (0,) * len(shape))


def wholes(arrays):
    return [whole(a.shape) for a in arrays]


def params():
    return pltpu.CompilerParams(vmem_limit_bytes=52 * 1024 * 1024)


def struct(shape, dtype):
    return jax.ShapeDtypeStruct(shape, dtype)


def attend_specs(length, heads, span):
    return [
        whole((length, 3 * heads * DH)),
        whole((8, span)),
        whole((1, length)),
        pl.BlockSpec((BQ, 1), lambda i: (i, 0)),
    ]


def attend_fwd(projected, rel, doc_row, doc_col, place_row, heads, parts, part_rows):
    length = projected.shape[0]
    span = rel.shape[1]
    width = heads * DH
    return pl.pallas_call(
        functools.partial(attend_fwd_kernel, heads=heads),
        grid=(length // BQ,),
        in_specs=attend_specs(length, heads, span) + [whole((1, length))],
        out_specs=[whole((length, width)), pl.BlockSpec((BQ, heads), lambda i: (i, 0))]
        + [whole((part_rows, width))] * parts,
        out_shape=[struct((length, width), BF16), struct((length, heads), F32)]
        + [struct((part_rows, width), BF16)] * parts,
        scratch_shapes=[pltpu.VMEM((heads, BQ, span), F32)],
        compiler_params=params(),
        name="attend_fwd",
    )(projected, rel, doc_row, doc_col, place_row)


def attend_bwd(projected, rel, doc_row, doc_col, lse, place_col, drop, grads, heads):
    length = projected.shape[0]
    span = rel.shape[1]
    width = heads * DH
    return pl.pallas_call(
        functools.partial(attend_bwd_kernel, heads=heads),
        grid=(length // BQ,),
        in_specs=attend_specs(length, heads, span)
        + [pl.BlockSpec((BQ, heads), lambda i: (i, 0)), whole((length, 1)), whole((length, width))]
        + wholes(grads),
        out_specs=[
            pl.BlockSpec((BQ, width), lambda i: (i, 0)),
            whole((width, length)),
            whole((width, length)),
            whole((8, span)),
        ],
        out_shape=[
            struct((length, width), BF16),
            struct((width, length), BF16),
            struct((width, length), BF16),
            struct((8, span), F32),
        ],
        scratch_shapes=[
            pltpu.VMEM((heads, BQ, span), F32),
            pltpu.VMEM((heads, BQ, span), F32),
            pltpu.VMEM((width, length), F32),
            pltpu.VMEM((width, length), F32),
            pltpu.VMEM((length, width), BF16),
        ],
        compiler_params=params(),
        name="attend_bwd",
    )(projected, rel, doc_row, doc_col, lse, place_col, drop, *grads)


def store_parts(refs, value):
    if len(refs) == 1:
        refs[0][...] = value
        return
    rows = refs[0].shape[0]
    for n, ref in enumerate(refs):
        ref[...] = value[n * rows : (n + 1) * rows]


def load_parts(refs):
    if len(refs) == 1:
        return refs[0][...]
    return jnp.concatenate([ref[...] for ref in refs], axis=0)


def slot_rows_kernel(place_g_ref, place_x_ref, cot_ref, tok_ref, x_ref, *g_refs):
    rows = g_refs[0].shape[0]
    place = place_g_ref[...]
    for n, ref in enumerate(g_refs):
        ref[...] = contract(pick_rows(place, n * rows, rows), cot_ref[...], 1, 0).astype(BF16)
    x_ref[...] = contract(pick_rows(place_x_ref[...], 0, x_ref.shape[0]), tok_ref[...], 1, 0).astype(BF16)


def slot_rows(place_g, place_x, cotangent, tokens, rows_x, parts, part_rows):
    width = tokens.shape[1]
    out = pl.pallas_call(
        slot_rows_kernel,
        out_shape=[struct((rows_x, width), BF16)] + [struct((part_rows, width), BF16)] * parts,
        compiler_params=params(),
        name="slot_rows",
    )(place_g, place_x, cotangent, tokens)
    return out[0], out[1:]


def middle_kernel(*refs, n_t, parts):
    att, (w_ref, x_ref, gain_ref) = refs[:n_t], refs[n_t : n_t + 3]
    unit_ref, inv_ref = refs[n_t + 3 : n_t + 5]
    outs = refs[n_t + 5 :]
    sides = []
    for half in range(2):
        total = contract(att[0][...], w_ref[half, 0], 1, 0)
        for k in range(1, n_t):
            total = total + contract(att[k][...], w_ref[half, k], 1, 0)
        sides.append(total)
    resid = x_ref[...].astype(F32) + jnp.concatenate(sides, axis=1)
    inv = lax.rsqrt(jnp.mean(resid * resid, axis=1, keepdims=True) + EPS)
    unit = resid * inv
    unit_ref[...] = unit
    inv_ref[...] = inv
    store_parts(outs, (unit * gain_ref[...]).astype(BF16))


def middle(att, w_rel, x_rows, gain, parts):
    rows, width = x_rows.shape
    out = pl.pallas_call(
        functools.partial(middle_kernel, n_t=len(att), parts=parts),
        out_shape=[struct((rows, width), F32), struct((rows, 1), F32)]
        + [struct((rows // parts, width), BF16)] * parts,
        compiler_params=params(),
        name="second_norm",
    )(*att, w_rel, x_rows, gain)
    return out[0], out[1], out[2:]


def expert_kernel(me_ref, *refs, parts, chunks, n_e):
    rows_refs, g_refs = refs[:parts], refs[parts : 2 * parts]
    win_refs = refs[2 * parts : 2 * parts + chunks]
    wout_refs = refs[2 * parts + chunks : 2 * parts + 2 * chunks]
    router_ref = refs[2 * parts + 2 * chunks]
    outs = refs[2 * parts + 2 * chunks + 1 :]
    grad_ref, rows_ref, slot_ref, gate_ref, logit_ref = outs[:5]
    hid_refs, gpre_refs = outs[5 : 5 + chunks], outs[5 + chunks :]
    rows = load_parts(rows_refs)
    g = load_parts(g_refs)
    half = g.shape[1] // 2
    router = router_ref[...]
    logits = contract(rows, router, 1, 1)
    exp_logits = jnp.exp(logits - jnp.max(logits, axis=1, keepdims=True))
    probs = exp_logits / jnp.sum(exp_logits, axis=1, keepdims=True)
    chosen = (lax.broadcasted_iota(jnp.int32, logits.shape, 1) == me_ref[0]).astype(F32)
    gate = jnp.sum(probs * chosen, axis=1, keepdims=True)
    grad_gate = jnp.zeros(gate.shape, F32)
    total = None
    for c in range(chunks):
        pre = contract(rows, win_refs[c][...], 1, 0)
        value, slope = gelu_pair(pre)
        hidden = value.astype(BF16)
        hid_refs[c][...] = hidden
        raw = contract(g[:, :half], wout_refs[c][0], 1, 1) + contract(g[:, half:], wout_refs[c][1], 1, 1)
        grad_gate = grad_gate + jnp.sum(hidden.astype(F32) * raw, axis=1, keepdims=True)
        grad_pre = (gate * raw * slope).astype(BF16)
        gpre_refs[c][...] = grad_pre
        part = contract(grad_pre, win_refs[c][...], 1, 1)
        total = part if total is None else total + part
    grad_logits = (grad_gate * probs * (chosen - gate)).astype(BF16)
    total = total + contract(grad_logits, router, 1, 0)
    grad_ref[...] = total.astype(grad_ref.dtype)
    rows_ref[...] = rows
    slot_ref[...] = (gate * g.astype(F32)).astype(BF16)
    gate_ref[...] = gate
    logit_ref[...] = grad_logits


def expert(me_d, rows, g, g_specs, w_in, w_out, router, grad_dtype):
    parts, chunks = len(rows), len(w_in)
    total = sum(r.shape[0] for r in rows)
    width = rows[0].shape[1]
    hidden = w_in[0].shape[1]
    n_e = router.shape[0]
    out = pl.pallas_call(
        functools.partial(expert_kernel, parts=parts, chunks=chunks, n_e=n_e),
        grid=(1,),
        in_specs=[pl.BlockSpec(memory_space=pltpu.SMEM)]
        + wholes(rows) + g_specs + wholes(w_in) + wholes(w_out) + [whole(router.shape)],
        out_specs=[
            whole((total, width)), whole((total, width)), whole((total, width)), whole((total, 1)), whole((total, n_e))
        ] + [whole((total, hidden))] * (2 * chunks),
        out_shape=[
            struct((total, width), grad_dtype),
            struct((total, width), BF16),
            struct((total, width), BF16),
            struct((total, 1), F32),
            struct((total, n_e), BF16),
        ]
        + [struct((total, hidden), BF16)] * (2 * chunks),
        compiler_params=params(),
        name="expert",
    )(me_d, *rows, *g, *w_in, *w_out, router)
    return out[:5], out[5 : 5 + chunks], out[5 + chunks :]


def expert_late_kernel(me_ref, *refs, groups, chunks):
    side = lambda n: refs[n * groups : (n + 1) * groups]
    rows, slot, gate, logit = (side(n) for n in range(4))
    at = 4 * groups
    hid = [refs[at + c * groups : at + (c + 1) * groups] for c in range(chunks)]
    at += chunks * groups
    gpre = [refs[at + c * groups : at + (c + 1) * groups] for c in range(chunks)]
    at += chunks * groups
    wout = refs[at : at + chunks]
    outs = refs[at + chunks :]
    res_own, res_other, router_ref = outs[:3]
    half = rows[0].shape[1] // 2
    mine = pl.multiple_of(me_ref[0] * half, half)
    theirs = pl.multiple_of((1 - me_ref[0]) * half, half)
    for r, ref in enumerate((res_own, res_other)):
        sides = []
        for s in range(2):
            total = contract(hid[0][r][...], wout[0][s], 1, 0)
            for c in range(1, chunks):
                total = total + contract(hid[c][r][...], wout[c][s], 1, 0)
            sides.append(total)
        ref[...] = (gate[r][...] * jnp.concatenate(sides, axis=1)).astype(ref.dtype)
    add = lambda f: f(0) + f(1)
    router_ref[...] = add(lambda r: contract(logit[r][...], rows[r][...], 0, 0))
    for c in range(chunks):
        own_in, other_in, own_out, other_out = outs[3 + 4 * c : 7 + 4 * c]
        for ref, start in ((own_in, mine), (other_in, theirs)):
            ref[...] = add(
                lambda r: contract(rows[r][:, pl.ds(start, half)], gpre[c][r][...], 0, 0)
            ).astype(ref.dtype)
        for ref, start in ((own_out, mine), (other_out, theirs)):
            ref[...] = add(
                lambda r: contract(hid[c][r][...], slot[r][:, pl.ds(start, half)], 0, 0)
            ).astype(ref.dtype)


def expert_late(me_s, groups, w_out):
    chunks = len(w_out)
    operands = []
    for n in (1, 2, 3, 4):
        operands += [grp[0][n] for grp in groups]
    for kind in (1, 2):
        for c in range(chunks):
            operands += [grp[kind][c] for grp in groups]
    operands += list(w_out)
    rows, width = groups[0][0][1].shape
    hidden = groups[0][1][0].shape[1]
    n_e = groups[0][0][4].shape[1]
    half = width // 2
    shapes = [struct((rows, width), F32), struct((rows, width), BF16), struct((n_e, width), F32)]
    for c in range(chunks):
        shapes += [
            struct((half, hidden), F32), struct((half, hidden), BF16),
            struct((hidden, half), F32), struct((hidden, half), BF16),
        ]
    out = pl.pallas_call(
        functools.partial(expert_late_kernel, groups=len(groups), chunks=chunks),
        grid=(1,),
        in_specs=[pl.BlockSpec(memory_space=pltpu.SMEM)] + wholes(operands),
        out_specs=[whole(s.shape) for s in shapes],
        out_shape=shapes,
        compiler_params=params(),
        name="expert_late",
    )(me_s, *operands)
    return out[0], out[1], out[2], [out[3 + 4 * c : 7 + 4 * c] for c in range(chunks)]


def add_parts_kernel(own_ref, other_ref, *outs):
    store_parts(outs, (own_ref[...] + other_ref[...].astype(F32)).astype(BF16))


def add_parts(own, other, parts):
    rows, width = own.shape
    return pl.pallas_call(
        add_parts_kernel,
        out_shape=[struct((rows // parts, width), BF16)] * parts,
        compiler_params=params(),
        name="add_parts",
    )(own, other)


def second_norm_bwd_kernel(*refs, parts, n_t):
    grads, g_refs = refs[:parts], refs[parts : 2 * parts]
    unit_ref, inv_ref, gain_ref, w_ref, mixed_ref, gain_out_ref = refs[2 * parts : 2 * parts + 6]
    outs = refs[2 * parts + 6 :]
    grad = load_parts(grads).astype(F32)
    unit = unit_ref[...]
    gain_out_ref[...] = jnp.sum(grad * unit, axis=0, keepdims=True)
    scaled = grad * gain_ref[...]
    resid = load_parts(g_refs).astype(F32) + inv_ref[...] * (
        scaled - unit * jnp.mean(scaled * unit, axis=1, keepdims=True)
    )
    mixed = resid.astype(BF16)
    mixed_ref[...] = mixed
    half = mixed.shape[1] // 2
    for k, ref in enumerate(outs):
        ref[...] = (
            contract(mixed[:, :half], w_ref[0, k], 1, 1) + contract(mixed[:, half:], w_ref[1, k], 1, 1)
        ).astype(BF16)


def second_norm_bwd(grads, g, g_specs, unit, inv, gain, w_rel):
    rows, width = unit.shape
    n_t, own = w_rel.shape[1:3]
    shapes = [struct((rows, width), BF16), struct((1, width), F32)] + [struct((rows, own), BF16)] * n_t
    out = pl.pallas_call(
        functools.partial(second_norm_bwd_kernel, parts=len(grads), n_t=n_t),
        grid=(1,),
        in_specs=wholes(grads) + g_specs + wholes([unit, inv, gain, w_rel]),
        out_specs=[whole(s.shape) for s in shapes],
        out_shape=shapes,
        compiler_params=params(),
        name="second_norm_bwd",
    )(*grads, *g, unit, inv, gain, w_rel)
    return out[0], out[1], out[2:]


def place_chunks_kernel(order_ref, base_ref, *refs, count):
    step = pl.program_id(0)
    out_ref = refs[count]
    for k in range(count):

        @pl.when(step == k)
        def _():
            out_ref[...] = base_ref[...].astype(F32) + refs[k][...].astype(F32)


def place_chunks(me_t, base, pieces):
    count = len(pieces)
    rows, width = pieces[0].shape
    order = (me_t ^ jnp.arange(count, dtype=jnp.int32)).astype(jnp.int32)
    at = lambda i, order: (order[i], 0)
    return pl.pallas_call(
        functools.partial(place_chunks_kernel, count=count),
        grid_spec=pltpu.PrefetchScalarGridSpec(
            num_scalar_prefetch=1,
            grid=(count,),
            in_specs=[pl.BlockSpec((rows, width), at)] + wholes(pieces),
            out_specs=pl.BlockSpec((rows, width), at),
        ),
        out_shape=struct(base.shape, F32),
        compiler_params=params(),
        name="place_chunks",
    )(order, base, *pieces)


def gelu_pair(pre):
    root = 0.7978845608028654
    cubic = 0.044715
    square = pre * pre
    th = jnp.tanh(root * pre * (1.0 + cubic * square))
    value = 0.5 * pre * (1.0 + th)
    slope = 0.5 * (1.0 + th) + 0.5 * pre * (1.0 - th * th) * root * (1.0 + 3.0 * cubic * square)
    return value, slope


def halves(value, dim):
    extent = value.shape[dim] // 2
    me = lax.axis_index("shard")
    own = lax.dynamic_slice_in_dim(value, me * extent, extent, dim)
    other = lax.dynamic_slice_in_dim(value, (1 - me) * extent, extent, dim)
    return other, own


def pair_scatter(value, dim):
    other, own = halves(value, dim)
    return own + partner(other.astype(BF16), "shard", 1).astype(F32)


def chunk_of(value, axis, step):
    size = lax.axis_size(axis)
    extent = value.shape[0] // size
    return lax.dynamic_slice_in_dim(value, (lax.axis_index(axis) ^ step) * extent, extent, 0)


def scatter_sum(value, axis):
    size = lax.axis_size(axis)
    total = chunk_of(value, axis, 0)
    for k in range(1, size):
        total = total + partner(chunk_of(value, axis, k).astype(BF16), axis, k).astype(F32)
    return total


def join_chunks(value, axis):
    size = lax.axis_size(axis)
    pieces = gather_pieces(value, axis)
    extent = value.shape[0]
    out = jnp.zeros((size * extent,) + value.shape[1:], value.dtype)
    me = lax.axis_index(axis)
    for k in range(size):
        out = lax.dynamic_update_slice_in_dim(out, pieces[k], (me ^ k) * extent, 0)
    return out


def total_over(value, axis):
    for piece in gather_pieces(value, axis)[1:]:
        value = value + piece
    return value


def tie(*values):
    return lax.optimization_barrier(values)


def body(
    tokens, segment_ids, buckets, routes, kept, slots, cotangent, norm_one, norm_two,
    qkv_weight, out_weight, bias_table, router_weight, expert_in, expert_out,
):
    n_t = lax.axis_size("tensor")
    n_d = lax.axis_size("dp")
    me_t = lax.axis_index("tensor")
    me_d = lax.axis_index("dp")
    me_s = lax.axis_index("shard")
    length, width = tokens.shape
    heads = qkv_weight.shape[2] // DH
    own = heads * DH
    n_e = router_weight.shape[1]
    n_b = 2 * bias_table.shape[1]
    capacity = 5 * length // (4 * n_d)
    quarter = capacity // n_t
    rows_q = n_d * quarter
    parts = n_d if quarter % 16 == 0 else 1
    half = width // 2
    scalar = lambda v: v.astype(jnp.int32).reshape(1)

    rel_t = (slots // quarter) ^ me_t
    rel_d = routes ^ me_d
    spot = slots % quarter
    taken = kept > 0
    place = jnp.where(taken, rel_t * rows_q + rel_d * quarter + spot, -1)
    place_g = jnp.where(taken & (rel_t < 2), (rel_d * 2 + rel_t) * quarter + spot, -1)
    place_row, place_col = place[None, :], place[:, None]
    dropped = (kept == 0)[:, None]

    out_pieces = gather_pieces(out_weight, "tensor")
    in_far = partner(expert_in[0], "tensor", 2)
    outw_far = partner(expert_out[0], "tensor", 2)
    packed = jnp.concatenate(
        [norm_one, norm_two, router_weight.T.reshape(-1), bias_table.reshape(-1)]
    ).reshape(1, -1)
    packed_far = partner(packed, "shard", 1)
    packed = jnp.where(
        me_s == 0,
        jnp.concatenate([packed, packed_far], axis=0),
        jnp.concatenate([packed_far, packed], axis=0),
    )
    gain_one = packed[:, :half].reshape(1, width).astype(F32)
    gain_two = packed[:, half : 2 * half].reshape(1, width).astype(F32)
    router = (
        packed[:, 2 * half : (2 + n_e) * half].reshape(2, n_e, half).transpose(1, 0, 2).reshape(n_e, width)
    )
    table = (
        packed[:, (2 + n_e) * half :].reshape(2, heads, n_b // 2).transpose(1, 0, 2).reshape(heads, n_b)
    )
    qkv_full = lax.all_gather(qkv_weight.reshape(half, 3 * own), "shard", axis=0, tiled=True)

    x_rows, g_send = slot_rows(place_g[None, :], place_row, cotangent, tokens, rows_q, parts, 2 * rows_q // parts)
    if parts == 1:
        g_send = [g_send[0][k * 2 * quarter : (k + 1) * 2 * quarter] for k in range(n_d)]

    inputs = tokens.astype(F32)
    inv_one = lax.rsqrt(jnp.mean(inputs * inputs, axis=1, keepdims=True) + EPS)
    normed_one = (inputs * inv_one * gain_one).astype(BF16)
    projected = contract(normed_one, qkv_full, 1, 0).astype(BF16)
    span = 2 * length
    onehot = (
        jnp.pad(buckets, (0, span - buckets.shape[0]), constant_values=-1)[None, :]
        == jnp.arange(n_b, dtype=jnp.int32)[:, None]
    )
    rel = jnp.pad(contract(table, onehot.astype(BF16), 1, 0), ((0, 8 - heads), (0, 0)))
    doc_row = segment_ids.reshape(1, length)
    doc_col = segment_ids.reshape(length, 1)
    projected, g_send = tie(projected, g_send)
    g_pieces = swap_chunks(g_send, "dp")
    attended, lse, *att_slots = attend_fwd(
        projected, rel, doc_row, doc_col, place_row, heads, n_t, rows_q
    )
    out_rel = lax.all_gather(jnp.stack(out_pieces), "shard", axis=0, tiled=False)
    out_lo, out_hi = (out_rel[i].reshape(n_t * own, half) for i in range(2))
    attended, att_slots, g_pieces, in_far, outw_far = tie(attended, att_slots, g_pieces, in_far, outw_far)
    w_in = [lax.all_gather(w, "shard", axis=0, tiled=True) for w in (expert_in[0], in_far)]
    w_out = [lax.all_gather(w, "shard", axis=0, tiled=False) for w in (expert_out[0], outw_far)]

    att_rows = swap_chunks(att_slots, "tensor")
    unit_two, inv_two, sent = middle(att_rows, out_rel, x_rows, gain_two, parts)

    if parts == 1:
        sent = [sent[0][k * quarter : (k + 1) * quarter] for k in range(n_d)]
    arrived = swap_chunks(sent, "dp")
    if parts == 1:
        arrived = [jnp.concatenate(arrived, axis=0)]
        g_own = [jnp.concatenate([p[:quarter] for p in g_send], axis=0)]
        g_sides = [
            [jnp.concatenate([p[r * quarter : (r + 1) * quarter] for p in g_pieces], axis=0)] for r in range(2)
        ]
        g_specs = [wholes(g) for g in g_sides]
    else:
        g_own = g_send
        g_sides = [g_pieces, g_pieces]
        at = lambda r: pl.BlockSpec((quarter, width), lambda i: (r, 0))
        g_specs = [[at(r)] * parts for r in range(2)]
    arrived_far = [partner(p, "tensor", 1) for p in arrived]

    near = expert(scalar(me_d), arrived, g_sides[0], g_specs[0], w_in, w_out, router, F32)
    far = expert(scalar(me_d), arrived_far, g_sides[1], g_specs[1], w_in, w_out, router, BF16)
    grad_far = partner(far[0][0], "tensor", 1)
    back = add_parts(near[0][0], grad_far, parts)
    if parts == 1:
        back = [back[0][k * quarter : (k + 1) * quarter] for k in range(n_d)]
    grad_two = swap_chunks(list(back), "dp")
    if parts == 1:
        grad_two = [jnp.concatenate(grad_two, axis=0)]
    res_own, res_other, router_part, wgrads = expert_late(scalar(me_s), [near, far], w_out)

    grad_mixed, gain_two_part, grad_att = second_norm_bwd(
        grad_two, g_own, g_specs[0], unit_two, inv_two, gain_two, out_rel
    )
    grad_att_slots = swap_chunks(list(grad_att), "tensor")
    drop_att = jnp.where(
        dropped,
        contract(cotangent[:, :half], out_rel[0, 0], 1, 1) + contract(cotangent[:, half:], out_rel[1, 0], 1, 1),
        0.0,
    ).astype(BF16)

    grad_q, grad_kt, grad_vt, drel = attend_bwd(
        projected, rel, doc_row, doc_col, lse, place_col, drop_att, grad_att_slots, heads
    )
    w_q, w_k, w_v = (qkv_full[:, i * own : (i + 1) * own] for i in range(3))
    grad_one = contract(grad_q, w_q, 1, 1) + contract(grad_kt, w_k, 0, 1) + contract(grad_vt, w_v, 0, 1)
    unit_one = inputs * inv_one
    gain_one_part = jnp.sum(grad_one * unit_one, axis=0)
    grad_one_q = scatter_sum(grad_one, "tensor")
    unit_q = chunk_of(unit_one, "tensor", 0)
    inv_q = chunk_of(inv_one, "tensor", 0)
    scaled_one = grad_one_q * gain_one
    delta = inv_q * (scaled_one - unit_q * jnp.mean(scaled_one * unit_q, axis=1, keepdims=True))
    delta_pieces = gather_pieces(delta.astype(BF16), "tensor")

    pick = (place_row == jnp.arange(n_t * rows_q, dtype=jnp.int32)[:, None]).astype(BF16)
    mixed_slots = jnp.concatenate(gather_pieces(grad_mixed, "tensor"), axis=0)
    mixed_tok = jnp.where(dropped, cotangent, contract(pick, mixed_slots, 0, 0).astype(BF16))
    grad_tokens = place_chunks(me_t, mixed_tok, delta_pieces)
    grad_out = pair_scatter(contract(attended, mixed_tok, 0, 0), 1)
    grad_out = join_chunks(scatter_sum(grad_out, "dp").astype(BF16), "dp").astype(F32)
    grad_qkv = jnp.concatenate(
        [contract(normed_one, grad_q, 0, 0), contract(normed_one, grad_kt, 0, 1), contract(normed_one, grad_vt, 0, 1)],
        axis=1,
    )
    grad_qkv = pair_scatter(grad_qkv, 0)
    grad_qkv = join_chunks(scatter_sum(grad_qkv, "dp").astype(BF16), "dp").astype(F32)

    res = list(add_parts(res_own, partner(res_other, "tensor", 1), parts))
    if parts == 1:
        res = [res[0][k * quarter : (k + 1) * quarter] for k in range(n_d)]
    res = jnp.concatenate(swap_chunks(res, "dp"), axis=0)
    res_slots = jnp.concatenate(gather_pieces(res, "tensor"), axis=0)
    att_all = jnp.concatenate(gather_pieces(attended, "tensor"), axis=1)
    residual = inputs + jnp.concatenate([contract(att_all, out_lo, 1, 0), contract(att_all, out_hi, 1, 0)], axis=1)
    output = (residual + contract(pick, res_slots, 0, 0)).astype(BF16)

    (in0, in0_other, out0, out0_other), (in1, in1_other, out1, out1_other) = wgrads
    pair = lambda mine, other: mine + partner(other, "shard", 1).astype(F32)
    far_in = partner(pair(in1, in1_other).astype(BF16), "tensor", 2).astype(F32)
    far_out = partner(pair(out1, out1_other).astype(BF16), "tensor", 2).astype(F32)
    grad_inw = (pair(in0, in0_other) + far_in)[None]
    grad_outw = (pair(out0, out0_other) + far_out)[None]

    grad_table = jnp.dot(drel[:heads], onehot.astype(F32).T, precision=HIGH)
    small = jnp.concatenate([gain_one_part[None], gain_two_part, router_part], axis=0)
    small = total_over(total_over(total_over(small, "shard"), "dp"), "tensor")
    small = lax.dynamic_slice_in_dim(small, me_s * half, half, 1)
    grad_table = total_over(total_over(grad_table, "shard"), "dp")
    grad_table = lax.dynamic_slice_in_dim(grad_table, me_s * (n_b // 2), n_b // 2, 1)
    return (
        output,
        grad_tokens,
        small[0],
        small[1],
        grad_qkv.reshape(half, 3, own),
        grad_out,
        grad_table,
        small[2:].T,
        grad_inw,
        grad_outw,
    )


def solution(mesh):
    placed = (
        P(("dp", "shard"), None),
        P(("dp", "shard"), None),
        P(),
        P(("dp", "shard")),
        P(("dp", "shard")),
        P(("dp", "shard")),
        P(("dp", "shard"), None),
        P("shard"),
        P("shard"),
        P("shard", None, "tensor"),
        P("tensor", "shard"),
        P("tensor", "shard"),
        P("shard", None),
        P("dp", "shard", "tensor"),
        P("dp", "tensor", "shard"),
    )
    return jax.shard_map(
        body,
        mesh=mesh,
        in_specs=placed,
        out_specs=(
            P(("dp", "shard"), None),
            P(("dp", "shard"), None),
            P("shard"),
            P("shard"),
            P("shard", None, "tensor"),
            P("tensor", "shard"),
            P("tensor", "shard"),
            P("shard", None),
            P("dp", "shard", "tensor"),
            P("dp", "tensor", "shard"),
        ),
        check_vma=False,
    )
```

```python
import functools

import jax
import jax.numpy as jnp
from jax import lax
from jax.experimental import pallas as pl
from jax.experimental.pallas import tpu as pltpu
from jax.sharding import PartitionSpec as P

DH = 64
EPS = 1e-06
NEG = -1e30
VMEM_MIB = 52
HIGH = lax.Precision.HIGHEST
BQ = 512
BQ_BACK = 1024
TB = 128
F32 = jnp.float32
BF16 = jnp.bfloat16


def contract(left, right, left_dim, right_dim):
    return lax.dot_general(
        left, right, (((left_dim,), (right_dim,)), ((), ())), preferred_element_type=F32
    )


def partner(value, axis, step):
    size = lax.axis_size(axis)
    return lax.ppermute(value, axis, [(i, i ^ step) for i in range(size)])


def swap_chunks(chunks, axis):
    return [chunks[0]] + [partner(c, axis, k) for k, c in enumerate(chunks) if k]


def gather_pieces(value, axis):
    return swap_chunks([value] * lax.axis_size(axis), axis)


def pick_rows(place_row, start, rows):
    at = lax.broadcasted_iota(jnp.int32, (rows, place_row.shape[1]), 0) + start
    return (at == place_row).astype(F32).astype(BF16)


def as_col(row):
    wide = jnp.broadcast_to(row.astype(F32), (128, row.shape[1]))
    return wide.T[:, :1].astype(jnp.int32)


def pick_cols(place_col, start, rows):
    at = lax.broadcasted_iota(jnp.int32, (place_col.shape[0], rows), 1) + start
    return (at == place_col).astype(F32).astype(BF16)


def shear_table(rel_ref, table_ref, heads, span):
    for h in range(heads):
        row = jnp.broadcast_to(rel_ref[h : h + 1, :], (TB, span))
        table_ref[h] = pltpu.roll(row, span - (TB - 1), 1, stride=1, stride_axis=0)


def table_starts(step, rows, length):
    last = length // TB - 1
    return [pl.multiple_of((last - step * (rows // TB) - a) * TB, TB) for a in range(rows // TB)]


def bias_of(table_ref, h, starts, length):
    return jnp.concatenate([table_ref[h, :, pl.ds(at, length)] for at in starts], axis=0)


def attend_fwd_kernel(
    qkv_ref, rel_ref, doc_row_ref, place_ref, out_ref, lse_ref, *rest, heads
):
    slot_refs, table_ref = rest[:-1], rest[-1]
    length = qkv_ref.shape[0]
    blocks = length // BQ
    width = heads * DH
    step = pl.program_id(0)

    @pl.when(step == 0)
    def _():
        shear_table(rel_ref, table_ref, heads, table_ref.shape[2])

    row0 = pl.multiple_of(step * BQ, BQ)
    starts = table_starts(step, BQ, length)
    same = as_col(doc_row_ref[:, pl.ds(row0, BQ)]) == doc_row_ref[...]
    outs, stats = [], []
    for h in range(heads):
        q = qkv_ref[pl.ds(row0, BQ), h * DH : (h + 1) * DH] * 0.125
        k = qkv_ref[:, width + h * DH : width + (h + 1) * DH]
        v = qkv_ref[:, 2 * width + h * DH : 2 * width + (h + 1) * DH]
        s = contract(q, k, 1, 1) + bias_of(table_ref, h, starts, length)
        s = jnp.where(same, s, NEG)
        top = jnp.max(s, axis=1, keepdims=True)
        e = jnp.exp(s - top)
        total = jnp.sum(e, axis=1, keepdims=True)
        o = contract(e.astype(BF16), v, 1, 0)
        outs.append(o * (1.0 / total))
        stats.append(top + jnp.log(total))
    out_ref[pl.ds(row0, BQ), :] = jnp.concatenate(outs, axis=1).astype(BF16)
    lse_ref[...] = jnp.concatenate(stats, axis=1)

    @pl.when(step == blocks - 1)
    def _():
        place = place_ref[...]
        for n, ref in enumerate(slot_refs):
            ref[...] = contract(pick_rows(place, n * ref.shape[0], ref.shape[0]), out_ref[...], 1, 0).astype(BF16)


def attend_bwd_kernel(
    qkv_ref, rel_ref, doc_row_ref, lse_ref, place_ref, drop_ref, *rest, heads,
):
    slot_refs = rest[:-9]
    dq_ref, dk_ref, dv_ref, drel_ref, table_ref, acc_ref, dk_acc, dv_acc, grad_ref = rest[-9:]
    length = qkv_ref.shape[0]
    blocks = length // BQ_BACK
    width = heads * DH
    span = table_ref.shape[2]
    step = pl.program_id(0)

    @pl.when(step == 0)
    def _():
        shear_table(rel_ref, table_ref, heads, span)
        acc_ref[...] = jnp.zeros(acc_ref.shape, F32)
        dk_acc[...] = jnp.zeros(dk_acc.shape, F32)
        dv_acc[...] = jnp.zeros(dv_acc.shape, F32)
        grad = drop_ref[...].astype(F32)
        place = as_col(place_ref[...])
        for n, ref in enumerate(slot_refs):
            grad = grad + contract(pick_cols(place, n * ref.shape[0], ref.shape[0]), ref[...], 1, 0)
        grad_ref[...] = grad.astype(BF16)

    row0 = pl.multiple_of(step * BQ_BACK, BQ_BACK)
    starts = table_starts(step, BQ_BACK, length)
    same = as_col(doc_row_ref[:, pl.ds(row0, BQ_BACK)]) == doc_row_ref[...]
    dqs = []
    for h in range(heads):
        q = qkv_ref[pl.ds(row0, BQ_BACK), h * DH : (h + 1) * DH] * 0.125
        k = qkv_ref[:, width + h * DH : width + (h + 1) * DH]
        v = qkv_ref[:, 2 * width + h * DH : 2 * width + (h + 1) * DH]
        g = grad_ref[pl.ds(row0, BQ_BACK), h * DH : (h + 1) * DH]
        s = contract(q, k, 1, 1) + bias_of(table_ref, h, starts, length)
        s = jnp.where(same, s, NEG)
        p = jnp.exp(s - lse_ref[:, h : h + 1])
        dp = contract(g, v, 1, 1)
        inner = jnp.sum(p * dp, axis=1, keepdims=True)
        ds = p * (dp - inner)
        dsb = ds.astype(BF16)
        for a, at in enumerate(starts):
            acc_ref[h, :, pl.ds(at, length)] += ds[a * TB : (a + 1) * TB]
        dqs.append(0.125 * contract(dsb, k, 1, 0))
        dk_acc[h * DH : (h + 1) * DH, :] += contract(q, dsb, 0, 0)
        dv_acc[h * DH : (h + 1) * DH, :] += contract(g, p.astype(BF16), 0, 0)
    dq_ref[...] = jnp.concatenate(dqs, axis=1).astype(BF16)

    @pl.when(step == blocks - 1)
    def _():
        dk_ref[...] = dk_acc[...].astype(BF16)
        dv_ref[...] = dv_acc[...].astype(BF16)
        for h in range(heads):
            rows = acc_ref[h]
            half = TB // 2
            while half >= 1:
                rows = pltpu.roll(rows[:half], half, 1) + rows[half:]
                half //= 2
            drel_ref[h : h + 1, :] = rows


def whole(shape):
    return pl.BlockSpec(shape, lambda *i: (0,) * len(shape))


def wholes(arrays):
    return [whole(a.shape) for a in arrays]


def params():
    return pltpu.CompilerParams(vmem_limit_bytes=VMEM_MIB * 1024 * 1024)


def struct(shape, dtype):
    return jax.ShapeDtypeStruct(shape, dtype)


def attend_specs(length, heads, span):
    return [
        whole((length, 3 * heads * DH)),
        whole((8, span)),
        whole((1, length)),
    ]


def attend_fwd(projected, rel, doc_row, place_row, heads, parts, part_rows):
    length = projected.shape[0]
    span = rel.shape[1]
    width = heads * DH
    return pl.pallas_call(
        functools.partial(attend_fwd_kernel, heads=heads),
        grid=(length // BQ,),
        in_specs=attend_specs(length, heads, span) + [whole((1, length))],
        out_specs=[whole((length, width)), pl.BlockSpec((BQ, heads), lambda i: (i, 0))]
        + [whole((part_rows, width))] * parts,
        out_shape=[struct((length, width), BF16), struct((length, heads), F32)]
        + [struct((part_rows, width), BF16)] * parts,
        scratch_shapes=[pltpu.VMEM((heads, TB, span), F32)],
        compiler_params=params(),
        name="attend_fwd",
    )(projected, rel, doc_row, place_row)


def attend_bwd(projected, rel, doc_row, lse, place_row, drop, grads, heads):
    length = projected.shape[0]
    span = rel.shape[1]
    width = heads * DH
    return pl.pallas_call(
        functools.partial(attend_bwd_kernel, heads=heads),
        grid=(length // BQ_BACK,),
        in_specs=attend_specs(length, heads, span)
        + [pl.BlockSpec((BQ_BACK, heads), lambda i: (i, 0)), whole((1, length)), whole((length, width))]
        + wholes(grads),
        out_specs=[
            pl.BlockSpec((BQ_BACK, width), lambda i: (i, 0)),
            whole((width, length)),
            whole((width, length)),
            whole((8, span)),
        ],
        out_shape=[
            struct((length, width), BF16),
            struct((width, length), BF16),
            struct((width, length), BF16),
            struct((8, span), F32),
        ],
        scratch_shapes=[
            pltpu.VMEM((heads, TB, span), F32),
            pltpu.VMEM((heads, TB, span), F32),
            pltpu.VMEM((width, length), F32),
            pltpu.VMEM((width, length), F32),
            pltpu.VMEM((length, width), BF16),
        ],
        compiler_params=params(),
        name="attend_bwd",
    )(projected, rel, doc_row, lse, place_row, drop, *grads)


def store_parts(refs, value):
    if len(refs) == 1:
        refs[0][...] = value
        return
    rows = refs[0].shape[0]
    for n, ref in enumerate(refs):
        ref[...] = value[n * rows : (n + 1) * rows]


def load_parts(refs):
    if len(refs) == 1:
        return refs[0][...]
    return jnp.concatenate([ref[...] for ref in refs], axis=0)


def slot_rows_kernel(me_ref, routes_ref, kept_ref, slots_ref, cot_ref, tok_ref, rel_ref, abs_ref, x_ref, *g_refs, quarter, n_t, rows_q):
    slots = slots_ref[...]
    part = jnp.zeros(slots.shape, jnp.int32)
    for k in range(1, n_t):
        part = part + (slots >= k * quarter).astype(jnp.int32)
    spot = slots - part * quarter
    taken = kept_ref[...] > 0
    rel_t = part ^ me_ref[0]
    rel_d = routes_ref[...] ^ me_ref[1]
    rel = jnp.where(taken, rel_t * rows_q + rel_d * quarter + spot, -1)
    rel_ref[...] = rel
    abs_ref[...] = jnp.where(taken, part * rows_q + rel_d * quarter + spot, -1)
    place_g = jnp.where(taken & (rel_t < 2), (rel_d * 2 + rel_t) * quarter + spot, -1)
    rows = g_refs[0].shape[0]
    for n, ref in enumerate(g_refs):
        ref[...] = contract(pick_rows(place_g, n * rows, rows), cot_ref[...], 1, 0).astype(BF16)
    x_ref[...] = contract(pick_rows(rel, 0, x_ref.shape[0]), tok_ref[...], 1, 0).astype(BF16)


def slot_rows(me, routes, kept, slots, cotangent, tokens, quarter, n_t, rows_q, parts, part_rows):
    length, width = tokens.shape
    shapes = [struct((1, length), jnp.int32)] * 2 + [struct((rows_q, width), BF16)]
    shapes += [struct((part_rows, width), BF16)] * parts
    operands = [routes.reshape(1, -1), kept.reshape(1, -1), slots.reshape(1, -1), cotangent, tokens]
    out = pl.pallas_call(
        functools.partial(slot_rows_kernel, quarter=quarter, n_t=n_t, rows_q=rows_q),
        grid=(1,),
        in_specs=[pl.BlockSpec(memory_space=pltpu.SMEM)] + wholes(operands),
        out_specs=[whole(v.shape) for v in shapes],
        out_shape=shapes,
        compiler_params=params(),
        name="slot_rows",
    )(me, *operands)
    return out[0], out[1], out[2], out[3:]


def first_norm_kernel(me_ref, tok_ref, gain_ref, w_ref, w_far_ref, normed_ref, inv_ref, proj_ref, full_ref):
    half = w_ref.shape[0]
    mine = pl.multiple_of(me_ref[0] * half, half)
    theirs = pl.multiple_of((1 - me_ref[0]) * half, half)
    x = tok_ref[...].astype(F32)
    inv = lax.rsqrt(jnp.mean(x * x, axis=1, keepdims=True) + EPS)
    inv_ref[...] = inv
    normed_ref[...] = (x * inv * gain_ref[...]).astype(BF16)
    proj_ref[...] = (
        contract(normed_ref[:, pl.ds(mine, half)], w_ref[...], 1, 0)
        + contract(normed_ref[:, pl.ds(theirs, half)], w_far_ref[...], 1, 0)
    ).astype(BF16)

    @pl.when(pl.program_id(0) == 0)
    def _():
        full_ref[pl.ds(mine, half), :] = w_ref[...]
        full_ref[pl.ds(theirs, half), :] = w_far_ref[...]


def first_norm(me_s, tokens, gain, w_own, w_far):
    length, width = tokens.shape
    out_width = w_own.shape[1]
    rows = length // 4
    block = lambda n: pl.BlockSpec((rows, n), lambda i: (i, 0))
    return pl.pallas_call(
        first_norm_kernel,
        grid=(4,),
        in_specs=[pl.BlockSpec(memory_space=pltpu.SMEM), block(width)] + wholes([gain, w_own, w_far]),
        out_specs=[block(width), block(1), block(out_width), whole((width, out_width))],
        out_shape=[
            struct((length, width), BF16),
            struct((length, 1), F32),
            struct((length, out_width), BF16),
            struct((width, out_width), BF16),
        ],
        compiler_params=params(),
        name="first_norm",
    )(me_s, tokens, gain, w_own, w_far)


def middle_kernel(me_ref, *refs, n_t, parts):
    att, (w_ref, x_ref, gain_ref) = refs[:n_t], refs[n_t : n_t + 3]
    unit_ref, inv_ref = refs[n_t + 3 : n_t + 5]
    outs = refs[n_t + 5 :]
    sides = []
    for half in range(2):
        total = contract(att[0][...], w_ref[me_ref[0], half], 1, 0)
        for k in range(1, n_t):
            total = total + contract(att[k][...], w_ref[me_ref[0] ^ k, half], 1, 0)
        sides.append(total)
    resid = x_ref[...].astype(F32) + jnp.concatenate(sides, axis=1)
    inv = lax.rsqrt(jnp.mean(resid * resid, axis=1, keepdims=True) + EPS)
    unit = resid * inv
    unit_ref[...] = unit
    inv_ref[...] = inv
    store_parts(outs, (unit * gain_ref[...]).astype(BF16))


def middle(me_t, att, w_rel, x_rows, gain, parts):
    rows, width = x_rows.shape
    operands = (*att, w_rel, x_rows, gain)
    shapes = [struct((rows, width), F32), struct((rows, 1), F32)]
    shapes += [struct((rows // parts, width), BF16)] * parts
    out = pl.pallas_call(
        functools.partial(middle_kernel, n_t=len(att), parts=parts),
        grid=(1,),
        in_specs=[pl.BlockSpec(memory_space=pltpu.SMEM)] + wholes(operands),
        out_specs=[whole(v.shape) for v in shapes],
        out_shape=shapes,
        compiler_params=params(),
        name="second_norm",
    )(me_t, *operands)
    return out[0], out[1], out[2:]


def expert_kernel(me_ref, *refs, parts, chunks, n_e):
    refs, (win_buf, wout_buf, sems) = refs[:-3], refs[-3:]
    rows_refs, g_refs = refs[:parts], refs[parts : 2 * parts]
    pieces, router_ref = refs[2 * parts : 2 * parts + 8], refs[2 * parts + 8]
    outs = refs[2 * parts + 9 :]
    half = pieces[0].shape[0]
    mine = pl.multiple_of(me_ref[1] * half, half)
    theirs = pl.multiple_of((1 - me_ref[1]) * half, half)
    copies = []
    for c in range(chunks):
        in_own, in_other, out_own, out_other = pieces[4 * c : 4 * c + 4]
        group = [
            (in_own, win_buf.at[c, pl.ds(mine, half)]),
            (in_other, win_buf.at[c, pl.ds(theirs, half)]),
            (out_own, wout_buf.at[c, me_ref[1]]),
            (out_other, wout_buf.at[c, 1 - me_ref[1]]),
        ]
        copies.append([pltpu.make_async_copy(a, b, sems.at[4 * c + i]) for i, (a, b) in enumerate(group)])
        for copy in copies[-1]:
            copy.start()
    grad_ref, rows_ref, slot_ref, gate_ref, logit_ref = outs[:5]
    hid_refs, gpre_refs = outs[5 : 5 + chunks], outs[5 + chunks :]
    rows = load_parts(rows_refs)
    g = load_parts(g_refs)
    router = router_ref[...]
    logits = contract(rows, router, 1, 1)
    exp_logits = jnp.exp(logits - jnp.max(logits, axis=1, keepdims=True))
    probs = exp_logits / jnp.sum(exp_logits, axis=1, keepdims=True)
    chosen = (lax.broadcasted_iota(jnp.int32, logits.shape, 1) == me_ref[0]).astype(F32)
    gate = jnp.sum(probs * chosen, axis=1, keepdims=True)
    grad_gate = jnp.zeros(gate.shape, F32)
    total = None
    for c in range(chunks):
        copies[c][0].wait()
        copies[c][1].wait()
        pre = contract(rows, win_buf[c], 1, 0)
        value, slope = gelu_pair(pre)
        hidden = value.astype(BF16)
        hid_refs[c][...] = hidden
        copies[c][2].wait()
        copies[c][3].wait()
        raw = contract(g[:, :half], wout_buf[c, 0], 1, 1) + contract(g[:, half:], wout_buf[c, 1], 1, 1)
        grad_gate = grad_gate + jnp.sum(hidden.astype(F32) * raw, axis=1, keepdims=True)
        grad_pre = (gate * raw * slope).astype(BF16)
        gpre_refs[c][...] = grad_pre
        part = contract(grad_pre, win_buf[c], 1, 1)
        total = part if total is None else total + part
    grad_logits = (grad_gate * probs * (chosen - gate)).astype(BF16)
    total = total + contract(grad_logits, router, 1, 0)
    grad_ref[...] = total.astype(grad_ref.dtype)
    rows_ref[...] = rows
    slot_ref[...] = (gate * g.astype(F32)).astype(BF16)
    gate_ref[...] = gate
    logit_ref[...] = grad_logits


def expert(me, rows, g, g_specs, weights, router, grad_dtype):
    parts, chunks = len(rows), 2
    total = sum(r.shape[0] for r in rows)
    width = rows[0].shape[1]
    hidden = weights[0].shape[1]
    n_e = router.shape[0]
    out = pl.pallas_call(
        functools.partial(expert_kernel, parts=parts, chunks=chunks, n_e=n_e),
        grid=(1,),
        in_specs=[pl.BlockSpec(memory_space=pltpu.SMEM)]
        + wholes(rows) + g_specs + [pl.BlockSpec(memory_space=pltpu.HBM)] * 8 + [whole(router.shape)],
        out_specs=[
            whole((total, width)), whole((total, width)), whole((total, width)), whole((total, 1)), whole((total, n_e))
        ] + [whole((total, hidden))] * (2 * chunks),
        out_shape=[
            struct((total, width), grad_dtype),
            struct((total, width), BF16),
            struct((total, width), BF16),
            struct((total, 1), F32),
            struct((total, n_e), BF16),
        ]
        + [struct((total, hidden), BF16)] * (2 * chunks),
        scratch_shapes=[
            pltpu.VMEM((chunks, width, hidden), BF16),
            pltpu.VMEM((chunks, 2, hidden, width // 2), BF16),
            pltpu.SemaphoreType.DMA((8,)),
        ],
        compiler_params=params(),
        name="expert",
    )(me, *rows, *g, *weights, router)
    return out[:5], out[5 : 5 + chunks], out[5 + chunks :]


def expert_late_kernel(me_ref, *refs, groups, chunks):
    side = lambda n: refs[n * groups : (n + 1) * groups]
    rows, slot, gate, logit = (side(n) for n in range(4))
    at = 4 * groups
    hid = [refs[at + c * groups : at + (c + 1) * groups] for c in range(chunks)]
    at += chunks * groups
    gpre = [refs[at + c * groups : at + (c + 1) * groups] for c in range(chunks)]
    at += chunks * groups
    out_own, out_other, far_out_own, far_out_other = refs[at : at + 4]
    res_own, res_other, router_ref, near_in, near_out, far_own, others = refs[at + 4 :]
    half = rows[0].shape[1] // 2
    mine = pl.multiple_of(me_ref[0] * half, half)
    theirs = pl.multiple_of((1 - me_ref[0]) * half, half)
    for r, ref in enumerate((res_own, res_other)):
        for start, near, far in ((mine, out_own, far_out_own), (theirs, out_other, far_out_other)):
            total = contract(hid[0][r][...], near[...], 1, 0) + contract(hid[1][r][...], far[...], 1, 0)
            ref[:, pl.ds(start, half)] = (gate[r][...] * total).astype(ref.dtype)
    router_ref[...] = contract(logit[0][...], rows[0][...], 0, 0) + contract(logit[1][...], rows[1][...], 0, 0)
    both = lambda refs, start: jnp.concatenate([ref[:, pl.ds(start, half)] for ref in refs], axis=0)
    rows_mine, rows_theirs = both(rows, mine).T, both(rows, theirs).T
    slot_mine, slot_theirs = both(slot, mine), both(slot, theirs)
    for c in range(chunks):
        grads = jnp.concatenate([ref[...] for ref in gpre[c]], axis=0)
        units = jnp.concatenate([ref[...] for ref in hid[c]], axis=0).T
        others[2 * c] = contract(rows_theirs, grads, 1, 0).astype(BF16)
        out_t = contract(units, slot_theirs, 1, 0).astype(BF16)
        others[2 * c + 1, :, :half] = out_t[:half]
        others[2 * c + 1, :, half:] = out_t[half:]
        in_m = contract(rows_mine, grads, 1, 0)
        out_m = contract(units, slot_mine, 1, 0)
        if c == 0:
            near_in[...] = in_m
            near_out[...] = out_m
        else:
            far_own[0] = in_m
            far_own[1, :, :half] = out_m[:half]
            far_own[1, :, half:] = out_m[half:]


def grad_sum_kernel(near_in, near_out, other_ref, far_ref, in_ref, out_ref):
    half = near_in.shape[0]
    in_ref[...] = near_in[...] + other_ref[0].astype(F32) + far_ref[0].astype(F32)
    side = other_ref[1].astype(F32) + far_ref[1].astype(F32)
    out_ref[:half] = near_out[:half] + side[:, :half]
    out_ref[half:] = near_out[half:] + side[:, half:]


def grad_sum(near_in, near_out, others, far):
    return pl.pallas_call(
        grad_sum_kernel,
        grid=(1,),
        in_specs=wholes([near_in, near_out]) + [whole((2,) + others.shape[1:]), whole(far.shape)],
        out_specs=wholes([near_in, near_out]),
        out_shape=[struct(near_in.shape, F32), struct(near_out.shape, F32)],
        compiler_params=params(),
        name="grad_sum",
    )(near_in, near_out, others, far)


def layer_output_kernel(place_ref, tok_ref, att_ref, w_ref, slots_ref, out_ref, *, n_t):
    sides = []
    for half in range(2):
        total = contract(att_ref[0], w_ref[0, half], 1, 0)
        for k in range(1, n_t):
            total = total + contract(att_ref[k], w_ref[k, half], 1, 0)
        sides.append(total)
    resid = tok_ref[...].astype(F32) + jnp.concatenate(sides, axis=1)
    found = contract(pick_cols(as_col(place_ref[...]), 0, slots_ref.shape[0]), slots_ref[...], 1, 0)
    out_ref[...] = (resid + found).astype(BF16)


def layer_output(place_row, tokens, att_all, w_all, res_slots):
    length, width = tokens.shape
    n_t, _, own = att_all.shape
    rows = length // 4
    block = lambda n: pl.BlockSpec((rows, n), lambda i: (i, 0))
    return pl.pallas_call(
        functools.partial(layer_output_kernel, n_t=n_t),
        grid=(4,),
        in_specs=[
            pl.BlockSpec((1, rows), lambda i: (0, i)), block(width), pl.BlockSpec((n_t, rows, own), lambda i: (0, i, 0)),
            whole(w_all.shape), whole(res_slots.shape),
        ],
        out_specs=block(width),
        out_shape=struct((length, width), BF16),
        compiler_params=params(),
        name="layer_output",
    )(place_row, tokens, att_all, w_all, res_slots)


def expert_late(me_s, groups, w_out):
    chunks = 2
    operands = []
    for n in (1, 2, 3, 4):
        operands += [grp[0][n] for grp in groups]
    for kind in (1, 2):
        for c in range(chunks):
            operands += [grp[kind][c] for grp in groups]
    operands += list(w_out)
    rows, width = groups[0][0][1].shape
    hidden = groups[0][1][0].shape[1]
    n_e = groups[0][0][4].shape[1]
    half = width // 2
    shapes = [struct((rows, width), F32), struct((rows, width), BF16), struct((n_e, width), F32)]
    shapes += [
        struct((half, hidden), F32), struct((hidden, half), F32),
        struct((2, half, hidden), F32), struct((4, half, hidden), BF16),
    ]
    out = pl.pallas_call(
        functools.partial(expert_late_kernel, groups=len(groups), chunks=chunks),
        grid=(1,),
        in_specs=[pl.BlockSpec(memory_space=pltpu.SMEM)] + wholes(operands),
        out_specs=[whole(s.shape) for s in shapes],
        out_shape=shapes,
        compiler_params=params(),
        name="expert_late",
    )(me_s, *operands)
    return out[:3], out[3:]


def add_parts_kernel(own_ref, other_ref, *outs):
    store_parts(outs, (own_ref[...] + other_ref[...].astype(F32)).astype(BF16))


def add_parts(own, other, parts):
    rows, width = own.shape
    return pl.pallas_call(
        add_parts_kernel,
        out_shape=[struct((rows // parts, width), BF16)] * parts,
        compiler_params=params(),
        name="add_parts",
    )(own, other)


def second_norm_bwd_kernel(me_ref, *refs, parts, n_t):
    grads, g_refs = refs[:parts], refs[parts : 2 * parts]
    unit_ref, inv_ref, gain_ref, w_ref, mixed_ref, gain_out_ref = refs[2 * parts : 2 * parts + 6]
    outs = refs[2 * parts + 6 :]
    grad = load_parts(grads).astype(F32)
    unit = unit_ref[...]
    gain_out_ref[...] = jnp.sum(grad * unit, axis=0, keepdims=True)
    scaled = grad * gain_ref[...]
    resid = load_parts(g_refs).astype(F32) + inv_ref[...] * (
        scaled - unit * jnp.mean(scaled * unit, axis=1, keepdims=True)
    )
    mixed = resid.astype(BF16)
    mixed_ref[...] = mixed
    half = mixed.shape[1] // 2
    for k, ref in enumerate(outs):
        at = me_ref[0] ^ k
        ref[...] = (
            contract(mixed[:, :half], w_ref[at, 0], 1, 1) + contract(mixed[:, half:], w_ref[at, 1], 1, 1)
        ).astype(BF16)


def second_norm_bwd(me_t, grads, g, g_specs, unit, inv, gain, w_rel):
    rows, width = unit.shape
    n_t, own = w_rel.shape[0], w_rel.shape[2]
    shapes = [struct((rows, width), BF16), struct((1, width), F32)] + [struct((rows, own), BF16)] * n_t
    out = pl.pallas_call(
        functools.partial(second_norm_bwd_kernel, parts=len(grads), n_t=n_t),
        grid=(1,),
        in_specs=[pl.BlockSpec(memory_space=pltpu.SMEM)]
        + wholes(grads) + g_specs + wholes([unit, inv, gain, w_rel]),
        out_specs=[whole(s.shape) for s in shapes],
        out_shape=shapes,
        compiler_params=params(),
        name="second_norm_bwd",
    )(me_t, *grads, *g, unit, inv, gain, w_rel)
    return out[0], out[1], out[2:]


def first_norm_bwd_kernel(order_ref, dq_ref, dk_ref, dv_ref, w_ref, tok_ref, inv_ref, proj_ref, gain_ref, own_ref, *sends):
    step = pl.program_id(0)
    flip = lambda ref: ref[...].astype(F32).T.astype(BF16)
    grads = jnp.concatenate([dq_ref[...], flip(dk_ref), flip(dv_ref)], axis=1)
    proj_ref[...] = grads
    part = contract(grads, w_ref[...], 1, 1)

    @pl.when(step == 0)
    def _():
        gain_ref[...] = jnp.zeros(gain_ref.shape, F32)
        own_ref[...] = part

    gain_ref[...] += jnp.sum(part * (tok_ref[...].astype(F32) * inv_ref[...]), axis=0, keepdims=True)
    for k, ref in enumerate(sends):

        @pl.when(step == k + 1)
        def _():
            ref[...] = part.astype(BF16)


def first_norm_bwd(order, grad_q, grad_kt, grad_vt, qkv_full, tokens, inv):
    count = order.shape[0]
    length, width = tokens.shape
    own = grad_q.shape[1]
    rows = length // count
    block = lambda n: pl.BlockSpec((rows, n), lambda i, order: (order[i], 0))
    side = pl.BlockSpec((own, rows), lambda i, order: (0, order[i]))
    out = pl.pallas_call(
        first_norm_bwd_kernel,
        grid_spec=pltpu.PrefetchScalarGridSpec(
            num_scalar_prefetch=1,
            grid=(count,),
            in_specs=[block(own), side, side, whole(qkv_full.shape), block(width), block(1)],
            out_specs=[block(3 * own), whole((1, width))] + [whole((rows, width))] * count,
        ),
        out_shape=[struct((length, 3 * own), BF16), struct((1, width), F32), struct((rows, width), F32)]
        + [struct((rows, width), BF16)] * (count - 1),
        compiler_params=params(),
        name="first_norm_bwd",
    )(order, grad_q, grad_kt, grad_vt, qkv_full, tokens, inv)
    return out[0], out[1], out[2], out[3:]


def token_delta_kernel(order_ref, tok_ref, inv_ref, gain_ref, own_ref, *refs):
    got, out_ref = refs[:-1], refs[-1]
    grad = own_ref[...]
    for ref in got:
        grad = grad + ref[...].astype(F32)
    inv = inv_ref[...]
    unit = tok_ref[...].astype(F32) * inv
    scaled = grad * gain_ref[...]
    out_ref[...] = (inv * (scaled - unit * jnp.mean(scaled * unit, axis=1, keepdims=True))).astype(BF16)


def token_delta(order, tokens, inv, gain, own, got):
    rows, width = own.shape
    block = lambda n: pl.BlockSpec((rows, n), lambda i, order: (order[0], 0))
    return pl.pallas_call(
        token_delta_kernel,
        grid_spec=pltpu.PrefetchScalarGridSpec(
            num_scalar_prefetch=1,
            grid=(1,),
            in_specs=[block(width), block(1)] + wholes([gain, own, *got]),
            out_specs=whole((rows, width)),
        ),
        out_shape=struct((rows, width), BF16),
        compiler_params=params(),
        name="token_delta",
    )(order, tokens, inv, gain, own, *got)


def weight_pack_kernel(me_ref, place_ref, cot_ref, att_ref, normed_ref, proj_ref, small_ref, *refs, half):
    slot_refs, (mixed_ref, own_ref, other_ref, acc_ref) = refs[:-4], refs[-4:]
    rows = att_ref.shape[1]
    mine = pl.multiple_of(me_ref[0] * half, half)
    theirs = pl.multiple_of((1 - me_ref[0]) * half, half)
    step = pl.program_id(0)
    place = as_col(place_ref[...])
    found = jnp.zeros(cot_ref.shape, F32)
    for n, ref in enumerate(slot_refs):
        found = found + contract(pick_cols(place, n * ref.shape[0], ref.shape[0]), ref[...], 1, 0)
    mixed_ref[...] = jnp.where(place < 0, cot_ref[...], found.astype(BF16))

    @pl.when(step == 0)
    def _():
        for ref, start in ((own_ref, mine), (acc_ref, theirs)):
            ref[...] = jnp.zeros(ref.shape, F32)
            ref[half + rows :, :half] = small_ref[:, pl.ds(start, half)]

    proj = proj_ref[...]
    att = att_ref[...]
    for ref, start in ((own_ref, mine), (acc_ref, theirs)):
        ref[:half] += contract(normed_ref[:, pl.ds(start, half)], proj, 0, 0)
        ref[half : half + rows, :half] += contract(att, mixed_ref[:, pl.ds(start, half)], 0, 0)

    @pl.when(step == pl.num_programs(0) - 1)
    def _():
        other_ref[...] = acc_ref[...].astype(BF16)


def weight_pack(me_s, place_row, cotangent, attended, normed, proj, small, mixed_slots):
    length, width = normed.shape
    own = attended.shape[1]
    shape = (width // 2 + own + small.shape[0], proj.shape[1])
    rows = length // 4
    block = lambda n: pl.BlockSpec((rows, n), lambda i: (i, 0))
    return pl.pallas_call(
        functools.partial(weight_pack_kernel, half=width // 2),
        grid=(4,),
        in_specs=[
            pl.BlockSpec(memory_space=pltpu.SMEM), pl.BlockSpec((1, rows), lambda i: (0, i)),
            block(width), block(own), block(width), block(proj.shape[1]), whole(small.shape),
        ]
        + wholes(mixed_slots),
        out_specs=[block(width), whole(shape), whole(shape)],
        out_shape=[struct((length, width), BF16), struct(shape, F32), struct(shape, BF16)],
        scratch_shapes=[pltpu.VMEM(shape, F32)],
        compiler_params=params(),
        name="weight_pack",
    )(me_s, place_row, cotangent, attended, normed, proj, small, *mixed_slots)


def pair_sum_kernel(order_ref, own_ref, other_ref, keep_ref, *sends):
    total = own_ref[...] + other_ref[...].astype(F32)
    step = pl.program_id(0)

    @pl.when(step == 0)
    def _():
        keep_ref[...] = total

    for k, ref in enumerate(sends):

        @pl.when(step == k + 1)
        def _():
            ref[...] = total.astype(BF16)


def pair_sum(order, own, other):
    count = order.shape[0]
    rows, width = own.shape[0] // count, own.shape[1]
    block = pl.BlockSpec((rows, width), lambda i, order: (order[i], 0))
    out = pl.pallas_call(
        pair_sum_kernel,
        grid_spec=pltpu.PrefetchScalarGridSpec(
            num_scalar_prefetch=1,
            grid=(count,),
            in_specs=[block, block],
            out_specs=[whole((rows, width))] * count,
        ),
        out_shape=[struct((rows, width), F32)] + [struct((rows, width), BF16)] * (count - 1),
        compiler_params=params(),
        name="pair_sum",
    )(order, own, other)
    return out[0], out[1:]


def place_chunks_kernel(order_ref, *refs, count):
    step = pl.program_id(0)
    out_ref = refs[-1]
    for k in range(count):

        @pl.when(step == k)
        def _():
            value = refs[len(refs) - 1 - count + k][...].astype(F32)
            out_ref[...] = value if len(refs) == count + 1 else refs[0][...].astype(F32) + value


def place_chunks(order, base, pieces):
    count = len(pieces)
    rows, width = pieces[0].shape
    at = lambda i, order: (order[i], 0)
    bases = [] if base is None else [base]
    return pl.pallas_call(
        functools.partial(place_chunks_kernel, count=count),
        grid_spec=pltpu.PrefetchScalarGridSpec(
            num_scalar_prefetch=1,
            grid=(count,),
            in_specs=[pl.BlockSpec((rows, width), at) for _ in bases] + wholes(pieces),
            out_specs=pl.BlockSpec((rows, width), at),
        ),
        out_shape=struct((count * rows, width), F32),
        compiler_params=params(),
        name="place_chunks",
    )(order, *bases, *pieces)


def gelu_pair(pre):
    root = 0.7978845608028654
    cubic = 0.044715
    square = pre * pre
    th = jnp.tanh(root * pre * (1.0 + cubic * square))
    value = 0.5 * pre * (1.0 + th)
    slope = 0.5 * (1.0 + th) + 0.5 * pre * (1.0 - th * th) * root * (1.0 + 3.0 * cubic * square)
    return value, slope


def total_over(value, axis):
    for piece in gather_pieces(value, axis)[1:]:
        value = value + piece
    return value


def tie(*values):
    return lax.optimization_barrier(values)


def body(
    tokens, segment_ids, buckets, routes, kept, slots, cotangent, norm_one, norm_two,
    qkv_weight, out_weight, bias_table, router_weight, expert_in, expert_out,
):
    n_t = lax.axis_size("tensor")
    n_d = lax.axis_size("dp")
    me_t = lax.axis_index("tensor")
    me_d = lax.axis_index("dp")
    me_s = lax.axis_index("shard")
    length, width = tokens.shape
    heads = qkv_weight.shape[2] // DH
    own = heads * DH
    n_e = router_weight.shape[1]
    n_b = 2 * bias_table.shape[1]
    capacity = 5 * length // (4 * n_d)
    quarter = capacity // n_t
    rows_q = n_d * quarter
    parts = n_d if quarter % 16 == 0 else 1
    half = width // 2
    scalar = lambda v: v.astype(jnp.int32).reshape(1)

    me_td = jnp.stack([me_t, me_d]).astype(jnp.int32)

    out_all = lax.all_gather(out_weight, ("tensor", "shard"), axis=0, tiled=False)
    out_all = out_all.reshape(n_t, 2, own, half)
    in_own, outw_own = expert_in[0], expert_out[0]
    in_far = partner(in_own, "tensor", 2)
    outw_far = partner(outw_own, "tensor", 2)
    in_other = partner(in_own, "shard", 1)
    outw_other = partner(outw_own, "shard", 1)
    order_d = (me_d ^ jnp.arange(n_d, dtype=jnp.int32)).astype(jnp.int32)
    order = (me_t ^ jnp.arange(n_t, dtype=jnp.int32)).astype(jnp.int32)
    table_row = jnp.pad(bias_table.reshape(1, -1), ((0, 0), (0, half - heads * (n_b // 2))))
    packed = jnp.concatenate([norm_one[None], norm_two[None], router_weight.T, table_row], axis=0)
    packed_far = partner(packed, "shard", 1)
    qkv_own = qkv_weight.reshape(half, 3 * own)
    qkv_far = partner(qkv_own, "shard", 1)

    place_row, place_abs, x_rows, g_send = slot_rows(
        me_td, routes, kept, slots, cotangent, tokens, quarter, n_t, rows_q, parts, 2 * rows_q // parts
    )
    if parts == 1:
        g_send = [g_send[0][k * 2 * quarter : (k + 1) * 2 * quarter] for k in range(n_d)]

    packed_far, qkv_far, x_rows, g_send = tie(packed_far, qkv_far, x_rows, g_send)
    g_pieces = swap_chunks(g_send, "dp")
    packed = jnp.where(
        me_s == 0,
        jnp.concatenate([packed, packed_far], axis=1),
        jnp.concatenate([packed_far, packed], axis=1),
    )
    gain_one = packed[:1].astype(F32)
    gain_two = packed[1:2].astype(F32)
    router = packed[2 : 2 + n_e]
    table = packed[2 + n_e].reshape(2, half)[:, : heads * (n_b // 2)]
    table = table.reshape(2, heads, n_b // 2).transpose(1, 0, 2).reshape(heads, n_b)

    inputs = tokens.astype(F32)
    normed_one, inv_one, projected, qkv_full = first_norm(scalar(me_s), tokens, gain_one, qkv_own, qkv_far)
    span = 2 * length
    onehot = (
        jnp.pad(buckets, (0, span - buckets.shape[0]), constant_values=-1)[None, :]
        == jnp.arange(n_b, dtype=jnp.int32)[:, None]
    )
    rel = jnp.pad(contract(table, onehot.astype(BF16), 1, 0), ((0, 8 - heads), (0, 0)))
    doc_row = segment_ids.reshape(1, length)
    attended, lse, *att_slots = attend_fwd(
        projected, rel, doc_row, place_row, heads, n_t, rows_q
    )
    attended, att_slots, g_pieces, in_far, outw_far = tie(attended, att_slots, g_pieces, in_far, outw_far)
    weights = (in_own, in_other, outw_own, outw_other)
    weights += (in_far, partner(in_far, "shard", 1), outw_far, partner(outw_far, "shard", 1))
    me_ds = jnp.stack([me_d, me_s]).astype(jnp.int32)

    att_rows = swap_chunks(att_slots, "tensor")
    att_ag, *att_rows = tie(attended, *att_rows)
    att_all = lax.all_gather(att_ag, "tensor", axis=0, tiled=False)
    unit_two, inv_two, sent = middle(scalar(me_t), att_rows, out_all, x_rows, gain_two, parts)

    if parts == 1:
        sent = [sent[0][k * quarter : (k + 1) * quarter] for k in range(n_d)]
    arrived = swap_chunks(sent, "dp")
    drop_att = jnp.where(
        (kept == 0)[:, None],
        contract(cotangent[:, :half], out_all[me_t, 0], 1, 1) + contract(cotangent[:, half:], out_all[me_t, 1], 1, 1),
        0.0,
    ).astype(BF16)
    drop_att, arrived = tie(drop_att, arrived)
    if parts == 1:
        arrived = [jnp.concatenate(arrived, axis=0)]
        g_own = [jnp.concatenate([p[:quarter] for p in g_send], axis=0)]
        g_sides = [
            [jnp.concatenate([p[r * quarter : (r + 1) * quarter] for p in g_pieces], axis=0)] for r in range(2)
        ]
        g_specs = [wholes(g) for g in g_sides]
    else:
        g_own = g_send
        g_sides = [g_pieces, g_pieces]
        at = lambda r: pl.BlockSpec((quarter, width), lambda i: (r, 0))
        g_specs = [[at(r)] * parts for r in range(2)]
    arrived_far = [partner(p, "tensor", 1) for p in arrived]

    near = expert(me_ds, arrived, g_sides[0], g_specs[0], weights, router, F32)
    near, arrived_far = tie(near, arrived_far)
    far = expert(me_ds, arrived_far, g_sides[1], g_specs[1], weights, router, BF16)
    grad_far = partner(far[0][0], "tensor", 1)
    late = expert_late(scalar(me_s), [near, far], weights[2:4] + weights[6:])
    grad_far, late = tie(grad_far, late)
    (res_own, res_other, router_part), (near_in, near_out, far_own, others) = late
    res_far = partner(res_other, "tensor", 1)
    others = partner(others, "shard", 1)
    far_sum = partner((far_own + others[2:].astype(F32)).astype(BF16), "tensor", 2)
    back = add_parts(near[0][0], grad_far, parts)
    if parts == 1:
        back = [back[0][k * quarter : (k + 1) * quarter] for k in range(n_d)]
    grad_two = swap_chunks(list(back), "dp")
    if parts == 1:
        grad_two = [jnp.concatenate(grad_two, axis=0)]

    grad_mixed, gain_two_part, grad_att = second_norm_bwd(
        scalar(me_t), grad_two, g_own, g_specs[0], unit_two, inv_two, gain_two, out_all
    )
    grad_att_slots = swap_chunks(list(grad_att), "tensor")
    grad_mixed_ag, res_far, *grad_att_slots = tie(grad_mixed, res_far, *grad_att_slots)
    mixed_slots = gather_pieces(grad_mixed_ag, "tensor")
    res = list(add_parts(res_own, res_far, parts))
    if parts == 1:
        res = [res[0][k * quarter : (k + 1) * quarter] for k in range(n_d)]
    res = swap_chunks(res, "dp")

    grad_q, grad_kt, grad_vt, drel = attend_bwd(
        projected, rel, doc_row, lse, place_row, drop_att, grad_att_slots, heads
    )
    grad_q, grad_kt, grad_vt, drel, res, att_all, mixed_slots = tie(
        grad_q, grad_kt, grad_vt, drel, res, att_all, mixed_slots
    )
    res_slots = lax.all_gather(jnp.concatenate(res, axis=0), "tensor", axis=0, tiled=True)
    grad_proj, gain_one_part, grad_one, sends = first_norm_bwd(
        order, grad_q, grad_kt, grad_vt, qkv_full, tokens, inv_one
    )
    sends, grad_proj = tie(sends, grad_proj)
    got = [partner(v, "tensor", k + 1) for k, v in enumerate(sends)]

    grad_table = jnp.dot(drel[:heads], onehot.astype(F32).T, precision=HIGH)
    small = jnp.concatenate([gain_one_part, gain_two_part, router_part], axis=0)
    n_small = 2 + n_e
    fill = -(half + own + n_small + 1) % (16 * n_d)
    table_row = grad_table.reshape(heads, 2, n_b // 2).transpose(1, 0, 2).reshape(1, 2, heads * n_b // 2)
    table_row = jnp.pad(table_row, ((0, fill), (0, 0), (0, half - heads * n_b // 2))).reshape(fill + 1, width)
    small = jnp.concatenate([small, table_row], axis=0)
    mixed_tok, total, theirs = weight_pack(
        scalar(me_s), place_row, cotangent, attended, normed_one, grad_proj, small, mixed_slots
    )
    got, total, theirs, mixed_tok, far_sum = tie(got, total, theirs, mixed_tok, far_sum)
    theirs = partner(theirs, "shard", 1)
    delta = token_delta(order, tokens, inv_one, gain_one, grad_one, got)
    theirs, delta = tie(theirs, delta)
    delta_pieces = gather_pieces(delta, "tensor")
    total, sends = pair_sum(order_d, total, theirs)
    for k, piece in enumerate(sends):
        total = total + partner(piece, "dp", k + 1).astype(F32)
    grad_inw, grad_outw = grad_sum(near_in, near_out, others, far_sum)
    grad_tokens = place_chunks(order, mixed_tok, delta_pieces)
    pieces = gather_pieces(total.astype(BF16), "dp")
    pieces, grad_tokens = tie(pieces, grad_tokens)
    total = place_chunks(order_d, None, pieces)
    grad_qkv = total[:half]
    grad_out = total[half : half + own, :half]
    small = total_over(total[half + own : half + own + n_small, :half], "tensor")
    grad_table = total[half + own + n_small, : heads * n_b // 2].reshape(heads, n_b // 2)

    output = layer_output(place_abs, tokens, att_all, out_all, res_slots)
    return (
        output,
        grad_tokens,
        small[0],
        small[1],
        grad_qkv.reshape(half, 3, own),
        grad_out,
        grad_table,
        small[2:].T,
        grad_inw[None],
        grad_outw[None],
    )


def solution(mesh):
    placed = (
        P(("dp", "shard"), None),
        P(("dp", "shard"), None),
        P(),
        P(("dp", "shard")),
        P(("dp", "shard")),
        P(("dp", "shard")),
        P(("dp", "shard"), None),
        P("shard"),
        P("shard"),
        P("shard", None, "tensor"),
        P("tensor", "shard"),
        P("tensor", "shard"),
        P("shard", None),
        P("dp", "shard", "tensor"),
        P("dp", "tensor", "shard"),
    )
    return jax.shard_map(
        body,
        mesh=mesh,
        in_specs=placed,
        out_specs=(
            P(("dp", "shard"), None),
            P(("dp", "shard"), None),
            P("shard"),
            P("shard"),
            P("shard", None, "tensor"),
            P("tensor", "shard"),
            P("tensor", "shard"),
            P("shard", None),
            P("dp", "shard", "tensor"),
            P("dp", "tensor", "shard"),
        ),
        check_vma=False,
    )
```

```python
import functools

import jax
import jax.numpy as jnp
from jax import lax
from jax.experimental import pallas as pl
from jax.experimental.pallas import tpu as pltpu
from jax.sharding import PartitionSpec as P

DH = 64
EPS = 1e-06
NEG = -1e30
VMEM_MIB = 52
HIGH = lax.Precision.HIGHEST
BQ = 512
BQ_BACK = 1024
TB = 128
F32 = jnp.float32
BF16 = jnp.bfloat16


def contract(left, right, left_dim, right_dim):
    return lax.dot_general(
        left, right, (((left_dim,), (right_dim,)), ((), ())), preferred_element_type=F32
    )


def partner(value, axis, step):
    size = lax.axis_size(axis)
    return lax.ppermute(value, axis, [(i, i ^ step) for i in range(size)])


def swap_chunks(chunks, axis):
    return [chunks[0]] + [partner(c, axis, k) for k, c in enumerate(chunks) if k]


def gather_pieces(value, axis):
    return swap_chunks([value] * lax.axis_size(axis), axis)


def pick_rows(place_row, start, rows):
    at = lax.broadcasted_iota(jnp.int32, (rows, place_row.shape[1]), 0) + start
    return (at == place_row).astype(F32).astype(BF16)


def as_col(row):
    wide = jnp.broadcast_to(row.astype(F32), (128, row.shape[1]))
    return wide.T[:, :1].astype(jnp.int32)


def pick_cols(place_col, start, rows):
    at = lax.broadcasted_iota(jnp.int32, (place_col.shape[0], rows), 1) + start
    return (at == place_col).astype(F32).astype(BF16)


def shear_table(rel_ref, table_ref, heads, span):
    for h in range(heads):
        row = jnp.broadcast_to(rel_ref[h : h + 1, :], (TB, span))
        table_ref[h] = pltpu.roll(row, span - (TB - 1), 1, stride=1, stride_axis=0)


def table_starts(step, rows, length):
    last = length // TB - 1
    return [pl.multiple_of((last - step * (rows // TB) - a) * TB, TB) for a in range(rows // TB)]


def bias_of(table_ref, h, starts, length):
    return jnp.concatenate([table_ref[h, :, pl.ds(at, length)] for at in starts], axis=0)


def attend_fwd_kernel(
    qkv_ref, rel_ref, doc_row_ref, place_ref, out_ref, lse_ref, *rest, heads
):
    slot_refs, table_ref = rest[:-1], rest[-1]
    length = qkv_ref.shape[0]
    blocks = length // BQ
    width = heads * DH
    step = pl.program_id(0)

    @pl.when(step == 0)
    def _():
        shear_table(rel_ref, table_ref, heads, table_ref.shape[2])

    row0 = pl.multiple_of(step * BQ, BQ)
    starts = table_starts(step, BQ, length)
    same = as_col(doc_row_ref[:, pl.ds(row0, BQ)]) == doc_row_ref[...]
    outs, stats = [], []
    for h in range(heads):
        q = qkv_ref[pl.ds(row0, BQ), h * DH : (h + 1) * DH] * 0.125
        k = qkv_ref[:, width + h * DH : width + (h + 1) * DH]
        v = qkv_ref[:, 2 * width + h * DH : 2 * width + (h + 1) * DH]
        s = contract(q, k, 1, 1) + bias_of(table_ref, h, starts, length)
        s = jnp.where(same, s, NEG)
        top = jnp.max(s, axis=1, keepdims=True)
        e = jnp.exp(s - top)
        total = jnp.sum(e, axis=1, keepdims=True)
        o = contract(e.astype(BF16), v, 1, 0)
        outs.append(o * (1.0 / total))
        stats.append(top + jnp.log(total))
    out_ref[pl.ds(row0, BQ), :] = jnp.concatenate(outs, axis=1).astype(BF16)
    lse_ref[...] = jnp.concatenate(stats, axis=1)

    @pl.when(step == blocks - 1)
    def _():
        place = place_ref[...]
        for n, ref in enumerate(slot_refs):
            ref[...] = contract(pick_rows(place, n * ref.shape[0], ref.shape[0]), out_ref[...], 1, 0).astype(BF16)


def attend_bwd_kernel(
    qkv_ref, rel_ref, doc_row_ref, lse_ref, place_ref, drop_ref, *rest, heads,
):
    slot_refs = rest[:-9]
    dq_ref, dk_ref, dv_ref, drel_ref, table_ref, acc_ref, dk_acc, dv_acc, grad_ref = rest[-9:]
    length = qkv_ref.shape[0]
    blocks = length // BQ_BACK
    width = heads * DH
    span = table_ref.shape[2]
    step = pl.program_id(0)

    @pl.when(step == 0)
    def _():
        shear_table(rel_ref, table_ref, heads, span)
        acc_ref[...] = jnp.zeros(acc_ref.shape, F32)
        dk_acc[...] = jnp.zeros(dk_acc.shape, F32)
        dv_acc[...] = jnp.zeros(dv_acc.shape, F32)
        grad = drop_ref[...].astype(F32)
        place = as_col(place_ref[...])
        for n, ref in enumerate(slot_refs):
            grad = grad + contract(pick_cols(place, n * ref.shape[0], ref.shape[0]), ref[...], 1, 0)
        grad_ref[...] = grad.astype(BF16)

    row0 = pl.multiple_of(step * BQ_BACK, BQ_BACK)
    starts = table_starts(step, BQ_BACK, length)
    same = as_col(doc_row_ref[:, pl.ds(row0, BQ_BACK)]) == doc_row_ref[...]
    dqs = []
    for h in range(heads):
        q = qkv_ref[pl.ds(row0, BQ_BACK), h * DH : (h + 1) * DH] * 0.125
        k = qkv_ref[:, width + h * DH : width + (h + 1) * DH]
        v = qkv_ref[:, 2 * width + h * DH : 2 * width + (h + 1) * DH]
        g = grad_ref[pl.ds(row0, BQ_BACK), h * DH : (h + 1) * DH]
        s = contract(q, k, 1, 1) + bias_of(table_ref, h, starts, length)
        s = jnp.where(same, s, NEG)
        p = jnp.exp(s - lse_ref[:, h : h + 1])
        dp = contract(g, v, 1, 1)
        inner = jnp.sum(p * dp, axis=1, keepdims=True)
        ds = p * (dp - inner)
        dsb = ds.astype(BF16)
        for a, at in enumerate(starts):
            acc_ref[h, :, pl.ds(at, length)] += ds[a * TB : (a + 1) * TB]
        dqs.append(0.125 * contract(dsb, k, 1, 0))
        dk_acc[h * DH : (h + 1) * DH, :] += contract(q, dsb, 0, 0)
        dv_acc[h * DH : (h + 1) * DH, :] += contract(g, p.astype(BF16), 0, 0)
    dq_ref[...] = jnp.concatenate(dqs, axis=1).astype(BF16)

    @pl.when(step == blocks - 1)
    def _():
        dk_ref[...] = dk_acc[...].astype(BF16)
        dv_ref[...] = dv_acc[...].astype(BF16)
        for h in range(heads):
            rows = acc_ref[h]
            half = TB // 2
            while half >= 1:
                rows = pltpu.roll(rows[:half], half, 1) + rows[half:]
                half //= 2
            drel_ref[h : h + 1, :] = rows


def whole(shape):
    return pl.BlockSpec(shape, lambda *i: (0,) * len(shape))


def wholes(arrays):
    return [whole(a.shape) for a in arrays]


def params():
    return pltpu.CompilerParams(vmem_limit_bytes=VMEM_MIB * 1024 * 1024)


def struct(shape, dtype):
    return jax.ShapeDtypeStruct(shape, dtype)


def attend_specs(length, heads, span):
    return [
        whole((length, 3 * heads * DH)),
        whole((8, span)),
        whole((1, length)),
    ]


def attend_fwd(projected, rel, doc_row, place_row, heads, parts, part_rows):
    length = projected.shape[0]
    span = rel.shape[1]
    width = heads * DH
    return pl.pallas_call(
        functools.partial(attend_fwd_kernel, heads=heads),
        grid=(length // BQ,),
        in_specs=attend_specs(length, heads, span) + [whole((1, length))],
        out_specs=[whole((length, width)), pl.BlockSpec((BQ, heads), lambda i: (i, 0))]
        + [whole((part_rows, width))] * parts,
        out_shape=[struct((length, width), BF16), struct((length, heads), F32)]
        + [struct((part_rows, width), BF16)] * parts,
        scratch_shapes=[pltpu.VMEM((heads, TB, span), F32)],
        compiler_params=params(),
        name="attend_fwd",
    )(projected, rel, doc_row, place_row)


def attend_bwd(projected, rel, doc_row, lse, place_row, drop, grads, heads):
    length = projected.shape[0]
    span = rel.shape[1]
    width = heads * DH
    return pl.pallas_call(
        functools.partial(attend_bwd_kernel, heads=heads),
        grid=(length // BQ_BACK,),
        in_specs=attend_specs(length, heads, span)
        + [pl.BlockSpec((BQ_BACK, heads), lambda i: (i, 0)), whole((1, length)), whole((length, width))]
        + wholes(grads),
        out_specs=[
            pl.BlockSpec((BQ_BACK, width), lambda i: (i, 0)),
            whole((width, length)),
            whole((width, length)),
            whole((8, span)),
        ],
        out_shape=[
            struct((length, width), BF16),
            struct((width, length), BF16),
            struct((width, length), BF16),
            struct((8, span), F32),
        ],
        scratch_shapes=[
            pltpu.VMEM((heads, TB, span), F32),
            pltpu.VMEM((heads, TB, span), F32),
            pltpu.VMEM((width, length), F32),
            pltpu.VMEM((width, length), F32),
            pltpu.VMEM((length, width), BF16),
        ],
        compiler_params=params(),
        name="attend_bwd",
    )(projected, rel, doc_row, lse, place_row, drop, *grads)


def store_parts(refs, value):
    if len(refs) == 1:
        refs[0][...] = value
        return
    rows = refs[0].shape[0]
    for n, ref in enumerate(refs):
        ref[...] = value[n * rows : (n + 1) * rows]


def load_parts(refs):
    if len(refs) == 1:
        return refs[0][...]
    return jnp.concatenate([ref[...] for ref in refs], axis=0)


def slot_rows_kernel(me_ref, routes_ref, kept_ref, slots_ref, cot_ref, tok_ref, rel_ref, abs_ref, x_ref, *g_refs, quarter, n_t, rows_q):
    slots = slots_ref[...]
    part = jnp.zeros(slots.shape, jnp.int32)
    for k in range(1, n_t):
        part = part + (slots >= k * quarter).astype(jnp.int32)
    spot = slots - part * quarter
    taken = kept_ref[...] > 0
    rel_t = part ^ me_ref[0]
    rel_d = routes_ref[...] ^ me_ref[1]
    rel = jnp.where(taken, rel_t * rows_q + rel_d * quarter + spot, -1)
    rel_ref[...] = rel
    abs_ref[...] = jnp.where(taken, part * rows_q + rel_d * quarter + spot, -1)
    place_g = jnp.where(taken & (rel_t < 2), (rel_d * 2 + rel_t) * quarter + spot, -1)
    rows = g_refs[0].shape[0]
    for n, ref in enumerate(g_refs):
        ref[...] = contract(pick_rows(place_g, n * rows, rows), cot_ref[...], 1, 0).astype(BF16)
    x_ref[...] = contract(pick_rows(rel, 0, x_ref.shape[0]), tok_ref[...], 1, 0).astype(BF16)


def slot_rows(me, routes, kept, slots, cotangent, tokens, quarter, n_t, rows_q, parts, part_rows):
    length, width = tokens.shape
    shapes = [struct((1, length), jnp.int32)] * 2 + [struct((rows_q, width), BF16)]
    shapes += [struct((part_rows, width), BF16)] * parts
    operands = [routes.reshape(1, -1), kept.reshape(1, -1), slots.reshape(1, -1), cotangent, tokens]
    out = pl.pallas_call(
        functools.partial(slot_rows_kernel, quarter=quarter, n_t=n_t, rows_q=rows_q),
        grid=(1,),
        in_specs=[pl.BlockSpec(memory_space=pltpu.SMEM)] + wholes(operands),
        out_specs=[whole(v.shape) for v in shapes],
        out_shape=shapes,
        compiler_params=params(),
        name="slot_rows",
    )(me, *operands)
    return out[0], out[1], out[2], out[3:]


def first_norm_kernel(me_ref, tok_ref, gain_ref, w_ref, w_far_ref, normed_ref, inv_ref, proj_ref, full_ref):
    half = w_ref.shape[0]
    mine = pl.multiple_of(me_ref[0] * half, half)
    theirs = pl.multiple_of((1 - me_ref[0]) * half, half)
    x = tok_ref[...].astype(F32)
    inv = lax.rsqrt(jnp.mean(x * x, axis=1, keepdims=True) + EPS)
    inv_ref[...] = inv
    normed_ref[...] = (x * inv * gain_ref[...]).astype(BF16)
    proj_ref[...] = (
        contract(normed_ref[:, pl.ds(mine, half)], w_ref[...], 1, 0)
        + contract(normed_ref[:, pl.ds(theirs, half)], w_far_ref[...], 1, 0)
    ).astype(BF16)

    @pl.when(pl.program_id(0) == 0)
    def _():
        full_ref[pl.ds(mine, half), :] = w_ref[...]
        full_ref[pl.ds(theirs, half), :] = w_far_ref[...]


def first_norm(me_s, tokens, gain, w_own, w_far):
    length, width = tokens.shape
    out_width = w_own.shape[1]
    rows = length // 4
    block = lambda n: pl.BlockSpec((rows, n), lambda i: (i, 0))
    return pl.pallas_call(
        first_norm_kernel,
        grid=(4,),
        in_specs=[pl.BlockSpec(memory_space=pltpu.SMEM), block(width)] + wholes([gain, w_own, w_far]),
        out_specs=[block(width), block(1), block(out_width), whole((width, out_width))],
        out_shape=[
            struct((length, width), BF16),
            struct((length, 1), F32),
            struct((length, out_width), BF16),
            struct((width, out_width), BF16),
        ],
        compiler_params=params(),
        name="first_norm",
    )(me_s, tokens, gain, w_own, w_far)


def middle_kernel(me_ref, *refs, n_t, parts):
    att, (w_ref, x_ref, gain_ref) = refs[:n_t], refs[n_t : n_t + 3]
    unit_ref, inv_ref = refs[n_t + 3 : n_t + 5]
    outs = refs[n_t + 5 :]
    sides = []
    for half in range(2):
        total = contract(att[0][...], w_ref[me_ref[0], half], 1, 0)
        for k in range(1, n_t):
            total = total + contract(att[k][...], w_ref[me_ref[0] ^ k, half], 1, 0)
        sides.append(total)
    resid = x_ref[...].astype(F32) + jnp.concatenate(sides, axis=1)
    inv = lax.rsqrt(jnp.mean(resid * resid, axis=1, keepdims=True) + EPS)
    unit = resid * inv
    unit_ref[...] = unit
    inv_ref[...] = inv
    store_parts(outs, (unit * gain_ref[...]).astype(BF16))


def middle(me_t, att, w_rel, x_rows, gain, parts):
    rows, width = x_rows.shape
    operands = (*att, w_rel, x_rows, gain)
    shapes = [struct((rows, width), F32), struct((rows, 1), F32)]
    shapes += [struct((rows // parts, width), BF16)] * parts
    out = pl.pallas_call(
        functools.partial(middle_kernel, n_t=len(att), parts=parts),
        grid=(1,),
        in_specs=[pl.BlockSpec(memory_space=pltpu.SMEM)] + wholes(operands),
        out_specs=[whole(v.shape) for v in shapes],
        out_shape=shapes,
        compiler_params=params(),
        name="second_norm",
    )(me_t, *operands)
    return out[0], out[1], out[2:]


def expert_kernel(me_ref, *refs, parts, chunks, n_e):
    refs, (win_buf, wout_buf, sems) = refs[:-3], refs[-3:]
    rows_refs, g_refs = refs[:parts], refs[parts : 2 * parts]
    pieces, router_ref = refs[2 * parts : 2 * parts + 4], refs[2 * parts + 4]
    outs = refs[2 * parts + 5 :]
    half = pieces[0].shape[1]
    mine = pl.multiple_of(me_ref[1] * half, half)
    theirs = pl.multiple_of((1 - me_ref[1]) * half, half)
    copies = []
    for c in range(chunks):
        moves = []
        for piece, start in ((pieces[2 * c], mine), (pieces[2 * c + 1], theirs)):
            moves.append((piece.at[0], win_buf.at[c, pl.ds(start, half)]))
        for piece, side in ((pieces[2 * c], me_ref[1]), (pieces[2 * c + 1], 1 - me_ref[1])):
            for n in range(2):
                part = pl.ds(n * half, half)
                moves.append((piece.at[1, :, part], wout_buf.at[c, side, part]))
        copies.append([pltpu.make_async_copy(a, b, sems.at[6 * c + i]) for i, (a, b) in enumerate(moves)])
        for copy in copies[-1]:
            copy.start()
    grad_ref, rows_ref, slot_ref, gate_ref, logit_ref = outs[:5]
    hid_refs, gpre_refs = outs[5 : 5 + chunks], outs[5 + chunks :]
    rows = load_parts(rows_refs)
    g = load_parts(g_refs)
    router = router_ref[...]
    logits = contract(rows, router, 1, 1)
    exp_logits = jnp.exp(logits - jnp.max(logits, axis=1, keepdims=True))
    probs = exp_logits / jnp.sum(exp_logits, axis=1, keepdims=True)
    chosen = (lax.broadcasted_iota(jnp.int32, logits.shape, 1) == me_ref[0]).astype(F32)
    gate = jnp.sum(probs * chosen, axis=1, keepdims=True)
    grad_gate = jnp.zeros(gate.shape, F32)
    total = None
    for c in range(chunks):
        for copy in copies[c][:2]:
            copy.wait()
        pre = contract(rows, win_buf[c], 1, 0)
        value, slope = gelu_pair(pre)
        hidden = value.astype(BF16)
        hid_refs[c][...] = hidden
        for copy in copies[c][2:]:
            copy.wait()
        raw = contract(g[:, :half], wout_buf[c, 0], 1, 1) + contract(g[:, half:], wout_buf[c, 1], 1, 1)
        grad_gate = grad_gate + jnp.sum(hidden.astype(F32) * raw, axis=1, keepdims=True)
        grad_pre = (gate * raw * slope).astype(BF16)
        gpre_refs[c][...] = grad_pre
        part = contract(grad_pre, win_buf[c], 1, 1)
        total = part if total is None else total + part
    grad_logits = (grad_gate * probs * (chosen - gate)).astype(BF16)
    total = total + contract(grad_logits, router, 1, 0)
    grad_ref[...] = total.astype(grad_ref.dtype)
    rows_ref[...] = rows
    slot_ref[...] = (gate * g.astype(F32)).astype(BF16)
    gate_ref[...] = gate
    logit_ref[...] = grad_logits


def expert(me, rows, g, g_specs, weights, router, grad_dtype):
    parts, chunks = len(rows), 2
    total = sum(r.shape[0] for r in rows)
    width = rows[0].shape[1]
    hidden = weights[0].shape[2]
    n_e = router.shape[0]
    out = pl.pallas_call(
        functools.partial(expert_kernel, parts=parts, chunks=chunks, n_e=n_e),
        grid=(1,),
        in_specs=[pl.BlockSpec(memory_space=pltpu.SMEM)]
        + wholes(rows) + g_specs + [pl.BlockSpec(memory_space=pltpu.HBM)] * 4 + [whole(router.shape)],
        out_specs=[
            whole((total, width)), whole((total, width)), whole((total, width)), whole((total, 1)), whole((total, n_e))
        ] + [whole((total, hidden))] * (2 * chunks),
        out_shape=[
            struct((total, width), grad_dtype),
            struct((total, width), BF16),
            struct((total, width), BF16),
            struct((total, 1), F32),
            struct((total, n_e), BF16),
        ]
        + [struct((total, hidden), BF16)] * (2 * chunks),
        scratch_shapes=[
            pltpu.VMEM((chunks, width, hidden), BF16),
            pltpu.VMEM((chunks, 2, hidden, width // 2), BF16),
            pltpu.SemaphoreType.DMA((12,)),
        ],
        compiler_params=params(),
        name="expert",
    )(me, *rows, *g, *weights, router)
    return out[:5], out[5 : 5 + chunks], out[5 + chunks :]


def expert_late_kernel(me_ref, *refs, groups, chunks):
    side = lambda n: refs[n * groups : (n + 1) * groups]
    rows, slot, gate, logit = (side(n) for n in range(4))
    at = 4 * groups
    hid = [refs[at + c * groups : at + (c + 1) * groups] for c in range(chunks)]
    at += chunks * groups
    gpre = [refs[at + c * groups : at + (c + 1) * groups] for c in range(chunks)]
    at += chunks * groups
    out_own, out_other, far_out_own, far_out_other = refs[at : at + 4]
    res_own, res_other, router_ref, near_in, near_out, far_own, others = refs[at + 4 :]
    half = rows[0].shape[1] // 2
    mine = pl.multiple_of(me_ref[0] * half, half)
    theirs = pl.multiple_of((1 - me_ref[0]) * half, half)
    for r, ref in enumerate((res_own, res_other)):
        for start, sides in ((mine, (out_own, far_out_own)), (theirs, (out_other, far_out_other))):
            total = jnp.zeros((ref.shape[0], half), F32)
            for c, side in enumerate(sides):
                for n in range(2):
                    part = slice(n * half, (n + 1) * half)
                    total = total + contract(hid[c][r][:, part], side[0, :, part], 1, 0)
            ref[:, pl.ds(start, half)] = (gate[r][...] * total).astype(ref.dtype)
    router_ref[...] = contract(logit[0][...], rows[0][...], 0, 0) + contract(logit[1][...], rows[1][...], 0, 0)
    both = lambda refs, start: jnp.concatenate([ref[:, pl.ds(start, half)] for ref in refs], axis=0)
    rows_mine, rows_theirs = both(rows, mine).T, both(rows, theirs).T
    slot_mine, slot_theirs = both(slot, mine), both(slot, theirs)
    for c in range(chunks):
        grads = jnp.concatenate([ref[...] for ref in gpre[c]], axis=0)
        units = jnp.concatenate([ref[...] for ref in hid[c]], axis=0).T
        others[2 * c] = contract(rows_theirs, grads, 1, 0).astype(BF16)
        out_t = contract(units, slot_theirs, 1, 0).astype(BF16)
        others[2 * c + 1, :, :half] = out_t[:half]
        others[2 * c + 1, :, half:] = out_t[half:]
        in_m = contract(rows_mine, grads, 1, 0)
        out_m = contract(units, slot_mine, 1, 0)
        if c == 0:
            near_in[...] = in_m
            near_out[...] = out_m
        else:
            far_own[0] = in_m
            far_own[1, :, :half] = out_m[:half]
            far_own[1, :, half:] = out_m[half:]


def grad_sum_kernel(near_in, near_out, other_ref, far_in, far_out, in_ref, out_ref):
    half = near_in.shape[0]
    in_ref[...] = near_in[...] + other_ref[0].astype(F32) + far_in[...].astype(F32)
    side = other_ref[1].astype(F32) + far_out[...].astype(F32)
    out_ref[:half] = near_out[:half] + side[:, :half]
    out_ref[half:] = near_out[half:] + side[:, half:]


def grad_sum(near_in, near_out, others, far):
    return pl.pallas_call(
        grad_sum_kernel,
        grid=(1,),
        in_specs=wholes([near_in, near_out]) + [whole((2,) + others.shape[1:])] + wholes(far),
        out_specs=wholes([near_in, near_out]),
        out_shape=[struct(near_in.shape, F32), struct(near_out.shape, F32)],
        compiler_params=params(),
        name="grad_sum",
    )(near_in, near_out, others, *far)


def layer_output_kernel(place_ref, tok_ref, att_ref, w_ref, slots_ref, out_ref, *, n_t):
    sides = []
    for half in range(2):
        total = contract(att_ref[0], w_ref[0, half], 1, 0)
        for k in range(1, n_t):
            total = total + contract(att_ref[k], w_ref[k, half], 1, 0)
        sides.append(total)
    resid = tok_ref[...].astype(F32) + jnp.concatenate(sides, axis=1)
    found = contract(pick_cols(as_col(place_ref[...]), 0, slots_ref.shape[0]), slots_ref[...], 1, 0)
    out_ref[...] = (resid + found).astype(BF16)


def layer_output(place_row, tokens, att_all, w_all, res_slots):
    length, width = tokens.shape
    n_t, _, own = att_all.shape
    rows = length // 4
    block = lambda n: pl.BlockSpec((rows, n), lambda i: (i, 0))
    return pl.pallas_call(
        functools.partial(layer_output_kernel, n_t=n_t),
        grid=(4,),
        in_specs=[
            pl.BlockSpec((1, rows), lambda i: (0, i)), block(width), pl.BlockSpec((n_t, rows, own), lambda i: (0, i, 0)),
            whole(w_all.shape), whole(res_slots.shape),
        ],
        out_specs=block(width),
        out_shape=struct((length, width), BF16),
        compiler_params=params(),
        name="layer_output",
    )(place_row, tokens, att_all, w_all, res_slots)


def expert_late(me_s, groups, w_out):
    chunks = 2
    operands = []
    for n in (1, 2, 3, 4):
        operands += [grp[0][n] for grp in groups]
    for kind in (1, 2):
        for c in range(chunks):
            operands += [grp[kind][c] for grp in groups]
    specs = wholes(operands) + [pl.BlockSpec((1,) + w.shape[1:], lambda i: (1, 0, 0)) for w in w_out]
    operands += list(w_out)
    rows, width = groups[0][0][1].shape
    hidden = groups[0][1][0].shape[1]
    n_e = groups[0][0][4].shape[1]
    half = width // 2
    shapes = [struct((rows, width), F32), struct((rows, width), BF16), struct((n_e, width), F32)]
    shapes += [
        struct((half, hidden), F32), struct((hidden, half), F32),
        struct((2, half, hidden), F32), struct((4, half, hidden), BF16),
    ]
    out = pl.pallas_call(
        functools.partial(expert_late_kernel, groups=len(groups), chunks=chunks),
        grid=(1,),
        in_specs=[pl.BlockSpec(memory_space=pltpu.SMEM)] + specs,
        out_specs=[whole(s.shape) for s in shapes],
        out_shape=shapes,
        compiler_params=params(),
        name="expert_late",
    )(me_s, *operands)
    return out[:3], out[3:]


def add_parts_kernel(own_ref, other_ref, *outs):
    store_parts(outs, (own_ref[...] + other_ref[...].astype(F32)).astype(BF16))


def add_parts(own, other, parts):
    rows, width = own.shape
    return pl.pallas_call(
        add_parts_kernel,
        out_shape=[struct((rows // parts, width), BF16)] * parts,
        compiler_params=params(),
        name="add_parts",
    )(own, other)


def second_norm_bwd_kernel(me_ref, *refs, parts, n_t):
    grads, g_refs = refs[:parts], refs[parts : 2 * parts]
    unit_ref, inv_ref, gain_ref, w_ref, mixed_ref, gain_out_ref = refs[2 * parts : 2 * parts + 6]
    outs = refs[2 * parts + 6 :]
    grad = load_parts(grads).astype(F32)
    unit = unit_ref[...]
    gain_out_ref[...] = jnp.sum(grad * unit, axis=0, keepdims=True)
    scaled = grad * gain_ref[...]
    resid = load_parts(g_refs).astype(F32) + inv_ref[...] * (
        scaled - unit * jnp.mean(scaled * unit, axis=1, keepdims=True)
    )
    mixed = resid.astype(BF16)
    mixed_ref[...] = mixed
    half = mixed.shape[1] // 2
    for k, ref in enumerate(outs):
        at = me_ref[0] ^ k
        ref[...] = (
            contract(mixed[:, :half], w_ref[at, 0], 1, 1) + contract(mixed[:, half:], w_ref[at, 1], 1, 1)
        ).astype(BF16)


def second_norm_bwd(me_t, grads, g, g_specs, unit, inv, gain, w_rel):
    rows, width = unit.shape
    n_t, own = w_rel.shape[0], w_rel.shape[2]
    shapes = [struct((rows, width), BF16), struct((1, width), F32)] + [struct((rows, own), BF16)] * n_t
    out = pl.pallas_call(
        functools.partial(second_norm_bwd_kernel, parts=len(grads), n_t=n_t),
        grid=(1,),
        in_specs=[pl.BlockSpec(memory_space=pltpu.SMEM)]
        + wholes(grads) + g_specs + wholes([unit, inv, gain, w_rel]),
        out_specs=[whole(s.shape) for s in shapes],
        out_shape=shapes,
        compiler_params=params(),
        name="second_norm_bwd",
    )(me_t, *grads, *g, unit, inv, gain, w_rel)
    return out[0], out[1], out[2:]


def first_norm_bwd_kernel(order_ref, dq_ref, dk_ref, dv_ref, w_ref, tok_ref, inv_ref, proj_ref, gain_ref, own_ref, *sends):
    step = pl.program_id(0)
    flip = lambda ref: ref[...].astype(F32).T.astype(BF16)
    grads = jnp.concatenate([dq_ref[...], flip(dk_ref), flip(dv_ref)], axis=1)
    proj_ref[...] = grads
    part = contract(grads, w_ref[...], 1, 1)

    @pl.when(step == 0)
    def _():
        gain_ref[...] = jnp.zeros(gain_ref.shape, F32)
        own_ref[...] = part

    gain_ref[...] += jnp.sum(part * (tok_ref[...].astype(F32) * inv_ref[...]), axis=0, keepdims=True)
    for k, ref in enumerate(sends):

        @pl.when(step == k + 1)
        def _():
            ref[...] = part.astype(BF16)


def first_norm_bwd(order, grad_q, grad_kt, grad_vt, qkv_full, tokens, inv):
    count = order.shape[0]
    length, width = tokens.shape
    own = grad_q.shape[1]
    rows = length // count
    block = lambda n: pl.BlockSpec((rows, n), lambda i, order: (order[i], 0))
    side = pl.BlockSpec((own, rows), lambda i, order: (0, order[i]))
    out = pl.pallas_call(
        first_norm_bwd_kernel,
        grid_spec=pltpu.PrefetchScalarGridSpec(
            num_scalar_prefetch=1,
            grid=(count,),
            in_specs=[block(own), side, side, whole(qkv_full.shape), block(width), block(1)],
            out_specs=[block(3 * own), whole((1, width))] + [whole((rows, width))] * count,
        ),
        out_shape=[struct((length, 3 * own), BF16), struct((1, width), F32), struct((rows, width), F32)]
        + [struct((rows, width), BF16)] * (count - 1),
        compiler_params=params(),
        name="first_norm_bwd",
    )(order, grad_q, grad_kt, grad_vt, qkv_full, tokens, inv)
    return out[0], out[1], out[2], out[3:]


def token_delta_kernel(order_ref, tok_ref, inv_ref, gain_ref, own_ref, *refs):
    got, out_ref = refs[:-1], refs[-1]
    grad = own_ref[...]
    for ref in got:
        grad = grad + ref[...].astype(F32)
    inv = inv_ref[...]
    unit = tok_ref[...].astype(F32) * inv
    scaled = grad * gain_ref[...]
    out_ref[...] = (inv * (scaled - unit * jnp.mean(scaled * unit, axis=1, keepdims=True))).astype(BF16)


def token_delta(order, tokens, inv, gain, own, got):
    rows, width = own.shape
    block = lambda n: pl.BlockSpec((rows, n), lambda i, order: (order[0], 0))
    return pl.pallas_call(
        token_delta_kernel,
        grid_spec=pltpu.PrefetchScalarGridSpec(
            num_scalar_prefetch=1,
            grid=(1,),
            in_specs=[block(width), block(1)] + wholes([gain, own, *got]),
            out_specs=whole((rows, width)),
        ),
        out_shape=struct((rows, width), BF16),
        compiler_params=params(),
        name="token_delta",
    )(order, tokens, inv, gain, own, *got)


def weight_pack_kernel(me_ref, place_ref, cot_ref, att_ref, normed_ref, proj_ref, small_ref, *refs, half):
    slot_refs, (mixed_ref, own_ref, other_ref, acc_ref) = refs[:-4], refs[-4:]
    rows = att_ref.shape[1]
    mine = pl.multiple_of(me_ref[0] * half, half)
    theirs = pl.multiple_of((1 - me_ref[0]) * half, half)
    step = pl.program_id(0)
    place = as_col(place_ref[...])
    found = jnp.zeros(cot_ref.shape, F32)
    for n, ref in enumerate(slot_refs):
        found = found + contract(pick_cols(place, n * ref.shape[0], ref.shape[0]), ref[...], 1, 0)
    mixed_ref[...] = jnp.where(place < 0, cot_ref[...], found.astype(BF16))

    @pl.when(step == 0)
    def _():
        for ref, start in ((own_ref, mine), (acc_ref, theirs)):
            ref[...] = jnp.zeros(ref.shape, F32)
            ref[half + rows :, :half] = small_ref[:, pl.ds(start, half)]

    proj = proj_ref[...]
    att = att_ref[...]
    for ref, start in ((own_ref, mine), (acc_ref, theirs)):
        ref[:half] += contract(normed_ref[:, pl.ds(start, half)], proj, 0, 0)
        ref[half : half + rows, :half] += contract(att, mixed_ref[:, pl.ds(start, half)], 0, 0)

    @pl.when(step == pl.num_programs(0) - 1)
    def _():
        other_ref[...] = acc_ref[...].astype(BF16)


def weight_pack(me_s, place_row, cotangent, attended, normed, proj, small, mixed_slots):
    length, width = normed.shape
    own = attended.shape[1]
    shape = (width // 2 + own + small.shape[0], proj.shape[1])
    rows = length // 4
    block = lambda n: pl.BlockSpec((rows, n), lambda i: (i, 0))
    return pl.pallas_call(
        functools.partial(weight_pack_kernel, half=width // 2),
        grid=(4,),
        in_specs=[
            pl.BlockSpec(memory_space=pltpu.SMEM), pl.BlockSpec((1, rows), lambda i: (0, i)),
            block(width), block(own), block(width), block(proj.shape[1]), whole(small.shape),
        ]
        + wholes(mixed_slots),
        out_specs=[block(width), whole(shape), whole(shape)],
        out_shape=[struct((length, width), BF16), struct(shape, F32), struct(shape, BF16)],
        scratch_shapes=[pltpu.VMEM(shape, F32)],
        compiler_params=params(),
        name="weight_pack",
    )(me_s, place_row, cotangent, attended, normed, proj, small, *mixed_slots)


def pair_sum_kernel(order_ref, own_ref, other_ref, keep_ref, *sends):
    total = own_ref[...] + other_ref[...].astype(F32)
    step = pl.program_id(0)

    @pl.when(step == 0)
    def _():
        keep_ref[...] = total

    for k, ref in enumerate(sends):

        @pl.when(step == k + 1)
        def _():
            ref[...] = total.astype(BF16)


def pair_sum(order, own, other):
    count = order.shape[0]
    rows, width = own.shape[0] // count, own.shape[1]
    block = pl.BlockSpec((rows, width), lambda i, order: (order[i], 0))
    out = pl.pallas_call(
        pair_sum_kernel,
        grid_spec=pltpu.PrefetchScalarGridSpec(
            num_scalar_prefetch=1,
            grid=(count,),
            in_specs=[block, block],
            out_specs=[whole((rows, width))] * count,
        ),
        out_shape=[struct((rows, width), F32)] + [struct((rows, width), BF16)] * (count - 1),
        compiler_params=params(),
        name="pair_sum",
    )(order, own, other)
    return out[0], out[1:]


def place_chunks_kernel(order_ref, base_ref, *refs, count):
    step = pl.program_id(0)
    out_ref = refs[-1]
    for k in range(count):

        @pl.when(step == k)
        def _():
            out_ref[...] = base_ref[...].astype(F32) + refs[k][...].astype(F32)


def place_chunks(order, base, pieces):
    count = len(pieces)
    rows, width = pieces[0].shape
    block = pl.BlockSpec((rows, width), lambda i, order: (order[i], 0))
    return pl.pallas_call(
        functools.partial(place_chunks_kernel, count=count),
        grid_spec=pltpu.PrefetchScalarGridSpec(
            num_scalar_prefetch=1, grid=(count,), in_specs=[block] + wholes(pieces), out_specs=block
        ),
        out_shape=struct((count * rows, width), F32),
        compiler_params=params(),
        name="place_chunks",
    )(order, base, *pieces)


def weight_unpack_kernel(order_ref, *refs):
    pieces, (qkv_ref, out_ref, rest_ref, all_ref) = refs[:-4], refs[-4:]
    rows = pieces[0].shape[0]
    for k, ref in enumerate(pieces):
        all_ref[pl.ds(pl.multiple_of(order_ref[k] * rows, rows), rows), :] = ref[...].astype(F32)
    first, second = qkv_ref.shape[0], qkv_ref.shape[0] + out_ref.shape[0]
    half = out_ref.shape[1]
    qkv_ref[...] = all_ref[:first]
    out_ref[...] = all_ref[first:second, :half]
    rest_ref[...] = all_ref[second:, :half]


def weight_unpack(order, pieces, half, own):
    rows, width = pieces[0].shape
    total = rows * len(pieces)
    shapes = [struct((half, width), F32), struct((own, half), F32), struct((total - half - own, half), F32)]
    return pl.pallas_call(
        weight_unpack_kernel,
        grid_spec=pltpu.PrefetchScalarGridSpec(
            num_scalar_prefetch=1,
            grid=(1,),
            in_specs=wholes(pieces),
            out_specs=[whole(v.shape) for v in shapes],
            scratch_shapes=[pltpu.VMEM((total, width), F32)],
        ),
        out_shape=shapes,
        compiler_params=params(),
        name="weight_unpack",
    )(order, *pieces)


def gelu_pair(pre):
    root = 0.7978845608028654
    cubic = 0.044715
    square = pre * pre
    th = jnp.tanh(root * pre * (1.0 + cubic * square))
    value = 0.5 * pre * (1.0 + th)
    slope = 0.5 * (1.0 + th) + 0.5 * pre * (1.0 - th * th) * root * (1.0 + 3.0 * cubic * square)
    return value, slope


def total_over(value, axis):
    for piece in gather_pieces(value, axis)[1:]:
        value = value + piece
    return value


def tie(*values):
    return lax.optimization_barrier(values)


def body(
    tokens, segment_ids, buckets, routes, kept, slots, cotangent, norm_one, norm_two,
    qkv_weight, out_weight, bias_table, router_weight, expert_in, expert_out,
):
    n_t = lax.axis_size("tensor")
    n_d = lax.axis_size("dp")
    me_t = lax.axis_index("tensor")
    me_d = lax.axis_index("dp")
    me_s = lax.axis_index("shard")
    length, width = tokens.shape
    heads = qkv_weight.shape[2] // DH
    own = heads * DH
    n_e = router_weight.shape[1]
    n_b = 2 * bias_table.shape[1]
    capacity = 5 * length // (4 * n_d)
    quarter = capacity // n_t
    rows_q = n_d * quarter
    parts = n_d if quarter % 16 == 0 else 1
    half = width // 2
    scalar = lambda v: v.astype(jnp.int32).reshape(1)

    me_td = jnp.stack([me_t, me_d]).astype(jnp.int32)

    out_all = lax.all_gather(out_weight, ("tensor", "shard"), axis=0, tiled=False)
    out_all = out_all.reshape(n_t, 2, own, half)
    split = expert_out.shape[1] // 2
    w_own = jnp.stack(
        [expert_in[0], jnp.concatenate([expert_out[0, :split], expert_out[0, split:]], axis=1)]
    )
    w_far = partner(w_own, "tensor", 2)
    w_other = partner(w_own, "shard", 1)
    order_d = (me_d ^ jnp.arange(n_d, dtype=jnp.int32)).astype(jnp.int32)
    order = (me_t ^ jnp.arange(n_t, dtype=jnp.int32)).astype(jnp.int32)
    table_row = jnp.pad(bias_table.reshape(1, -1), ((0, 0), (0, half - heads * (n_b // 2))))
    packed = jnp.concatenate([norm_one[None], norm_two[None], router_weight.T, table_row], axis=0)
    packed_far = partner(packed, "shard", 1)
    qkv_own = qkv_weight.reshape(half, 3 * own)
    qkv_far = partner(qkv_own, "shard", 1)

    place_row, place_abs, x_rows, g_send = slot_rows(
        me_td, routes, kept, slots, cotangent, tokens, quarter, n_t, rows_q, parts, 2 * rows_q // parts
    )
    if parts == 1:
        g_send = [g_send[0][k * 2 * quarter : (k + 1) * 2 * quarter] for k in range(n_d)]

    packed_far, qkv_far, x_rows, g_send = tie(packed_far, qkv_far, x_rows, g_send)
    g_pieces = swap_chunks(g_send, "dp")
    packed = jnp.where(
        me_s == 0,
        jnp.concatenate([packed, packed_far], axis=1),
        jnp.concatenate([packed_far, packed], axis=1),
    )
    gain_one = packed[:1].astype(F32)
    gain_two = packed[1:2].astype(F32)
    router = packed[2 : 2 + n_e]
    table = packed[2 + n_e].reshape(2, half)[:, : heads * (n_b // 2)]
    table = table.reshape(2, heads, n_b // 2).transpose(1, 0, 2).reshape(heads, n_b)

    inputs = tokens.astype(F32)
    normed_one, inv_one, projected, qkv_full = first_norm(scalar(me_s), tokens, gain_one, qkv_own, qkv_far)
    span = 2 * length
    onehot = (
        jnp.pad(buckets, (0, span - buckets.shape[0]), constant_values=-1)[None, :]
        == jnp.arange(n_b, dtype=jnp.int32)[:, None]
    )
    rel = jnp.pad(contract(table, onehot.astype(BF16), 1, 0), ((0, 8 - heads), (0, 0)))
    doc_row = segment_ids.reshape(1, length)
    attended, lse, *att_slots = attend_fwd(
        projected, rel, doc_row, place_row, heads, n_t, rows_q
    )
    attended, att_slots, g_pieces, w_far = tie(attended, att_slots, g_pieces, w_far)
    weights = (w_own, w_other, w_far, partner(w_far, "shard", 1))
    me_ds = jnp.stack([me_d, me_s]).astype(jnp.int32)

    att_rows = swap_chunks(att_slots, "tensor")
    att_ag, *att_rows = tie(attended, *att_rows)
    att_all = lax.all_gather(att_ag, "tensor", axis=0, tiled=False)
    unit_two, inv_two, sent = middle(scalar(me_t), att_rows, out_all, x_rows, gain_two, parts)

    if parts == 1:
        sent = [sent[0][k * quarter : (k + 1) * quarter] for k in range(n_d)]
    arrived = swap_chunks(sent, "dp")
    drop_att = jnp.where(
        (kept == 0)[:, None],
        contract(cotangent[:, :half], out_all[me_t, 0], 1, 1) + contract(cotangent[:, half:], out_all[me_t, 1], 1, 1),
        0.0,
    ).astype(BF16)
    far_first = partner(arrived[0], "tensor", 1) if parts > 1 else None
    drop_att, arrived, far_first = tie(drop_att, arrived, far_first)
    if parts == 1:
        arrived = [jnp.concatenate(arrived, axis=0)]
        g_own = [jnp.concatenate([p[:quarter] for p in g_send], axis=0)]
        g_sides = [
            [jnp.concatenate([p[r * quarter : (r + 1) * quarter] for p in g_pieces], axis=0)] for r in range(2)
        ]
        g_specs = [wholes(g) for g in g_sides]
    else:
        g_own = g_send
        g_sides = [g_pieces, g_pieces]
        at = lambda r: pl.BlockSpec((quarter, width), lambda i: (r, 0))
        g_specs = [[at(r)] * parts for r in range(2)]
    arrived_far = [partner(p, "tensor", 1) for p in arrived[parts > 1 :]]
    if parts > 1:
        arrived_far = [far_first] + arrived_far

    near = expert(me_ds, arrived, g_sides[0], g_specs[0], weights, router, F32)
    near, arrived_far = tie(near, arrived_far)
    far = expert(me_ds, arrived_far, g_sides[1], g_specs[1], weights, router, BF16)
    grad_far = partner(far[0][0], "tensor", 1)
    near, far, att_all = tie(near, far, att_all)
    late = expert_late(scalar(me_s), [near, far], weights)
    grad_far, late = tie(grad_far, late)
    (res_own, res_other, router_part), (near_in, near_out, far_own, others) = late
    res_far = partner(res_other, "tensor", 1)
    others = partner(others, "shard", 1)
    far_part = [(far_own[n] + others[2 + n].astype(F32)).astype(BF16) for n in range(2)]
    back = add_parts(near[0][0], grad_far, parts)
    if parts == 1:
        back = [back[0][k * quarter : (k + 1) * quarter] for k in range(n_d)]
    grad_two = swap_chunks(list(back), "dp")
    if parts == 1:
        grad_two = [jnp.concatenate(grad_two, axis=0)]

    grad_two, far_part = tie(grad_two, far_part)
    far_sum = [partner(v, "tensor", 2) for v in far_part]

    grad_mixed, gain_two_part, grad_att = second_norm_bwd(
        scalar(me_t), grad_two, g_own, g_specs[0], unit_two, inv_two, gain_two, out_all
    )
    grad_att_slots = swap_chunks(list(grad_att), "tensor")
    grad_mixed_ag, res_far, far_sum[0], *grad_att_slots = tie(grad_mixed, res_far, far_sum[0], *grad_att_slots)
    mixed_slots = lax.all_gather(grad_mixed_ag, "tensor", axis=0, tiled=True)
    res = list(add_parts(res_own, res_far, parts))
    if parts == 1:
        res = [res[0][k * quarter : (k + 1) * quarter] for k in range(n_d)]
    res = swap_chunks(res, "dp")

    grad_q, grad_kt, grad_vt, drel = attend_bwd(
        projected, rel, doc_row, lse, place_row, drop_att, grad_att_slots, heads
    )
    grad_q, grad_kt, grad_vt, drel, res, far_sum[1] = tie(grad_q, grad_kt, grad_vt, drel, res, far_sum[1])
    res_slots = lax.all_gather(jnp.concatenate(res, axis=0), "tensor", axis=0, tiled=True)
    grad_proj, gain_one_part, grad_one, sends = first_norm_bwd(
        order, grad_q, grad_kt, grad_vt, qkv_full, tokens, inv_one
    )
    sends, grad_proj = tie(sends, grad_proj)
    got = [partner(v, "tensor", k + 1) for k, v in enumerate(sends)]

    grad_table = jnp.dot(drel[:heads], onehot.astype(F32).T, precision=HIGH)
    small = jnp.concatenate([gain_one_part, gain_two_part, router_part], axis=0)
    n_small = 2 + n_e
    fill = -(half + own + n_small + 1) % (16 * n_d)
    table_row = grad_table.reshape(heads, 2, n_b // 2).transpose(1, 0, 2).reshape(1, 2, heads * n_b // 2)
    table_row = jnp.pad(table_row, ((0, fill), (0, 0), (0, half - heads * n_b // 2))).reshape(fill + 1, width)
    small = jnp.concatenate([small, table_row], axis=0)
    mixed_tok, total, theirs = weight_pack(
        scalar(me_s), place_abs, cotangent, attended, normed_one, grad_proj, small, [mixed_slots]
    )
    got, total, theirs, mixed_tok, far_sum = tie(got, total, theirs, mixed_tok, far_sum)
    theirs = partner(theirs, "shard", 1)
    delta = token_delta(order, tokens, inv_one, gain_one, grad_one, got)
    theirs, delta = tie(theirs, delta)
    delta_pieces = gather_pieces(delta, "tensor")
    total, sends = pair_sum(order_d, total, theirs)
    for k, piece in enumerate(sends):
        total = total + partner(piece, "dp", k + 1).astype(F32)
    grad_inw, grad_outw = grad_sum(near_in, near_out, others, far_sum)
    grad_tokens = place_chunks(order, mixed_tok, delta_pieces)
    pieces = gather_pieces(total.astype(BF16), "dp")
    pieces, grad_tokens = tie(pieces, grad_tokens)
    grad_qkv, grad_out, rest = weight_unpack(order_d, pieces, half, own)
    small = total_over(rest[:n_small], "tensor")
    grad_table = rest[n_small, : heads * n_b // 2].reshape(heads, n_b // 2)

    output = layer_output(place_abs, tokens, att_all, out_all, res_slots)
    return (
        output,
        grad_tokens,
        small[0],
        small[1],
        grad_qkv.reshape(half, 3, own),
        grad_out,
        grad_table,
        small[2:].T,
        grad_inw[None],
        grad_outw[None],
    )


def solution(mesh):
    placed = (
        P(("dp", "shard"), None),
        P(("dp", "shard"), None),
        P(),
        P(("dp", "shard")),
        P(("dp", "shard")),
        P(("dp", "shard")),
        P(("dp", "shard"), None),
        P("shard"),
        P("shard"),
        P("shard", None, "tensor"),
        P("tensor", "shard"),
        P("tensor", "shard"),
        P("shard", None),
        P("dp", "shard", "tensor"),
        P("dp", "tensor", "shard"),
    )
    return jax.shard_map(
        body,
        mesh=mesh,
        in_specs=placed,
        out_specs=(
            P(("dp", "shard"), None),
            P(("dp", "shard"), None),
            P("shard"),
            P("shard"),
            P("shard", None, "tensor"),
            P("tensor", "shard"),
            P("tensor", "shard"),
            P("shard", None),
            P("dp", "shard", "tensor"),
            P("dp", "tensor", "shard"),
        ),
        check_vma=False,
    )
```

```python
import functools

import jax
import jax.numpy as jnp
from jax import lax
from jax.experimental import pallas as pl
from jax.experimental.pallas import tpu as pltpu
from jax.sharding import PartitionSpec as P

DH = 64
EPS = 1e-06
NEG = -1e30
VMEM_MIB = 52
HIGH = lax.Precision.HIGHEST
BQ = 512
BQ_BACK = 1024
TB = 128
F32 = jnp.float32
BF16 = jnp.bfloat16


def contract(left, right, left_dim, right_dim):
    return lax.dot_general(
        left, right, (((left_dim,), (right_dim,)), ((), ())), preferred_element_type=F32
    )


def partner(value, axis, step):
    size = lax.axis_size(axis)
    return lax.ppermute(value, axis, [(i, i ^ step) for i in range(size)])


def swap_chunks(chunks, axis):
    return [chunks[0]] + [partner(c, axis, k) for k, c in enumerate(chunks) if k]


def gather_pieces(value, axis):
    return swap_chunks([value] * lax.axis_size(axis), axis)


def pick_rows(place_row, start, rows):
    at = lax.broadcasted_iota(jnp.int32, (rows, place_row.shape[1]), 0) + start
    return (at == place_row).astype(F32).astype(BF16)


def as_col(row):
    wide = jnp.broadcast_to(row.astype(F32), (128, row.shape[1]))
    return wide.T[:, :1].astype(jnp.int32)


def pick_cols(place_col, start, rows):
    at = lax.broadcasted_iota(jnp.int32, (place_col.shape[0], rows), 1) + start
    return (at == place_col).astype(F32).astype(BF16)


def shear_table(rel_ref, table_ref, heads, span):
    for h in range(heads):
        row = jnp.broadcast_to(rel_ref[h : h + 1, :], (TB, span))
        table_ref[h] = pltpu.roll(row, span - (TB - 1), 1, stride=1, stride_axis=0)


def table_starts(step, rows, length):
    last = length // TB - 1
    return [pl.multiple_of((last - step * (rows // TB) - a) * TB, TB) for a in range(rows // TB)]


def bias_of(table_ref, h, starts, length):
    return jnp.concatenate([table_ref[h, :, pl.ds(at, length)] for at in starts], axis=0)


def attend_fwd_kernel(
    qkv_ref, rel_ref, doc_row_ref, place_ref, out_ref, lse_ref, *rest, heads
):
    slot_refs, table_ref = rest[:-1], rest[-1]
    length = qkv_ref.shape[0]
    blocks = length // BQ
    width = heads * DH
    step = pl.program_id(0)

    @pl.when(step == 0)
    def _():
        shear_table(rel_ref, table_ref, heads, table_ref.shape[2])

    row0 = pl.multiple_of(step * BQ, BQ)
    starts = table_starts(step, BQ, length)
    same = as_col(doc_row_ref[:, pl.ds(row0, BQ)]) == doc_row_ref[...]
    outs, stats = [], []
    for h in range(heads):
        q = qkv_ref[pl.ds(row0, BQ), h * DH : (h + 1) * DH] * 0.125
        k = qkv_ref[:, width + h * DH : width + (h + 1) * DH]
        v = qkv_ref[:, 2 * width + h * DH : 2 * width + (h + 1) * DH]
        s = contract(q, k, 1, 1) + bias_of(table_ref, h, starts, length)
        s = jnp.where(same, s, NEG)
        top = jnp.max(s, axis=1, keepdims=True)
        e = jnp.exp(s - top)
        total = jnp.sum(e, axis=1, keepdims=True)
        o = contract(e.astype(BF16), v, 1, 0)
        outs.append(o * (1.0 / total))
        stats.append(top + jnp.log(total))
    out_ref[pl.ds(row0, BQ), :] = jnp.concatenate(outs, axis=1).astype(BF16)
    lse_ref[...] = jnp.concatenate(stats, axis=1)

    @pl.when(step == blocks - 1)
    def _():
        place = place_ref[...]
        for n, ref in enumerate(slot_refs):
            ref[...] = contract(pick_rows(place, n * ref.shape[0], ref.shape[0]), out_ref[...], 1, 0).astype(BF16)


def attend_bwd_kernel(
    qkv_ref, rel_ref, doc_row_ref, lse_ref, place_ref, drop_ref, *rest, heads,
):
    slot_refs = rest[:-9]
    dq_ref, dk_ref, dv_ref, drel_ref, table_ref, acc_ref, dk_acc, dv_acc, grad_ref = rest[-9:]
    length = qkv_ref.shape[0]
    blocks = length // BQ_BACK
    width = heads * DH
    span = table_ref.shape[2]
    step = pl.program_id(0)

    @pl.when(step == 0)
    def _():
        shear_table(rel_ref, table_ref, heads, span)
        acc_ref[...] = jnp.zeros(acc_ref.shape, F32)
        dk_acc[...] = jnp.zeros(dk_acc.shape, F32)
        dv_acc[...] = jnp.zeros(dv_acc.shape, F32)
        grad = drop_ref[...].astype(F32)
        place = as_col(place_ref[...])
        for n, ref in enumerate(slot_refs):
            grad = grad + contract(pick_cols(place, n * ref.shape[0], ref.shape[0]), ref[...], 1, 0)
        grad_ref[...] = grad.astype(BF16)

    row0 = pl.multiple_of(step * BQ_BACK, BQ_BACK)
    starts = table_starts(step, BQ_BACK, length)
    same = as_col(doc_row_ref[:, pl.ds(row0, BQ_BACK)]) == doc_row_ref[...]
    dqs = []
    for h in range(heads):
        q = qkv_ref[pl.ds(row0, BQ_BACK), h * DH : (h + 1) * DH] * 0.125
        k = qkv_ref[:, width + h * DH : width + (h + 1) * DH]
        v = qkv_ref[:, 2 * width + h * DH : 2 * width + (h + 1) * DH]
        g = grad_ref[pl.ds(row0, BQ_BACK), h * DH : (h + 1) * DH]
        s = contract(q, k, 1, 1) + bias_of(table_ref, h, starts, length)
        s = jnp.where(same, s, NEG)
        p = jnp.exp(s - lse_ref[:, h : h + 1])
        dp = contract(g, v, 1, 1)
        inner = jnp.sum(p * dp, axis=1, keepdims=True)
        ds = p * (dp - inner)
        dsb = ds.astype(BF16)
        for a, at in enumerate(starts):
            acc_ref[h, :, pl.ds(at, length)] += ds[a * TB : (a + 1) * TB]
        dqs.append(0.125 * contract(dsb, k, 1, 0))
        dk_acc[h * DH : (h + 1) * DH, :] += contract(q, dsb, 0, 0)
        dv_acc[h * DH : (h + 1) * DH, :] += contract(g, p.astype(BF16), 0, 0)
    dq_ref[...] = jnp.concatenate(dqs, axis=1).astype(BF16)

    @pl.when(step == blocks - 1)
    def _():
        dk_ref[...] = dk_acc[...].astype(BF16)
        dv_ref[...] = dv_acc[...].astype(BF16)
        for h in range(heads):
            rows = acc_ref[h]
            half = TB // 2
            while half >= 1:
                rows = pltpu.roll(rows[:half], half, 1) + rows[half:]
                half //= 2
            drel_ref[h : h + 1, :] = rows


def whole(shape):
    return pl.BlockSpec(shape, lambda *i: (0,) * len(shape))


def wholes(arrays):
    return [whole(a.shape) for a in arrays]


def params():
    return pltpu.CompilerParams(vmem_limit_bytes=VMEM_MIB * 1024 * 1024)


def struct(shape, dtype):
    return jax.ShapeDtypeStruct(shape, dtype)


def attend_specs(length, heads, span):
    return [
        whole((length, 3 * heads * DH)),
        whole((8, span)),
        whole((1, length)),
    ]


def attend_fwd(projected, rel, doc_row, place_row, heads, parts, part_rows):
    length = projected.shape[0]
    span = rel.shape[1]
    width = heads * DH
    return pl.pallas_call(
        functools.partial(attend_fwd_kernel, heads=heads),
        grid=(length // BQ,),
        in_specs=attend_specs(length, heads, span) + [whole((1, length))],
        out_specs=[whole((length, width)), pl.BlockSpec((BQ, heads), lambda i: (i, 0))]
        + [whole((part_rows, width))] * parts,
        out_shape=[struct((length, width), BF16), struct((length, heads), F32)]
        + [struct((part_rows, width), BF16)] * parts,
        scratch_shapes=[pltpu.VMEM((heads, TB, span), F32)],
        compiler_params=params(),
        name="attend_fwd",
    )(projected, rel, doc_row, place_row)


def attend_bwd(projected, rel, doc_row, lse, place_row, drop, grads, heads):
    length = projected.shape[0]
    span = rel.shape[1]
    width = heads * DH
    return pl.pallas_call(
        functools.partial(attend_bwd_kernel, heads=heads),
        grid=(length // BQ_BACK,),
        in_specs=attend_specs(length, heads, span)
        + [pl.BlockSpec((BQ_BACK, heads), lambda i: (i, 0)), whole((1, length)), whole((length, width))]
        + wholes(grads),
        out_specs=[
            pl.BlockSpec((BQ_BACK, width), lambda i: (i, 0)),
            whole((width, length)),
            whole((width, length)),
            whole((8, span)),
        ],
        out_shape=[
            struct((length, width), BF16),
            struct((width, length), BF16),
            struct((width, length), BF16),
            struct((8, span), F32),
        ],
        scratch_shapes=[
            pltpu.VMEM((heads, TB, span), F32),
            pltpu.VMEM((heads, TB, span), F32),
            pltpu.VMEM((width, length), F32),
            pltpu.VMEM((width, length), F32),
            pltpu.VMEM((length, width), BF16),
        ],
        compiler_params=params(),
        name="attend_bwd",
    )(projected, rel, doc_row, lse, place_row, drop, *grads)


def store_parts(refs, value):
    if len(refs) == 1:
        refs[0][...] = value
        return
    rows = refs[0].shape[0]
    for n, ref in enumerate(refs):
        ref[...] = value[n * rows : (n + 1) * rows]


def load_parts(refs):
    if len(refs) == 1:
        return refs[0][...]
    return jnp.concatenate([ref[...] for ref in refs], axis=0)


def slot_rows_kernel(me_ref, routes_ref, kept_ref, slots_ref, cot_ref, tok_ref, rel_ref, abs_ref, x_ref, *g_refs, quarter, n_t, rows_q):
    slots = slots_ref[...]
    part = jnp.zeros(slots.shape, jnp.int32)
    for k in range(1, n_t):
        part = part + (slots >= k * quarter).astype(jnp.int32)
    spot = slots - part * quarter
    taken = kept_ref[...] > 0
    rel_t = part ^ me_ref[0]
    rel_d = routes_ref[...] ^ me_ref[1]
    rel = jnp.where(taken, rel_t * rows_q + rel_d * quarter + spot, -1)
    rel_ref[...] = rel
    abs_ref[...] = jnp.where(taken, part * rows_q + rel_d * quarter + spot, -1)
    place_g = jnp.where(taken & (rel_t < 2), (rel_d * 2 + rel_t) * quarter + spot, -1)
    rows = g_refs[0].shape[0]
    for n, ref in enumerate(g_refs):
        ref[...] = contract(pick_rows(place_g, n * rows, rows), cot_ref[...], 1, 0).astype(BF16)
    x_ref[...] = contract(pick_rows(rel, 0, x_ref.shape[0]), tok_ref[...], 1, 0).astype(BF16)


def slot_rows(me, routes, kept, slots, cotangent, tokens, quarter, n_t, rows_q, parts, part_rows):
    length, width = tokens.shape
    shapes = [struct((1, length), jnp.int32)] * 2 + [struct((rows_q, width), BF16)]
    shapes += [struct((part_rows, width), BF16)] * parts
    operands = [routes.reshape(1, -1), kept.reshape(1, -1), slots.reshape(1, -1), cotangent, tokens]
    out = pl.pallas_call(
        functools.partial(slot_rows_kernel, quarter=quarter, n_t=n_t, rows_q=rows_q),
        grid=(1,),
        in_specs=[pl.BlockSpec(memory_space=pltpu.SMEM)] + wholes(operands),
        out_specs=[whole(v.shape) for v in shapes],
        out_shape=shapes,
        compiler_params=params(),
        name="slot_rows",
    )(me, *operands)
    return out[0], out[1], out[2], out[3:]


def first_norm_kernel(me_ref, tok_ref, gain_ref, w_ref, w_far_ref, normed_ref, inv_ref, proj_ref, full_ref):
    half = w_ref.shape[0]
    mine = pl.multiple_of(me_ref[0] * half, half)
    theirs = pl.multiple_of((1 - me_ref[0]) * half, half)
    x = tok_ref[...].astype(F32)
    inv = lax.rsqrt(jnp.mean(x * x, axis=1, keepdims=True) + EPS)
    inv_ref[...] = inv
    normed_ref[...] = (x * inv * gain_ref[...]).astype(BF16)
    proj_ref[...] = (
        contract(normed_ref[:, pl.ds(mine, half)], w_ref[...], 1, 0)
        + contract(normed_ref[:, pl.ds(theirs, half)], w_far_ref[...], 1, 0)
    ).astype(BF16)

    @pl.when(pl.program_id(0) == 0)
    def _():
        full_ref[pl.ds(mine, half), :] = w_ref[...]
        full_ref[pl.ds(theirs, half), :] = w_far_ref[...]


def first_norm(me_s, tokens, gain, w_own, w_far):
    length, width = tokens.shape
    out_width = w_own.shape[1]
    rows = length // 4
    block = lambda n: pl.BlockSpec((rows, n), lambda i: (i, 0))
    return pl.pallas_call(
        first_norm_kernel,
        grid=(4,),
        in_specs=[pl.BlockSpec(memory_space=pltpu.SMEM), block(width)] + wholes([gain, w_own, w_far]),
        out_specs=[block(width), block(1), block(out_width), whole((width, out_width))],
        out_shape=[
            struct((length, width), BF16),
            struct((length, 1), F32),
            struct((length, out_width), BF16),
            struct((width, out_width), BF16),
        ],
        compiler_params=params(),
        name="first_norm",
    )(me_s, tokens, gain, w_own, w_far)


def middle_kernel(me_ref, *refs, n_t, parts):
    att, (w_ref, x_ref, gain_ref) = refs[:n_t], refs[n_t : n_t + 3]
    unit_ref, inv_ref = refs[n_t + 3 : n_t + 5]
    outs = refs[n_t + 5 :]
    sides = []
    for half in range(2):
        total = contract(att[0][...], w_ref[me_ref[0], half], 1, 0)
        for k in range(1, n_t):
            total = total + contract(att[k][...], w_ref[me_ref[0] ^ k, half], 1, 0)
        sides.append(total)
    resid = x_ref[...].astype(F32) + jnp.concatenate(sides, axis=1)
    inv = lax.rsqrt(jnp.mean(resid * resid, axis=1, keepdims=True) + EPS)
    unit = resid * inv
    unit_ref[...] = unit
    inv_ref[...] = inv
    store_parts(outs, (unit * gain_ref[...]).astype(BF16))


def middle(me_t, att, w_rel, x_rows, gain, parts):
    rows, width = x_rows.shape
    operands = (*att, w_rel, x_rows, gain)
    shapes = [struct((rows, width), F32), struct((rows, 1), F32)]
    shapes += [struct((rows // parts, width), BF16)] * parts
    out = pl.pallas_call(
        functools.partial(middle_kernel, n_t=len(att), parts=parts),
        grid=(1,),
        in_specs=[pl.BlockSpec(memory_space=pltpu.SMEM)] + wholes(operands),
        out_specs=[whole(v.shape) for v in shapes],
        out_shape=shapes,
        compiler_params=params(),
        name="second_norm",
    )(me_t, *operands)
    return out[0], out[1], out[2:]


def expert_kernel(me_ref, *refs, parts, chunks, n_e):
    refs, (win_buf, wout_buf, sems) = refs[:-3], refs[-3:]
    rows_refs, g_refs = refs[:parts], refs[parts : 2 * parts]
    pieces, router_ref = refs[2 * parts : 2 * parts + 4], refs[2 * parts + 4]
    outs = refs[2 * parts + 5 :]
    half = pieces[0].shape[1]
    mine = pl.multiple_of(me_ref[1] * half, half)
    theirs = pl.multiple_of((1 - me_ref[1]) * half, half)
    copies = []
    for c in range(chunks):
        moves = []
        for piece, start in ((pieces[2 * c], mine), (pieces[2 * c + 1], theirs)):
            moves.append((piece.at[0], win_buf.at[c, pl.ds(start, half)]))
        for piece, side in ((pieces[2 * c], me_ref[1]), (pieces[2 * c + 1], 1 - me_ref[1])):
            for n in range(2):
                part = pl.ds(n * half, half)
                moves.append((piece.at[1, :, part], wout_buf.at[c, side, part]))
        copies.append([pltpu.make_async_copy(a, b, sems.at[6 * c + i]) for i, (a, b) in enumerate(moves)])
        for copy in copies[-1]:
            copy.start()
    grad_ref, rows_ref, slot_ref, gate_ref, logit_ref = outs[:5]
    hid_refs, gpre_refs = outs[5 : 5 + chunks], outs[5 + chunks :]
    rows = load_parts(rows_refs)
    g = load_parts(g_refs)
    router = router_ref[...]
    logits = contract(rows, router, 1, 1)
    exp_logits = jnp.exp(logits - jnp.max(logits, axis=1, keepdims=True))
    probs = exp_logits / jnp.sum(exp_logits, axis=1, keepdims=True)
    chosen = (lax.broadcasted_iota(jnp.int32, logits.shape, 1) == me_ref[0]).astype(F32)
    gate = jnp.sum(probs * chosen, axis=1, keepdims=True)
    grad_gate = jnp.zeros(gate.shape, F32)
    total = None
    for c in range(chunks):
        for copy in copies[c][:2]:
            copy.wait()
        pre = contract(rows, win_buf[c], 1, 0)
        value, slope = gelu_pair(pre)
        hidden = value.astype(BF16)
        hid_refs[c][...] = hidden
        for copy in copies[c][2:]:
            copy.wait()
        raw = contract(g[:, :half], wout_buf[c, 0], 1, 1) + contract(g[:, half:], wout_buf[c, 1], 1, 1)
        grad_gate = grad_gate + jnp.sum(hidden.astype(F32) * raw, axis=1, keepdims=True)
        grad_pre = (gate * raw * slope).astype(BF16)
        gpre_refs[c][...] = grad_pre
        part = contract(grad_pre, win_buf[c], 1, 1)
        total = part if total is None else total + part
    grad_logits = (grad_gate * probs * (chosen - gate)).astype(BF16)
    total = total + contract(grad_logits, router, 1, 0)
    grad_ref[...] = total.astype(grad_ref.dtype)
    rows_ref[...] = rows
    slot_ref[...] = (gate * g.astype(F32)).astype(BF16)
    gate_ref[...] = gate
    logit_ref[...] = grad_logits


def expert(me, rows, g, g_specs, weights, router, grad_dtype):
    parts, chunks = len(rows), 2
    total = sum(r.shape[0] for r in rows)
    width = rows[0].shape[1]
    hidden = weights[0].shape[2]
    n_e = router.shape[0]
    out = pl.pallas_call(
        functools.partial(expert_kernel, parts=parts, chunks=chunks, n_e=n_e),
        grid=(1,),
        in_specs=[pl.BlockSpec(memory_space=pltpu.SMEM)]
        + wholes(rows) + g_specs + [pl.BlockSpec(memory_space=pltpu.HBM)] * 4 + [whole(router.shape)],
        out_specs=[
            whole((total, width)), whole((total, width)), whole((total, width)), whole((total, 1)), whole((total, n_e))
        ] + [whole((total, hidden))] * (2 * chunks),
        out_shape=[
            struct((total, width), grad_dtype),
            struct((total, width), BF16),
            struct((total, width), BF16),
            struct((total, 1), F32),
            struct((total, n_e), BF16),
        ]
        + [struct((total, hidden), BF16)] * (2 * chunks),
        scratch_shapes=[
            pltpu.VMEM((chunks, width, hidden), BF16),
            pltpu.VMEM((chunks, 2, hidden, width // 2), BF16),
            pltpu.SemaphoreType.DMA((12,)),
        ],
        compiler_params=params(),
        name="expert",
    )(me, *rows, *g, *weights, router)
    return out[:5], out[5 : 5 + chunks], out[5 + chunks :]


def expert_late_kernel(me_ref, *refs, groups, chunks):
    side = lambda n: refs[n * groups : (n + 1) * groups]
    rows, slot, gate, logit = (side(n) for n in range(4))
    at = 4 * groups
    hid = [refs[at + c * groups : at + (c + 1) * groups] for c in range(chunks)]
    at += chunks * groups
    gpre = [refs[at + c * groups : at + (c + 1) * groups] for c in range(chunks)]
    at += chunks * groups
    out_own, out_other, far_out_own, far_out_other = refs[at : at + 4]
    res_own, res_other, router_ref, near_in, near_out, far_own, others = refs[at + 4 :]
    half = rows[0].shape[1] // 2
    mine = pl.multiple_of(me_ref[0] * half, half)
    theirs = pl.multiple_of((1 - me_ref[0]) * half, half)
    for r, ref in enumerate((res_own, res_other)):
        for start, sides in ((mine, (out_own, far_out_own)), (theirs, (out_other, far_out_other))):
            total = jnp.zeros((ref.shape[0], half), F32)
            for c, side in enumerate(sides):
                for n in range(2):
                    part = slice(n * half, (n + 1) * half)
                    total = total + contract(hid[c][r][:, part], side[0, :, part], 1, 0)
            ref[:, pl.ds(start, half)] = (gate[r][...] * total).astype(ref.dtype)
    router_ref[...] = contract(logit[0][...], rows[0][...], 0, 0) + contract(logit[1][...], rows[1][...], 0, 0)
    both = lambda refs, start: jnp.concatenate([ref[:, pl.ds(start, half)] for ref in refs], axis=0)
    rows_mine, rows_theirs = both(rows, mine).T, both(rows, theirs).T
    slot_mine, slot_theirs = both(slot, mine), both(slot, theirs)
    for c in range(chunks):
        grads = jnp.concatenate([ref[...] for ref in gpre[c]], axis=0)
        units = jnp.concatenate([ref[...] for ref in hid[c]], axis=0).T
        others[2 * c] = contract(rows_theirs, grads, 1, 0).astype(BF16)
        out_t = contract(units, slot_theirs, 1, 0).astype(BF16)
        others[2 * c + 1, :, :half] = out_t[:half]
        others[2 * c + 1, :, half:] = out_t[half:]
        in_m = contract(rows_mine, grads, 1, 0)
        out_m = contract(units, slot_mine, 1, 0)
        if c == 0:
            near_in[...] = in_m
            near_out[...] = out_m
        else:
            far_own[0] = in_m
            far_own[1, :, :half] = out_m[:half]
            far_own[1, :, half:] = out_m[half:]


def grad_sum_kernel(near_in, near_out, other_ref, far_in, far_out, in_ref, out_ref):
    half = near_in.shape[0]
    in_ref[...] = near_in[...] + other_ref[0].astype(F32) + far_in[...].astype(F32)
    side = other_ref[1].astype(F32) + far_out[...].astype(F32)
    out_ref[:half] = near_out[:half] + side[:, :half]
    out_ref[half:] = near_out[half:] + side[:, half:]


def grad_sum(near_in, near_out, others, far):
    return pl.pallas_call(
        grad_sum_kernel,
        grid=(1,),
        in_specs=wholes([near_in, near_out]) + [whole((2,) + others.shape[1:])] + wholes(far),
        out_specs=wholes([near_in, near_out]),
        out_shape=[struct(near_in.shape, F32), struct(near_out.shape, F32)],
        compiler_params=params(),
        name="grad_sum",
    )(near_in, near_out, others, *far)


def layer_output_kernel(place_ref, tok_ref, att_ref, w_ref, slots_ref, out_ref, *, n_t):
    sides = []
    for half in range(2):
        total = contract(att_ref[0], w_ref[0, half], 1, 0)
        for k in range(1, n_t):
            total = total + contract(att_ref[k], w_ref[k, half], 1, 0)
        sides.append(total)
    resid = tok_ref[...].astype(F32) + jnp.concatenate(sides, axis=1)
    found = contract(pick_cols(as_col(place_ref[...]), 0, slots_ref.shape[0]), slots_ref[...], 1, 0)
    out_ref[...] = (resid + found).astype(BF16)


def layer_output(place_row, tokens, att_all, w_all, res_slots):
    length, width = tokens.shape
    n_t, _, own = att_all.shape
    rows = length // 4
    block = lambda n: pl.BlockSpec((rows, n), lambda i: (i, 0))
    return pl.pallas_call(
        functools.partial(layer_output_kernel, n_t=n_t),
        grid=(4,),
        in_specs=[
            pl.BlockSpec((1, rows), lambda i: (0, i)), block(width), pl.BlockSpec((n_t, rows, own), lambda i: (0, i, 0)),
            whole(w_all.shape), whole(res_slots.shape),
        ],
        out_specs=block(width),
        out_shape=struct((length, width), BF16),
        compiler_params=params(),
        name="layer_output",
    )(place_row, tokens, att_all, w_all, res_slots)


def expert_late(me_s, groups, w_out):
    chunks = 2
    operands = []
    for n in (1, 2, 3, 4):
        operands += [grp[0][n] for grp in groups]
    for kind in (1, 2):
        for c in range(chunks):
            operands += [grp[kind][c] for grp in groups]
    specs = wholes(operands) + [pl.BlockSpec((1,) + w.shape[1:], lambda i: (1, 0, 0)) for w in w_out]
    operands += list(w_out)
    rows, width = groups[0][0][1].shape
    hidden = groups[0][1][0].shape[1]
    n_e = groups[0][0][4].shape[1]
    half = width // 2
    shapes = [struct((rows, width), F32), struct((rows, width), BF16), struct((n_e, width), F32)]
    shapes += [
        struct((half, hidden), F32), struct((hidden, half), F32),
        struct((2, half, hidden), F32), struct((4, half, hidden), BF16),
    ]
    out = pl.pallas_call(
        functools.partial(expert_late_kernel, groups=len(groups), chunks=chunks),
        grid=(1,),
        in_specs=[pl.BlockSpec(memory_space=pltpu.SMEM)] + specs,
        out_specs=[whole(s.shape) for s in shapes],
        out_shape=shapes,
        compiler_params=params(),
        name="expert_late",
    )(me_s, *operands)
    return out[:3], out[3:]


def add_parts_kernel(own_ref, other_ref, *outs):
    store_parts(outs, (own_ref[...] + other_ref[...].astype(F32)).astype(BF16))


def add_parts(own, other, parts):
    rows, width = own.shape
    return pl.pallas_call(
        add_parts_kernel,
        out_shape=[struct((rows // parts, width), BF16)] * parts,
        compiler_params=params(),
        name="add_parts",
    )(own, other)


def second_norm_bwd_kernel(me_ref, *refs, parts, n_t):
    grads, g_refs = refs[:parts], refs[parts : 2 * parts]
    unit_ref, inv_ref, gain_ref, w_ref, mixed_ref, gain_out_ref = refs[2 * parts : 2 * parts + 6]
    outs = refs[2 * parts + 6 :]
    grad = load_parts(grads).astype(F32)
    unit = unit_ref[...]
    gain_out_ref[...] = jnp.sum(grad * unit, axis=0, keepdims=True)
    scaled = grad * gain_ref[...]
    resid = load_parts(g_refs).astype(F32) + inv_ref[...] * (
        scaled - unit * jnp.mean(scaled * unit, axis=1, keepdims=True)
    )
    mixed = resid.astype(BF16)
    mixed_ref[...] = mixed
    half = mixed.shape[1] // 2
    for k, ref in enumerate(outs):
        at = me_ref[0] ^ k
        ref[...] = (
            contract(mixed[:, :half], w_ref[at, 0], 1, 1) + contract(mixed[:, half:], w_ref[at, 1], 1, 1)
        ).astype(BF16)


def second_norm_bwd(me_t, grads, g, g_specs, unit, inv, gain, w_rel):
    rows, width = unit.shape
    n_t, own = w_rel.shape[0], w_rel.shape[2]
    shapes = [struct((rows, width), BF16), struct((1, width), F32)] + [struct((rows, own), BF16)] * n_t
    out = pl.pallas_call(
        functools.partial(second_norm_bwd_kernel, parts=len(grads), n_t=n_t),
        grid=(1,),
        in_specs=[pl.BlockSpec(memory_space=pltpu.SMEM)]
        + wholes(grads) + g_specs + wholes([unit, inv, gain, w_rel]),
        out_specs=[whole(s.shape) for s in shapes],
        out_shape=shapes,
        compiler_params=params(),
        name="second_norm_bwd",
    )(me_t, *grads, *g, unit, inv, gain, w_rel)
    return out[0], out[1], out[2:]


def first_norm_bwd_kernel(order_ref, dq_ref, dk_ref, dv_ref, w_ref, tok_ref, inv_ref, proj_ref, gain_ref, own_ref, *sends):
    step = pl.program_id(0)
    flip = lambda ref: ref[...].astype(F32).T.astype(BF16)
    grads = jnp.concatenate([dq_ref[...], flip(dk_ref), flip(dv_ref)], axis=1)
    proj_ref[...] = grads
    part = contract(grads, w_ref[...], 1, 1)

    @pl.when(step == 0)
    def _():
        gain_ref[...] = jnp.zeros(gain_ref.shape, F32)
        own_ref[...] = part

    gain_ref[...] += jnp.sum(part * (tok_ref[...].astype(F32) * inv_ref[...]), axis=0, keepdims=True)
    for k, ref in enumerate(sends):

        @pl.when(step == k + 1)
        def _():
            ref[...] = part.astype(BF16)


def first_norm_bwd(order, grad_q, grad_kt, grad_vt, qkv_full, tokens, inv):
    count = order.shape[0]
    length, width = tokens.shape
    own = grad_q.shape[1]
    rows = length // count
    block = lambda n: pl.BlockSpec((rows, n), lambda i, order: (order[i], 0))
    side = pl.BlockSpec((own, rows), lambda i, order: (0, order[i]))
    out = pl.pallas_call(
        first_norm_bwd_kernel,
        grid_spec=pltpu.PrefetchScalarGridSpec(
            num_scalar_prefetch=1,
            grid=(count,),
            in_specs=[block(own), side, side, whole(qkv_full.shape), block(width), block(1)],
            out_specs=[block(3 * own), whole((1, width))] + [whole((rows, width))] * count,
        ),
        out_shape=[struct((length, 3 * own), BF16), struct((1, width), F32), struct((rows, width), F32)]
        + [struct((rows, width), BF16)] * (count - 1),
        compiler_params=params(),
        name="first_norm_bwd",
    )(order, grad_q, grad_kt, grad_vt, qkv_full, tokens, inv)
    return out[0], out[1], out[2], out[3:]


def token_delta_kernel(order_ref, tok_ref, inv_ref, gain_ref, own_ref, *refs):
    got, out_ref = refs[:-1], refs[-1]
    grad = own_ref[...]
    for ref in got:
        grad = grad + ref[...].astype(F32)
    inv = inv_ref[...]
    unit = tok_ref[...].astype(F32) * inv
    scaled = grad * gain_ref[...]
    out_ref[...] = (inv * (scaled - unit * jnp.mean(scaled * unit, axis=1, keepdims=True))).astype(BF16)


def token_delta(order, tokens, inv, gain, own, got):
    rows, width = own.shape
    block = lambda n: pl.BlockSpec((rows, n), lambda i, order: (order[0], 0))
    return pl.pallas_call(
        token_delta_kernel,
        grid_spec=pltpu.PrefetchScalarGridSpec(
            num_scalar_prefetch=1,
            grid=(1,),
            in_specs=[block(width), block(1)] + wholes([gain, own, *got]),
            out_specs=whole((rows, width)),
        ),
        out_shape=struct((rows, width), BF16),
        compiler_params=params(),
        name="token_delta",
    )(order, tokens, inv, gain, own, *got)


def weight_pack_kernel(me_ref, place_ref, cot_ref, att_ref, normed_ref, proj_ref, small_ref, *refs, half):
    slot_refs, (mixed_ref, own_ref, other_ref, acc_ref) = refs[:-4], refs[-4:]
    rows = att_ref.shape[1]
    mine = pl.multiple_of(me_ref[0] * half, half)
    theirs = pl.multiple_of((1 - me_ref[0]) * half, half)
    step = pl.program_id(0)
    place = as_col(place_ref[...])
    found = jnp.zeros(cot_ref.shape, F32)
    for n, ref in enumerate(slot_refs):
        found = found + contract(pick_cols(place, n * ref.shape[0], ref.shape[0]), ref[...], 1, 0)
    mixed_ref[...] = jnp.where(place < 0, cot_ref[...], found.astype(BF16))

    @pl.when(step == 0)
    def _():
        for ref, start in ((own_ref, mine), (acc_ref, theirs)):
            ref[...] = jnp.zeros(ref.shape, F32)
            ref[half + rows :, :half] = small_ref[:, pl.ds(start, half)]

    proj = proj_ref[...]
    att = att_ref[...]
    for ref, start in ((own_ref, mine), (acc_ref, theirs)):
        ref[:half] += contract(normed_ref[:, pl.ds(start, half)], proj, 0, 0)
        ref[half : half + rows, :half] += contract(att, mixed_ref[:, pl.ds(start, half)], 0, 0)

    @pl.when(step == pl.num_programs(0) - 1)
    def _():
        other_ref[...] = acc_ref[...].astype(BF16)


def weight_pack(me_s, place_row, cotangent, attended, normed, proj, small, mixed_slots):
    length, width = normed.shape
    own = attended.shape[1]
    shape = (width // 2 + own + small.shape[0], proj.shape[1])
    rows = length // 4
    block = lambda n: pl.BlockSpec((rows, n), lambda i: (i, 0))
    return pl.pallas_call(
        functools.partial(weight_pack_kernel, half=width // 2),
        grid=(4,),
        in_specs=[
            pl.BlockSpec(memory_space=pltpu.SMEM), pl.BlockSpec((1, rows), lambda i: (0, i)),
            block(width), block(own), block(width), block(proj.shape[1]), whole(small.shape),
        ]
        + wholes(mixed_slots),
        out_specs=[block(width), whole(shape), whole(shape)],
        out_shape=[struct((length, width), BF16), struct(shape, F32), struct(shape, BF16)],
        scratch_shapes=[pltpu.VMEM(shape, F32)],
        compiler_params=params(),
        name="weight_pack",
    )(me_s, place_row, cotangent, attended, normed, proj, small, *mixed_slots)


def pair_sum_kernel(order_ref, own_ref, other_ref, keep_ref, *sends):
    total = own_ref[...] + other_ref[...].astype(F32)
    step = pl.program_id(0)

    @pl.when(step == 0)
    def _():
        keep_ref[...] = total

    for k, ref in enumerate(sends):

        @pl.when(step == k + 1)
        def _():
            ref[...] = total.astype(BF16)


def pair_sum(order, own, other):
    count = order.shape[0]
    rows, width = own.shape[0] // count, own.shape[1]
    block = pl.BlockSpec((rows, width), lambda i, order: (order[i], 0))
    out = pl.pallas_call(
        pair_sum_kernel,
        grid_spec=pltpu.PrefetchScalarGridSpec(
            num_scalar_prefetch=1,
            grid=(count,),
            in_specs=[block, block],
            out_specs=[whole((rows, width))] * count,
        ),
        out_shape=[struct((rows, width), F32)] + [struct((rows, width), BF16)] * (count - 1),
        compiler_params=params(),
        name="pair_sum",
    )(order, own, other)
    return out[0], out[1:]


def place_chunks_kernel(order_ref, base_ref, *refs, count):
    step = pl.program_id(0)
    out_ref = refs[-1]
    for k in range(count):

        @pl.when(step == k)
        def _():
            out_ref[...] = base_ref[...].astype(F32) + refs[k][...].astype(F32)


def place_chunks(order, base, pieces):
    count = len(pieces)
    rows, width = pieces[0].shape
    block = pl.BlockSpec((rows, width), lambda i, order: (order[i], 0))
    return pl.pallas_call(
        functools.partial(place_chunks_kernel, count=count),
        grid_spec=pltpu.PrefetchScalarGridSpec(
            num_scalar_prefetch=1, grid=(count,), in_specs=[block] + wholes(pieces), out_specs=block
        ),
        out_shape=struct((count * rows, width), F32),
        compiler_params=params(),
        name="place_chunks",
    )(order, base, *pieces)


def weight_unpack_kernel(order_ref, *refs):
    pieces, (qkv_ref, out_ref, rest_ref, all_ref) = refs[:-4], refs[-4:]
    rows = pieces[0].shape[0]
    for k, ref in enumerate(pieces):
        all_ref[pl.ds(pl.multiple_of(order_ref[k] * rows, rows), rows), :] = ref[...].astype(F32)
    first, second = qkv_ref.shape[0], qkv_ref.shape[0] + out_ref.shape[0]
    half = out_ref.shape[1]
    qkv_ref[...] = all_ref[:first]
    out_ref[...] = all_ref[first:second, :half]
    rest_ref[...] = all_ref[second:, :half]


def weight_unpack(order, pieces, half, own):
    rows, width = pieces[0].shape
    total = rows * len(pieces)
    shapes = [struct((half, width), F32), struct((own, half), F32), struct((total - half - own, half), F32)]
    return pl.pallas_call(
        weight_unpack_kernel,
        grid_spec=pltpu.PrefetchScalarGridSpec(
            num_scalar_prefetch=1,
            grid=(1,),
            in_specs=wholes(pieces),
            out_specs=[whole(v.shape) for v in shapes],
            scratch_shapes=[pltpu.VMEM((total, width), F32)],
        ),
        out_shape=shapes,
        compiler_params=params(),
        name="weight_unpack",
    )(order, *pieces)


def gelu_pair(pre):
    root = 0.7978845608028654
    cubic = 0.044715
    square = pre * pre
    th = jnp.tanh(root * pre * (1.0 + cubic * square))
    value = 0.5 * pre * (1.0 + th)
    slope = 0.5 * (1.0 + th) + 0.5 * pre * (1.0 - th * th) * root * (1.0 + 3.0 * cubic * square)
    return value, slope


def total_over(value, axis):
    for piece in gather_pieces(value, axis)[1:]:
        value = value + piece
    return value


def tie(*values):
    return lax.optimization_barrier(values)


def body(
    tokens, segment_ids, buckets, routes, kept, slots, cotangent, norm_one, norm_two,
    qkv_weight, out_weight, bias_table, router_weight, expert_in, expert_out,
):
    n_t = lax.axis_size("tensor")
    n_d = lax.axis_size("dp")
    me_t = lax.axis_index("tensor")
    me_d = lax.axis_index("dp")
    me_s = lax.axis_index("shard")
    length, width = tokens.shape
    heads = qkv_weight.shape[2] // DH
    own = heads * DH
    n_e = router_weight.shape[1]
    n_b = 2 * bias_table.shape[1]
    capacity = 5 * length // (4 * n_d)
    quarter = capacity // n_t
    rows_q = n_d * quarter
    parts = n_d if quarter % 16 == 0 else 1
    half = width // 2
    scalar = lambda v: v.astype(jnp.int32).reshape(1)

    me_td = jnp.stack([me_t, me_d]).astype(jnp.int32)

    out_all = lax.all_gather(out_weight, ("tensor", "shard"), axis=0, tiled=False)
    out_all = out_all.reshape(n_t, 2, own, half)
    split = expert_out.shape[1] // 2
    w_own = jnp.stack(
        [expert_in[0], jnp.concatenate([expert_out[0, :split], expert_out[0, split:]], axis=1)]
    )
    w_far = partner(w_own, "tensor", 2)
    w_other = partner(w_own, "shard", 1)
    order_d = (me_d ^ jnp.arange(n_d, dtype=jnp.int32)).astype(jnp.int32)
    order = (me_t ^ jnp.arange(n_t, dtype=jnp.int32)).astype(jnp.int32)
    table_row = jnp.pad(bias_table.reshape(1, -1), ((0, 0), (0, half - heads * (n_b // 2))))
    packed = jnp.concatenate([norm_one[None], norm_two[None], router_weight.T, table_row], axis=0)
    packed_far = partner(packed, "shard", 1)
    qkv_own = qkv_weight.reshape(half, 3 * own)
    qkv_far = partner(qkv_own, "shard", 1)

    place_row, place_abs, x_rows, g_send = slot_rows(
        me_td, routes, kept, slots, cotangent, tokens, quarter, n_t, rows_q, parts, 2 * rows_q // parts
    )
    if parts == 1:
        g_send = [g_send[0][k * 2 * quarter : (k + 1) * 2 * quarter] for k in range(n_d)]

    packed_far, qkv_far, x_rows, g_send = tie(packed_far, qkv_far, x_rows, g_send)
    g_pieces = swap_chunks(g_send, "dp")
    packed = jnp.where(
        me_s == 0,
        jnp.concatenate([packed, packed_far], axis=1),
        jnp.concatenate([packed_far, packed], axis=1),
    )
    gain_one = packed[:1].astype(F32)
    gain_two = packed[1:2].astype(F32)
    router = packed[2 : 2 + n_e]
    table = packed[2 + n_e].reshape(2, half)[:, : heads * (n_b // 2)]
    table = table.reshape(2, heads, n_b // 2).transpose(1, 0, 2).reshape(heads, n_b)

    inputs = tokens.astype(F32)
    normed_one, inv_one, projected, qkv_full = first_norm(scalar(me_s), tokens, gain_one, qkv_own, qkv_far)
    span = 2 * length
    onehot = (
        jnp.pad(buckets, (0, span - buckets.shape[0]), constant_values=-1)[None, :]
        == jnp.arange(n_b, dtype=jnp.int32)[:, None]
    )
    rel = jnp.pad(contract(table, onehot.astype(BF16), 1, 0), ((0, 8 - heads), (0, 0)))
    doc_row = segment_ids.reshape(1, length)
    attended, lse, *att_slots = attend_fwd(
        projected, rel, doc_row, place_row, heads, n_t, rows_q
    )
    attended, att_slots, g_pieces, w_far = tie(attended, att_slots, g_pieces, w_far)
    weights = (w_own, w_other, w_far, partner(w_far, "shard", 1))
    me_ds = jnp.stack([me_d, me_s]).astype(jnp.int32)

    att_rows = swap_chunks(att_slots, "tensor")
    att_ag, *att_rows = tie(attended, *att_rows)
    att_all = lax.all_gather(att_ag, "tensor", axis=0, tiled=False)
    unit_two, inv_two, sent = middle(scalar(me_t), att_rows, out_all, x_rows, gain_two, parts)

    if parts == 1:
        sent = [sent[0][k * quarter : (k + 1) * quarter] for k in range(n_d)]
    arrived = swap_chunks(sent, "dp")
    drop_att = jnp.where(
        (kept == 0)[:, None],
        contract(cotangent[:, :half], out_all[me_t, 0], 1, 1) + contract(cotangent[:, half:], out_all[me_t, 1], 1, 1),
        0.0,
    ).astype(BF16)
    far_first = partner(arrived[0], "tensor", 1) if parts > 1 else None
    drop_att, arrived, far_first = tie(drop_att, arrived, far_first)
    if parts == 1:
        arrived = [jnp.concatenate(arrived, axis=0)]
        g_own = [jnp.concatenate([p[:quarter] for p in g_send], axis=0)]
        g_sides = [
            [jnp.concatenate([p[r * quarter : (r + 1) * quarter] for p in g_pieces], axis=0)] for r in range(2)
        ]
        g_specs = [wholes(g) for g in g_sides]
    else:
        g_own = g_send
        g_sides = [g_pieces, g_pieces]
        at = lambda r: pl.BlockSpec((quarter, width), lambda i: (r, 0))
        g_specs = [[at(r)] * parts for r in range(2)]
    arrived_far = [partner(p, "tensor", 1) for p in arrived[parts > 1 :]]
    if parts > 1:
        arrived_far = [far_first] + arrived_far

    near = expert(me_ds, arrived, g_sides[0], g_specs[0], weights, router, F32)
    near, arrived_far = tie(near, arrived_far)
    far = expert(me_ds, arrived_far, g_sides[1], g_specs[1], weights, router, BF16)
    grad_far = partner(far[0][0], "tensor", 1)
    near, far, att_all = tie(near, far, att_all)
    late = expert_late(scalar(me_s), [near, far], weights)
    grad_far, late = tie(grad_far, late)
    (res_own, res_other, router_part), (near_in, near_out, far_own, others) = late
    res_far = partner(res_other, "tensor", 1)
    others = partner(others, "shard", 1)
    far_part = [(far_own[n] + others[2 + n].astype(F32)).astype(BF16) for n in range(2)]
    back = add_parts(near[0][0], grad_far, parts)
    if parts == 1:
        back = [back[0][k * quarter : (k + 1) * quarter] for k in range(n_d)]
    grad_two = swap_chunks(list(back), "dp")
    if parts == 1:
        grad_two = [jnp.concatenate(grad_two, axis=0)]

    grad_two, far_part = tie(grad_two, far_part)
    far_sum = [partner(v, "tensor", 2) for v in far_part]

    grad_mixed, gain_two_part, grad_att = second_norm_bwd(
        scalar(me_t), grad_two, g_own, g_specs[0], unit_two, inv_two, gain_two, out_all
    )
    grad_att_slots = swap_chunks(list(grad_att), "tensor")
    grad_mixed_ag, res_far, far_sum[0], *grad_att_slots = tie(grad_mixed, res_far, far_sum[0], *grad_att_slots)
    mixed_slots = lax.all_gather(grad_mixed_ag, "tensor", axis=0, tiled=True)
    res = list(add_parts(res_own, res_far, parts))
    if parts == 1:
        res = [res[0][k * quarter : (k + 1) * quarter] for k in range(n_d)]
    res = swap_chunks(res, "dp")

    grad_q, grad_kt, grad_vt, drel = attend_bwd(
        projected, rel, doc_row, lse, place_row, drop_att, grad_att_slots, heads
    )
    grad_q, grad_kt, grad_vt, drel, res, far_sum[1] = tie(grad_q, grad_kt, grad_vt, drel, res, far_sum[1])
    res_slots = lax.all_gather(jnp.concatenate(res, axis=0), "tensor", axis=0, tiled=True)
    grad_proj, gain_one_part, grad_one, sends = first_norm_bwd(
        order, grad_q, grad_kt, grad_vt, qkv_full, tokens, inv_one
    )
    sends, grad_proj = tie(sends, grad_proj)
    got = [partner(v, "tensor", k + 1) for k, v in enumerate(sends)]

    grad_table = jnp.dot(drel[:heads], onehot.astype(F32).T, precision=HIGH)
    small = jnp.concatenate([gain_one_part, gain_two_part, router_part], axis=0)
    n_small = 2 + n_e
    fill = -(half + own + n_small + 1) % (16 * n_d)
    table_row = grad_table.reshape(heads, 2, n_b // 2).transpose(1, 0, 2).reshape(1, 2, heads * n_b // 2)
    table_row = jnp.pad(table_row, ((0, fill), (0, 0), (0, half - heads * n_b // 2))).reshape(fill + 1, width)
    small = jnp.concatenate([small, table_row], axis=0)
    mixed_tok, total, theirs = weight_pack(
        scalar(me_s), place_abs, cotangent, attended, normed_one, grad_proj, small, [mixed_slots]
    )
    got, total, theirs, mixed_tok, far_sum = tie(got, total, theirs, mixed_tok, far_sum)
    theirs = partner(theirs, "shard", 1)
    delta = token_delta(order, tokens, inv_one, gain_one, grad_one, got)
    theirs, delta = tie(theirs, delta)
    delta_pieces = gather_pieces(delta, "tensor")
    total, sends = pair_sum(order_d, total, theirs)
    got = [partner(piece, "dp", k + 1) for k, piece in enumerate(sends)]
    grad_inw, grad_outw = grad_sum(near_in, near_out, others, far_sum)
    got, grad_inw, grad_outw = tie(got, grad_inw, grad_outw)
    for piece in got:
        total = total + piece.astype(F32)
    grad_tokens = place_chunks(order, mixed_tok, delta_pieces)
    pieces = gather_pieces(total.astype(BF16), "dp")
    pieces, grad_tokens = tie(pieces, grad_tokens)
    grad_qkv, grad_out, rest = weight_unpack(order_d, pieces, half, own)
    small = total_over(rest[:n_small], "tensor")
    grad_table = rest[n_small, : heads * n_b // 2].reshape(heads, n_b // 2)

    output = layer_output(place_abs, tokens, att_all, out_all, res_slots)
    return (
        output,
        grad_tokens,
        small[0],
        small[1],
        grad_qkv.reshape(half, 3, own),
        grad_out,
        grad_table,
        small[2:].T,
        grad_inw[None],
        grad_outw[None],
    )


def solution(mesh):
    placed = (
        P(("dp", "shard"), None),
        P(("dp", "shard"), None),
        P(),
        P(("dp", "shard")),
        P(("dp", "shard")),
        P(("dp", "shard")),
        P(("dp", "shard"), None),
        P("shard"),
        P("shard"),
        P("shard", None, "tensor"),
        P("tensor", "shard"),
        P("tensor", "shard"),
        P("shard", None),
        P("dp", "shard", "tensor"),
        P("dp", "tensor", "shard"),
    )
    return jax.shard_map(
        body,
        mesh=mesh,
        in_specs=placed,
        out_specs=(
            P(("dp", "shard"), None),
            P(("dp", "shard"), None),
            P("shard"),
            P("shard"),
            P("shard", None, "tensor"),
            P("tensor", "shard"),
            P("tensor", "shard"),
            P("shard", None),
            P("dp", "shard", "tensor"),
            P("dp", "tensor", "shard"),
        ),
        check_vma=False,
    )
```

```python
import functools

import jax
import jax.numpy as jnp
from jax import lax
from jax.experimental import pallas as pl
from jax.experimental.pallas import tpu as pltpu
from jax.sharding import PartitionSpec as P

DH = 64
EPS = 1e-06
NEG = -1e30
VMEM_MIB = 52
HIGH = lax.Precision.HIGHEST
BQ = 512
BQ_BACK = 1024
TB = 128
F32 = jnp.float32
BF16 = jnp.bfloat16


def contract(left, right, left_dim, right_dim):
    return lax.dot_general(
        left, right, (((left_dim,), (right_dim,)), ((), ())), preferred_element_type=F32
    )


def partner(value, axis, step):
    size = lax.axis_size(axis)
    return lax.ppermute(value, axis, [(i, i ^ step) for i in range(size)])


def swap_chunks(chunks, axis):
    return [chunks[0]] + [partner(c, axis, k) for k, c in enumerate(chunks) if k]


def gather_pieces(value, axis):
    return swap_chunks([value] * lax.axis_size(axis), axis)


def pick_rows(place_row, start, rows):
    at = lax.broadcasted_iota(jnp.int32, (rows, place_row.shape[1]), 0) + start
    return (at == place_row).astype(F32).astype(BF16)


def as_col(row):
    wide = jnp.broadcast_to(row.astype(F32), (128, row.shape[1]))
    return wide.T[:, :1].astype(jnp.int32)


def pick_cols(place_col, start, rows):
    at = lax.broadcasted_iota(jnp.int32, (place_col.shape[0], rows), 1) + start
    return (at == place_col).astype(F32).astype(BF16)


def shear_table(rel_ref, table_ref, heads, span):
    for h in range(heads):
        row = jnp.broadcast_to(rel_ref[h : h + 1, :], (TB, span))
        table_ref[h] = pltpu.roll(row, span - (TB - 1), 1, stride=1, stride_axis=0)


def table_starts(step, rows, length):
    last = length // TB - 1
    return [pl.multiple_of((last - step * (rows // TB) - a) * TB, TB) for a in range(rows // TB)]


def bias_of(table_ref, h, starts, length):
    return jnp.concatenate([table_ref[h, :, pl.ds(at, length)] for at in starts], axis=0)


def attend_fwd_kernel(
    qkv_ref, rel_ref, doc_row_ref, place_ref, out_ref, lse_ref, *rest, heads
):
    slot_refs, table_ref = rest[:-1], rest[-1]
    length = qkv_ref.shape[0]
    blocks = length // BQ
    width = heads * DH
    step = pl.program_id(0)

    @pl.when(step == 0)
    def _():
        shear_table(rel_ref, table_ref, heads, table_ref.shape[2])

    row0 = pl.multiple_of(step * BQ, BQ)
    starts = table_starts(step, BQ, length)
    same = as_col(doc_row_ref[:, pl.ds(row0, BQ)]) == doc_row_ref[...]
    outs, stats = [], []
    for h in range(heads):
        q = qkv_ref[pl.ds(row0, BQ), h * DH : (h + 1) * DH] * 0.125
        k = qkv_ref[:, width + h * DH : width + (h + 1) * DH]
        v = qkv_ref[:, 2 * width + h * DH : 2 * width + (h + 1) * DH]
        s = contract(q, k, 1, 1) + bias_of(table_ref, h, starts, length)
        s = jnp.where(same, s, NEG)
        top = jnp.max(s, axis=1, keepdims=True)
        e = jnp.exp(s - top)
        total = jnp.sum(e, axis=1, keepdims=True)
        o = contract(e.astype(BF16), v, 1, 0)
        outs.append(o * (1.0 / total))
        stats.append(top + jnp.log(total))
    out_ref[pl.ds(row0, BQ), :] = jnp.concatenate(outs, axis=1).astype(BF16)
    lse_ref[...] = jnp.concatenate(stats, axis=1)

    @pl.when(step == blocks - 1)
    def _():
        place = place_ref[...]
        for n, ref in enumerate(slot_refs):
            ref[...] = contract(pick_rows(place, n * ref.shape[0], ref.shape[0]), out_ref[...], 1, 0).astype(BF16)


def attend_bwd_kernel(
    qkv_ref, rel_ref, doc_row_ref, lse_ref, place_ref, drop_ref, *rest, heads,
):
    slot_refs = rest[:-9]
    dq_ref, dk_ref, dv_ref, drel_ref, table_ref, acc_ref, dk_acc, dv_acc, grad_ref = rest[-9:]
    length = qkv_ref.shape[0]
    blocks = length // BQ_BACK
    width = heads * DH
    span = table_ref.shape[2]
    step = pl.program_id(0)

    @pl.when(step == 0)
    def _():
        shear_table(rel_ref, table_ref, heads, span)
        acc_ref[...] = jnp.zeros(acc_ref.shape, F32)
        dk_acc[...] = jnp.zeros(dk_acc.shape, F32)
        dv_acc[...] = jnp.zeros(dv_acc.shape, F32)
        grad = drop_ref[...].astype(F32)
        place = as_col(place_ref[...])
        for n, ref in enumerate(slot_refs):
            grad = grad + contract(pick_cols(place, n * ref.shape[0], ref.shape[0]), ref[...], 1, 0)
        grad_ref[...] = grad.astype(BF16)

    row0 = pl.multiple_of(step * BQ_BACK, BQ_BACK)
    starts = table_starts(step, BQ_BACK, length)
    same = as_col(doc_row_ref[:, pl.ds(row0, BQ_BACK)]) == doc_row_ref[...]
    dqs = []
    for h in range(heads):
        q = qkv_ref[pl.ds(row0, BQ_BACK), h * DH : (h + 1) * DH] * 0.125
        k = qkv_ref[:, width + h * DH : width + (h + 1) * DH]
        v = qkv_ref[:, 2 * width + h * DH : 2 * width + (h + 1) * DH]
        g = grad_ref[pl.ds(row0, BQ_BACK), h * DH : (h + 1) * DH]
        s = contract(q, k, 1, 1) + bias_of(table_ref, h, starts, length)
        s = jnp.where(same, s, NEG)
        p = jnp.exp(s - lse_ref[:, h : h + 1])
        dp = contract(g, v, 1, 1)
        inner = jnp.sum(p * dp, axis=1, keepdims=True)
        ds = p * (dp - inner)
        dsb = ds.astype(BF16)
        for a, at in enumerate(starts):
            acc_ref[h, :, pl.ds(at, length)] += ds[a * TB : (a + 1) * TB]
        dqs.append(0.125 * contract(dsb, k, 1, 0))
        dk_acc[h * DH : (h + 1) * DH, :] += contract(q, dsb, 0, 0)
        dv_acc[h * DH : (h + 1) * DH, :] += contract(g, p.astype(BF16), 0, 0)
    dq_ref[...] = jnp.concatenate(dqs, axis=1).astype(BF16)

    @pl.when(step == blocks - 1)
    def _():
        dk_ref[...] = dk_acc[...].astype(BF16)
        dv_ref[...] = dv_acc[...].astype(BF16)
        for h in range(heads):
            rows = acc_ref[h]
            half = TB // 2
            while half >= 1:
                rows = pltpu.roll(rows[:half], half, 1) + rows[half:]
                half //= 2
            drel_ref[h : h + 1, :] = rows


def whole(shape):
    return pl.BlockSpec(shape, lambda *i: (0,) * len(shape))


def wholes(arrays):
    return [whole(a.shape) for a in arrays]


def params():
    return pltpu.CompilerParams(vmem_limit_bytes=VMEM_MIB * 1024 * 1024)


def struct(shape, dtype):
    return jax.ShapeDtypeStruct(shape, dtype)


def attend_specs(length, heads, span):
    return [
        whole((length, 3 * heads * DH)),
        whole((8, span)),
        whole((1, length)),
    ]


def attend_fwd(projected, rel, doc_row, place_row, heads, parts, part_rows):
    length = projected.shape[0]
    span = rel.shape[1]
    width = heads * DH
    return pl.pallas_call(
        functools.partial(attend_fwd_kernel, heads=heads),
        grid=(length // BQ,),
        in_specs=attend_specs(length, heads, span) + [whole((1, length))],
        out_specs=[whole((length, width)), pl.BlockSpec((BQ, heads), lambda i: (i, 0))]
        + [whole((part_rows, width))] * parts,
        out_shape=[struct((length, width), BF16), struct((length, heads), F32)]
        + [struct((part_rows, width), BF16)] * parts,
        scratch_shapes=[pltpu.VMEM((heads, TB, span), F32)],
        compiler_params=params(),
        name="attend_fwd",
    )(projected, rel, doc_row, place_row)


def attend_bwd(projected, rel, doc_row, lse, place_row, drop, grads, heads):
    length = projected.shape[0]
    span = rel.shape[1]
    width = heads * DH
    return pl.pallas_call(
        functools.partial(attend_bwd_kernel, heads=heads),
        grid=(length // BQ_BACK,),
        in_specs=attend_specs(length, heads, span)
        + [pl.BlockSpec((BQ_BACK, heads), lambda i: (i, 0)), whole((1, length)), whole((length, width))]
        + wholes(grads),
        out_specs=[
            pl.BlockSpec((BQ_BACK, width), lambda i: (i, 0)),
            whole((width, length)),
            whole((width, length)),
            whole((8, span)),
        ],
        out_shape=[
            struct((length, width), BF16),
            struct((width, length), BF16),
            struct((width, length), BF16),
            struct((8, span), F32),
        ],
        scratch_shapes=[
            pltpu.VMEM((heads, TB, span), F32),
            pltpu.VMEM((heads, TB, span), F32),
            pltpu.VMEM((width, length), F32),
            pltpu.VMEM((width, length), F32),
            pltpu.VMEM((length, width), BF16),
        ],
        compiler_params=params(),
        name="attend_bwd",
    )(projected, rel, doc_row, lse, place_row, drop, *grads)


def store_parts(refs, value):
    if len(refs) == 1:
        refs[0][...] = value
        return
    rows = refs[0].shape[0]
    for n, ref in enumerate(refs):
        ref[...] = value[n * rows : (n + 1) * rows]


def load_parts(refs):
    if len(refs) == 1:
        return refs[0][...]
    return jnp.concatenate([ref[...] for ref in refs], axis=0)


def slot_rows_kernel(me_ref, routes_ref, kept_ref, slots_ref, cot_ref, tok_ref, rel_ref, abs_ref, x_ref, *g_refs, quarter, n_t, rows_q):
    slots = slots_ref[...]
    part = jnp.zeros(slots.shape, jnp.int32)
    for k in range(1, n_t):
        part = part + (slots >= k * quarter).astype(jnp.int32)
    spot = slots - part * quarter
    taken = kept_ref[...] > 0
    rel_t = part ^ me_ref[0]
    rel_d = routes_ref[...] ^ me_ref[1]
    rel = jnp.where(taken, rel_t * rows_q + rel_d * quarter + spot, -1)
    rel_ref[...] = rel
    abs_ref[...] = jnp.where(taken, part * rows_q + rel_d * quarter + spot, -1)
    place_g = jnp.where(taken & (rel_t < 2), (rel_d * 2 + rel_t) * quarter + spot, -1)
    rows = g_refs[0].shape[0]
    for n, ref in enumerate(g_refs):
        ref[...] = contract(pick_rows(place_g, n * rows, rows), cot_ref[...], 1, 0).astype(BF16)
    x_ref[...] = contract(pick_rows(rel, 0, x_ref.shape[0]), tok_ref[...], 1, 0).astype(BF16)


def slot_rows(me, routes, kept, slots, cotangent, tokens, quarter, n_t, rows_q, parts, part_rows):
    length, width = tokens.shape
    shapes = [struct((1, length), jnp.int32)] * 2 + [struct((rows_q, width), BF16)]
    shapes += [struct((part_rows, width), BF16)] * parts
    operands = [routes.reshape(1, -1), kept.reshape(1, -1), slots.reshape(1, -1), cotangent, tokens]
    out = pl.pallas_call(
        functools.partial(slot_rows_kernel, quarter=quarter, n_t=n_t, rows_q=rows_q),
        grid=(1,),
        in_specs=[pl.BlockSpec(memory_space=pltpu.SMEM)] + wholes(operands),
        out_specs=[whole(v.shape) for v in shapes],
        out_shape=shapes,
        compiler_params=params(),
        name="slot_rows",
    )(me, *operands)
    return out[0], out[1], out[2], out[3:]


def first_norm_kernel(me_ref, tok_ref, gain_ref, w_ref, w_far_ref, normed_ref, inv_ref, proj_ref, full_ref):
    half = w_ref.shape[0]
    mine = pl.multiple_of(me_ref[0] * half, half)
    theirs = pl.multiple_of((1 - me_ref[0]) * half, half)
    x = tok_ref[...].astype(F32)
    inv = lax.rsqrt(jnp.mean(x * x, axis=1, keepdims=True) + EPS)
    inv_ref[...] = inv
    normed_ref[...] = (x * inv * gain_ref[...]).astype(BF16)
    proj_ref[...] = (
        contract(normed_ref[:, pl.ds(mine, half)], w_ref[...], 1, 0)
        + contract(normed_ref[:, pl.ds(theirs, half)], w_far_ref[...], 1, 0)
    ).astype(BF16)

    @pl.when(pl.program_id(0) == 0)
    def _():
        full_ref[pl.ds(mine, half), :] = w_ref[...]
        full_ref[pl.ds(theirs, half), :] = w_far_ref[...]


def first_norm(me_s, tokens, gain, w_own, w_far):
    length, width = tokens.shape
    out_width = w_own.shape[1]
    rows = length // 4
    block = lambda n: pl.BlockSpec((rows, n), lambda i: (i, 0))
    return pl.pallas_call(
        first_norm_kernel,
        grid=(4,),
        in_specs=[pl.BlockSpec(memory_space=pltpu.SMEM), block(width)] + wholes([gain, w_own, w_far]),
        out_specs=[block(width), block(1), block(out_width), whole((width, out_width))],
        out_shape=[
            struct((length, width), BF16),
            struct((length, 1), F32),
            struct((length, out_width), BF16),
            struct((width, out_width), BF16),
        ],
        compiler_params=params(),
        name="first_norm",
    )(me_s, tokens, gain, w_own, w_far)


def middle_kernel(me_ref, *refs, n_t, parts):
    att, (w_ref, x_ref, gain_ref) = refs[:n_t], refs[n_t : n_t + 3]
    unit_ref, inv_ref = refs[n_t + 3 : n_t + 5]
    outs = refs[n_t + 5 :]
    sides = []
    for half in range(2):
        total = contract(att[0][...], w_ref[me_ref[0], half], 1, 0)
        for k in range(1, n_t):
            total = total + contract(att[k][...], w_ref[me_ref[0] ^ k, half], 1, 0)
        sides.append(total)
    resid = x_ref[...].astype(F32) + jnp.concatenate(sides, axis=1)
    inv = lax.rsqrt(jnp.mean(resid * resid, axis=1, keepdims=True) + EPS)
    unit = resid * inv
    unit_ref[...] = unit
    inv_ref[...] = inv
    store_parts(outs, (unit * gain_ref[...]).astype(BF16))


def middle(me_t, att, w_rel, x_rows, gain, parts):
    rows, width = x_rows.shape
    operands = (*att, w_rel, x_rows, gain)
    shapes = [struct((rows, width), F32), struct((rows, 1), F32)]
    shapes += [struct((rows // parts, width), BF16)] * parts
    out = pl.pallas_call(
        functools.partial(middle_kernel, n_t=len(att), parts=parts),
        grid=(1,),
        in_specs=[pl.BlockSpec(memory_space=pltpu.SMEM)] + wholes(operands),
        out_specs=[whole(v.shape) for v in shapes],
        out_shape=shapes,
        compiler_params=params(),
        name="second_norm",
    )(me_t, *operands)
    return out[0], out[1], out[2:]


def expert_kernel(me_ref, *refs, parts, chunks, n_e):
    refs, (win_buf, wout_buf, sems) = refs[:-3], refs[-3:]
    rows_refs, g_refs = refs[:parts], refs[parts : 2 * parts]
    pieces, router_ref = refs[2 * parts : 2 * parts + 4], refs[2 * parts + 4]
    outs = refs[2 * parts + 5 :]
    half = pieces[0].shape[1]
    mine = pl.multiple_of(me_ref[1] * half, half)
    theirs = pl.multiple_of((1 - me_ref[1]) * half, half)
    copies = []
    for c in range(chunks):
        moves = []
        for piece, start in ((pieces[2 * c], mine), (pieces[2 * c + 1], theirs)):
            moves.append((piece.at[0], win_buf.at[c, pl.ds(start, half)]))
        for piece, side in ((pieces[2 * c], me_ref[1]), (pieces[2 * c + 1], 1 - me_ref[1])):
            for n in range(2):
                part = pl.ds(n * half, half)
                moves.append((piece.at[1, :, part], wout_buf.at[c, side, part]))
        copies.append([pltpu.make_async_copy(a, b, sems.at[6 * c + i]) for i, (a, b) in enumerate(moves)])
        for copy in copies[-1]:
            copy.start()
    grad_ref, rows_ref, slot_ref, gate_ref, logit_ref = outs[:5]
    hid_refs, gpre_refs = outs[5 : 5 + chunks], outs[5 + chunks :]
    rows = load_parts(rows_refs)
    g = load_parts(g_refs)
    router = router_ref[...]
    logits = contract(rows, router, 1, 1)
    exp_logits = jnp.exp(logits - jnp.max(logits, axis=1, keepdims=True))
    probs = exp_logits / jnp.sum(exp_logits, axis=1, keepdims=True)
    chosen = (lax.broadcasted_iota(jnp.int32, logits.shape, 1) == me_ref[0]).astype(F32)
    gate = jnp.sum(probs * chosen, axis=1, keepdims=True)
    grad_gate = jnp.zeros(gate.shape, F32)
    total = None
    for c in range(chunks):
        for copy in copies[c][:2]:
            copy.wait()
        pre = contract(rows, win_buf[c], 1, 0)
        value, slope = gelu_pair(pre)
        hidden = value.astype(BF16)
        hid_refs[c][...] = hidden
        for copy in copies[c][2:]:
            copy.wait()
        raw = contract(g[:, :half], wout_buf[c, 0], 1, 1) + contract(g[:, half:], wout_buf[c, 1], 1, 1)
        grad_gate = grad_gate + jnp.sum(hidden.astype(F32) * raw, axis=1, keepdims=True)
        grad_pre = (gate * raw * slope).astype(BF16)
        gpre_refs[c][...] = grad_pre
        part = contract(grad_pre, win_buf[c], 1, 1)
        total = part if total is None else total + part
    grad_logits = (grad_gate * probs * (chosen - gate)).astype(BF16)
    total = total + contract(grad_logits, router, 1, 0)
    grad_ref[...] = total.astype(grad_ref.dtype)
    rows_ref[...] = rows
    slot_ref[...] = (gate * g.astype(F32)).astype(BF16)
    gate_ref[...] = gate
    logit_ref[...] = grad_logits


def expert(me, rows, g, g_specs, weights, router, grad_dtype):
    parts, chunks = len(rows), 2
    total = sum(r.shape[0] for r in rows)
    width = rows[0].shape[1]
    hidden = weights[0].shape[2]
    n_e = router.shape[0]
    out = pl.pallas_call(
        functools.partial(expert_kernel, parts=parts, chunks=chunks, n_e=n_e),
        grid=(1,),
        in_specs=[pl.BlockSpec(memory_space=pltpu.SMEM)]
        + wholes(rows) + g_specs + [pl.BlockSpec(memory_space=pltpu.HBM)] * 4 + [whole(router.shape)],
        out_specs=[
            whole((total, width)), whole((total, width)), whole((total, width)), whole((total, 1)), whole((total, n_e))
        ] + [whole((total, hidden))] * (2 * chunks),
        out_shape=[
            struct((total, width), grad_dtype),
            struct((total, width), BF16),
            struct((total, width), BF16),
            struct((total, 1), F32),
            struct((total, n_e), BF16),
        ]
        + [struct((total, hidden), BF16)] * (2 * chunks),
        scratch_shapes=[
            pltpu.VMEM((chunks, width, hidden), BF16),
            pltpu.VMEM((chunks, 2, hidden, width // 2), BF16),
            pltpu.SemaphoreType.DMA((12,)),
        ],
        compiler_params=params(),
        name="expert",
    )(me, *rows, *g, *weights, router)
    return out[:5], out[5 : 5 + chunks], out[5 + chunks :]


def expert_late_kernel(me_ref, *refs, groups, chunks):
    side = lambda n: refs[n * groups : (n + 1) * groups]
    rows, slot, gate, logit = (side(n) for n in range(4))
    at = 4 * groups
    hid = [refs[at + c * groups : at + (c + 1) * groups] for c in range(chunks)]
    at += chunks * groups
    gpre = [refs[at + c * groups : at + (c + 1) * groups] for c in range(chunks)]
    at += chunks * groups
    out_own, out_other, far_out_own, far_out_other = refs[at : at + 4]
    res_own, res_other, router_ref, near_in, near_out, far_own, others = refs[at + 4 :]
    half = rows[0].shape[1] // 2
    mine = pl.multiple_of(me_ref[0] * half, half)
    theirs = pl.multiple_of((1 - me_ref[0]) * half, half)
    for r, ref in enumerate((res_own, res_other)):
        for start, sides in ((mine, (out_own, far_out_own)), (theirs, (out_other, far_out_other))):
            total = jnp.zeros((ref.shape[0], half), F32)
            for c, side in enumerate(sides):
                for n in range(2):
                    part = slice(n * half, (n + 1) * half)
                    total = total + contract(hid[c][r][:, part], side[0, :, part], 1, 0)
            ref[:, pl.ds(start, half)] = (gate[r][...] * total).astype(ref.dtype)
    router_ref[...] = contract(logit[0][...], rows[0][...], 0, 0) + contract(logit[1][...], rows[1][...], 0, 0)
    both = lambda refs, start: jnp.concatenate([ref[:, pl.ds(start, half)] for ref in refs], axis=0)
    rows_mine, rows_theirs = both(rows, mine).T, both(rows, theirs).T
    slot_mine, slot_theirs = both(slot, mine), both(slot, theirs)
    for c in range(chunks):
        grads = jnp.concatenate([ref[...] for ref in gpre[c]], axis=0)
        units = jnp.concatenate([ref[...] for ref in hid[c]], axis=0).T
        others[2 * c] = contract(rows_theirs, grads, 1, 0).astype(BF16)
        out_t = contract(units, slot_theirs, 1, 0).astype(BF16)
        others[2 * c + 1, :, :half] = out_t[:half]
        others[2 * c + 1, :, half:] = out_t[half:]
        in_m = contract(rows_mine, grads, 1, 0)
        out_m = contract(units, slot_mine, 1, 0)
        if c == 0:
            near_in[...] = in_m
            near_out[...] = out_m
        else:
            far_own[0] = in_m
            far_own[1, :, :half] = out_m[:half]
            far_own[1, :, half:] = out_m[half:]


def grad_sum_kernel(near_in, near_out, other_ref, far_in, far_out, in_ref, out_ref):
    half = near_in.shape[0]
    in_ref[...] = near_in[...] + other_ref[0].astype(F32) + far_in[...].astype(F32)
    side = other_ref[1].astype(F32) + far_out[...].astype(F32)
    out_ref[:half] = near_out[:half] + side[:, :half]
    out_ref[half:] = near_out[half:] + side[:, half:]


def grad_sum(near_in, near_out, others, far):
    return pl.pallas_call(
        grad_sum_kernel,
        grid=(1,),
        in_specs=wholes([near_in, near_out]) + [whole((2,) + others.shape[1:])] + wholes(far),
        out_specs=wholes([near_in, near_out]),
        out_shape=[struct(near_in.shape, F32), struct(near_out.shape, F32)],
        compiler_params=params(),
        name="grad_sum",
    )(near_in, near_out, others, *far)


def layer_output_kernel(place_ref, tok_ref, att_ref, w_ref, slots_ref, out_ref, *, n_t):
    sides = []
    for half in range(2):
        total = contract(att_ref[0], w_ref[0, half], 1, 0)
        for k in range(1, n_t):
            total = total + contract(att_ref[k], w_ref[k, half], 1, 0)
        sides.append(total)
    resid = tok_ref[...].astype(F32) + jnp.concatenate(sides, axis=1)
    found = contract(pick_cols(as_col(place_ref[...]), 0, slots_ref.shape[0]), slots_ref[...], 1, 0)
    out_ref[...] = (resid + found).astype(BF16)


def layer_output(place_row, tokens, att_all, w_all, res_slots):
    length, width = tokens.shape
    n_t, _, own = att_all.shape
    rows = length // 4
    block = lambda n: pl.BlockSpec((rows, n), lambda i: (i, 0))
    return pl.pallas_call(
        functools.partial(layer_output_kernel, n_t=n_t),
        grid=(4,),
        in_specs=[
            pl.BlockSpec((1, rows), lambda i: (0, i)), block(width), pl.BlockSpec((n_t, rows, own), lambda i: (0, i, 0)),
            whole(w_all.shape), whole(res_slots.shape),
        ],
        out_specs=block(width),
        out_shape=struct((length, width), BF16),
        compiler_params=params(),
        name="layer_output",
    )(place_row, tokens, att_all, w_all, res_slots)


def expert_late(me_s, groups, w_out):
    chunks = 2
    operands = []
    for n in (1, 2, 3, 4):
        operands += [grp[0][n] for grp in groups]
    for kind in (1, 2):
        for c in range(chunks):
            operands += [grp[kind][c] for grp in groups]
    specs = wholes(operands) + [pl.BlockSpec((1,) + w.shape[1:], lambda i: (1, 0, 0)) for w in w_out]
    operands += list(w_out)
    rows, width = groups[0][0][1].shape
    hidden = groups[0][1][0].shape[1]
    n_e = groups[0][0][4].shape[1]
    half = width // 2
    shapes = [struct((rows, width), F32), struct((rows, width), BF16), struct((n_e, width), F32)]
    shapes += [
        struct((half, hidden), F32), struct((hidden, half), F32),
        struct((2, half, hidden), F32), struct((4, half, hidden), BF16),
    ]
    out = pl.pallas_call(
        functools.partial(expert_late_kernel, groups=len(groups), chunks=chunks),
        grid=(1,),
        in_specs=[pl.BlockSpec(memory_space=pltpu.SMEM)] + specs,
        out_specs=[whole(s.shape) for s in shapes],
        out_shape=shapes,
        compiler_params=params(),
        name="expert_late",
    )(me_s, *operands)
    return out[:3], out[3:]


def add_parts_kernel(own_ref, other_ref, *outs):
    store_parts(outs, (own_ref[...] + other_ref[...].astype(F32)).astype(BF16))


def add_parts(own, other, parts):
    rows, width = own.shape
    return pl.pallas_call(
        add_parts_kernel,
        out_shape=[struct((rows // parts, width), BF16)] * parts,
        compiler_params=params(),
        name="add_parts",
    )(own, other)


def second_norm_bwd_kernel(me_ref, *refs, parts, n_t):
    grads, g_refs = refs[:parts], refs[parts : 2 * parts]
    unit_ref, inv_ref, gain_ref, w_ref, mixed_ref, gain_out_ref = refs[2 * parts : 2 * parts + 6]
    outs = refs[2 * parts + 6 :]
    grad = load_parts(grads).astype(F32)
    unit = unit_ref[...]
    gain_out_ref[...] = jnp.sum(grad * unit, axis=0, keepdims=True)
    scaled = grad * gain_ref[...]
    resid = load_parts(g_refs).astype(F32) + inv_ref[...] * (
        scaled - unit * jnp.mean(scaled * unit, axis=1, keepdims=True)
    )
    mixed = resid.astype(BF16)
    mixed_ref[...] = mixed
    half = mixed.shape[1] // 2
    for k, ref in enumerate(outs):
        at = me_ref[0] ^ k
        ref[...] = (
            contract(mixed[:, :half], w_ref[at, 0], 1, 1) + contract(mixed[:, half:], w_ref[at, 1], 1, 1)
        ).astype(BF16)


def second_norm_bwd(me_t, grads, g, g_specs, unit, inv, gain, w_rel):
    rows, width = unit.shape
    n_t, own = w_rel.shape[0], w_rel.shape[2]
    shapes = [struct((rows, width), BF16), struct((1, width), F32)] + [struct((rows, own), BF16)] * n_t
    out = pl.pallas_call(
        functools.partial(second_norm_bwd_kernel, parts=len(grads), n_t=n_t),
        grid=(1,),
        in_specs=[pl.BlockSpec(memory_space=pltpu.SMEM)]
        + wholes(grads) + g_specs + wholes([unit, inv, gain, w_rel]),
        out_specs=[whole(s.shape) for s in shapes],
        out_shape=shapes,
        compiler_params=params(),
        name="second_norm_bwd",
    )(me_t, *grads, *g, unit, inv, gain, w_rel)
    return out[0], out[1], out[2:]


def first_norm_bwd_kernel(order_ref, dq_ref, dk_ref, dv_ref, w_ref, tok_ref, inv_ref, proj_ref, gain_ref, own_ref, *sends):
    step = pl.program_id(0)
    flip = lambda ref: ref[...].astype(F32).T.astype(BF16)
    grads = jnp.concatenate([dq_ref[...], flip(dk_ref), flip(dv_ref)], axis=1)
    proj_ref[...] = grads
    part = contract(grads, w_ref[...], 1, 1)

    @pl.when(step == 0)
    def _():
        gain_ref[...] = jnp.zeros(gain_ref.shape, F32)
        own_ref[...] = part

    gain_ref[...] += jnp.sum(part * (tok_ref[...].astype(F32) * inv_ref[...]), axis=0, keepdims=True)
    for k, ref in enumerate(sends):

        @pl.when(step == k + 1)
        def _():
            ref[...] = part.astype(BF16)


def first_norm_bwd(order, grad_q, grad_kt, grad_vt, qkv_full, tokens, inv):
    count = order.shape[0]
    length, width = tokens.shape
    own = grad_q.shape[1]
    rows = length // count
    block = lambda n: pl.BlockSpec((rows, n), lambda i, order: (order[i], 0))
    side = pl.BlockSpec((own, rows), lambda i, order: (0, order[i]))
    out = pl.pallas_call(
        first_norm_bwd_kernel,
        grid_spec=pltpu.PrefetchScalarGridSpec(
            num_scalar_prefetch=1,
            grid=(count,),
            in_specs=[block(own), side, side, whole(qkv_full.shape), block(width), block(1)],
            out_specs=[block(3 * own), whole((1, width))] + [whole((rows, width))] * count,
        ),
        out_shape=[struct((length, 3 * own), BF16), struct((1, width), F32), struct((rows, width), F32)]
        + [struct((rows, width), BF16)] * (count - 1),
        compiler_params=params(),
        name="first_norm_bwd",
    )(order, grad_q, grad_kt, grad_vt, qkv_full, tokens, inv)
    return out[0], out[1], out[2], out[3:]


def token_delta_kernel(order_ref, tok_ref, inv_ref, gain_ref, own_ref, *refs):
    got, out_ref = refs[:-1], refs[-1]
    grad = own_ref[...]
    for ref in got:
        grad = grad + ref[...].astype(F32)
    inv = inv_ref[...]
    unit = tok_ref[...].astype(F32) * inv
    scaled = grad * gain_ref[...]
    out_ref[...] = (inv * (scaled - unit * jnp.mean(scaled * unit, axis=1, keepdims=True))).astype(BF16)


def token_delta(order, tokens, inv, gain, own, got):
    rows, width = own.shape
    block = lambda n: pl.BlockSpec((rows, n), lambda i, order: (order[0], 0))
    return pl.pallas_call(
        token_delta_kernel,
        grid_spec=pltpu.PrefetchScalarGridSpec(
            num_scalar_prefetch=1,
            grid=(1,),
            in_specs=[block(width), block(1)] + wholes([gain, own, *got]),
            out_specs=whole((rows, width)),
        ),
        out_shape=struct((rows, width), BF16),
        compiler_params=params(),
        name="token_delta",
    )(order, tokens, inv, gain, own, *got)


def weight_pack_kernel(me_ref, place_ref, cot_ref, att_ref, normed_ref, proj_ref, small_ref, *refs, half):
    slot_refs, (mixed_ref, own_ref, other_ref, acc_ref) = refs[:-4], refs[-4:]
    rows = att_ref.shape[1]
    mine = pl.multiple_of(me_ref[0] * half, half)
    theirs = pl.multiple_of((1 - me_ref[0]) * half, half)
    step = pl.program_id(0)
    place = as_col(place_ref[...])
    found = jnp.zeros(cot_ref.shape, F32)
    for n, ref in enumerate(slot_refs):
        found = found + contract(pick_cols(place, n * ref.shape[0], ref.shape[0]), ref[...], 1, 0)
    mixed_ref[...] = jnp.where(place < 0, cot_ref[...], found.astype(BF16))

    @pl.when(step == 0)
    def _():
        for ref, start in ((own_ref, mine), (acc_ref, theirs)):
            ref[...] = jnp.zeros(ref.shape, F32)
            side = small_ref[:, pl.ds(start, half)]
            count, lanes = side.shape[0], ref.shape[1] - half
            ref[half : half + count, half:] = side[:, :lanes]
            ref[half + count : half + 2 * count, half:] = side[:, lanes:]

    proj = proj_ref[...]
    att = att_ref[...]
    for ref, start in ((own_ref, mine), (acc_ref, theirs)):
        ref[:half] += contract(normed_ref[:, pl.ds(start, half)], proj, 0, 0)
        ref[half : half + rows, :half] += contract(att, mixed_ref[:, pl.ds(start, half)], 0, 0)

    @pl.when(step == pl.num_programs(0) - 1)
    def _():
        other_ref[...] = acc_ref[...].astype(BF16)


def weight_pack(me_s, place_row, cotangent, attended, normed, proj, small, mixed_slots, total):
    length, width = normed.shape
    own = attended.shape[1]
    shape = (total, proj.shape[1])
    rows = length // 4
    block = lambda n: pl.BlockSpec((rows, n), lambda i: (i, 0))
    return pl.pallas_call(
        functools.partial(weight_pack_kernel, half=width // 2),
        grid=(4,),
        in_specs=[
            pl.BlockSpec(memory_space=pltpu.SMEM), pl.BlockSpec((1, rows), lambda i: (0, i)),
            block(width), block(own), block(width), block(proj.shape[1]), whole(small.shape),
        ]
        + wholes(mixed_slots),
        out_specs=[block(width), whole(shape), whole(shape)],
        out_shape=[struct((length, width), BF16), struct(shape, F32), struct(shape, BF16)],
        scratch_shapes=[pltpu.VMEM(shape, F32)],
        compiler_params=params(),
        name="weight_pack",
    )(me_s, place_row, cotangent, attended, normed, proj, small, *mixed_slots)


def pair_sum_kernel(order_ref, own_ref, other_ref, keep_ref, *sends):
    total = own_ref[...] + other_ref[...].astype(F32)
    step = pl.program_id(0)

    @pl.when(step == 0)
    def _():
        keep_ref[...] = total

    for k, ref in enumerate(sends):

        @pl.when(step == k + 1)
        def _():
            ref[...] = total.astype(BF16)


def pair_sum(order, own, other):
    count = order.shape[0]
    rows, width = own.shape[0] // count, own.shape[1]
    block = pl.BlockSpec((rows, width), lambda i, order: (order[i], 0))
    out = pl.pallas_call(
        pair_sum_kernel,
        grid_spec=pltpu.PrefetchScalarGridSpec(
            num_scalar_prefetch=1,
            grid=(count,),
            in_specs=[block, block],
            out_specs=[whole((rows, width))] * count,
        ),
        out_shape=[struct((rows, width), F32)] + [struct((rows, width), BF16)] * (count - 1),
        compiler_params=params(),
        name="pair_sum",
    )(order, own, other)
    return out[0], out[1:]


def place_chunks_kernel(order_ref, base_ref, *refs, count):
    step = pl.program_id(0)
    out_ref = refs[-1]
    for k in range(count):

        @pl.when(step == k)
        def _():
            out_ref[...] = base_ref[...].astype(F32) + refs[k][...].astype(F32)


def place_chunks(order, base, pieces):
    count = len(pieces)
    rows, width = pieces[0].shape
    block = pl.BlockSpec((rows, width), lambda i, order: (order[i], 0))
    return pl.pallas_call(
        functools.partial(place_chunks_kernel, count=count),
        grid_spec=pltpu.PrefetchScalarGridSpec(
            num_scalar_prefetch=1, grid=(count,), in_specs=[block] + wholes(pieces), out_specs=block
        ),
        out_shape=struct((count * rows, width), F32),
        compiler_params=params(),
        name="place_chunks",
    )(order, base, *pieces)


def weight_unpack_kernel(order_ref, *refs):
    pieces, (qkv_ref, out_ref, rest_ref, all_ref) = refs[:-4], refs[-4:]
    rows = pieces[0].shape[0]
    for k, ref in enumerate(pieces):
        all_ref[pl.ds(pl.multiple_of(order_ref[k] * rows, rows), rows), :] = ref[...].astype(F32)
    first, second = qkv_ref.shape[0], qkv_ref.shape[0] + out_ref.shape[0]
    half = out_ref.shape[1]
    qkv_ref[...] = all_ref[:first]
    out_ref[...] = all_ref[first:second, :half]
    count = rest_ref.shape[0]
    rest_ref[...] = jnp.concatenate(
        [all_ref[first : first + count, half:], all_ref[first + count : first + 2 * count, half:]], axis=1
    )


def weight_unpack(order, pieces, half, own, count):
    rows, width = pieces[0].shape
    total = rows * len(pieces)
    shapes = [struct((half, width), F32), struct((own, half), F32), struct((count, half), F32)]
    return pl.pallas_call(
        weight_unpack_kernel,
        grid_spec=pltpu.PrefetchScalarGridSpec(
            num_scalar_prefetch=1,
            grid=(1,),
            in_specs=wholes(pieces),
            out_specs=[whole(v.shape) for v in shapes],
            scratch_shapes=[pltpu.VMEM((total, width), F32)],
        ),
        out_shape=shapes,
        compiler_params=params(),
        name="weight_unpack",
    )(order, *pieces)


def gelu_pair(pre):
    root = 0.7978845608028654
    cubic = 0.044715
    square = pre * pre
    th = jnp.tanh(root * pre * (1.0 + cubic * square))
    value = 0.5 * pre * (1.0 + th)
    slope = 0.5 * (1.0 + th) + 0.5 * pre * (1.0 - th * th) * root * (1.0 + 3.0 * cubic * square)
    return value, slope


def total_over(value, axis):
    for piece in gather_pieces(value, axis)[1:]:
        value = value + piece
    return value


def tie(*values):
    return lax.optimization_barrier(values)


def body(
    tokens, segment_ids, buckets, routes, kept, slots, cotangent, norm_one, norm_two,
    qkv_weight, out_weight, bias_table, router_weight, expert_in, expert_out,
):
    n_t = lax.axis_size("tensor")
    n_d = lax.axis_size("dp")
    me_t = lax.axis_index("tensor")
    me_d = lax.axis_index("dp")
    me_s = lax.axis_index("shard")
    length, width = tokens.shape
    heads = qkv_weight.shape[2] // DH
    own = heads * DH
    n_e = router_weight.shape[1]
    n_b = 2 * bias_table.shape[1]
    capacity = 5 * length // (4 * n_d)
    quarter = capacity // n_t
    rows_q = n_d * quarter
    parts = n_d if quarter % 16 == 0 else 1
    half = width // 2
    scalar = lambda v: v.astype(jnp.int32).reshape(1)

    me_td = jnp.stack([me_t, me_d]).astype(jnp.int32)

    out_all = lax.all_gather(out_weight, ("tensor", "shard"), axis=0, tiled=False)
    out_all = out_all.reshape(n_t, 2, own, half)
    split = expert_out.shape[1] // 2
    w_own = jnp.stack(
        [expert_in[0], jnp.concatenate([expert_out[0, :split], expert_out[0, split:]], axis=1)]
    )
    w_far = partner(w_own, "tensor", 2)
    w_other = partner(w_own, "shard", 1)
    order_d = (me_d ^ jnp.arange(n_d, dtype=jnp.int32)).astype(jnp.int32)
    order = (me_t ^ jnp.arange(n_t, dtype=jnp.int32)).astype(jnp.int32)
    table_row = jnp.pad(bias_table.reshape(1, -1), ((0, 0), (0, half - heads * (n_b // 2))))
    packed = jnp.concatenate([norm_one[None], norm_two[None], router_weight.T, table_row], axis=0)
    packed_far = partner(packed, "shard", 1)
    qkv_own = qkv_weight.reshape(half, 3 * own)
    qkv_far = partner(qkv_own, "shard", 1)

    place_row, place_abs, x_rows, g_send = slot_rows(
        me_td, routes, kept, slots, cotangent, tokens, quarter, n_t, rows_q, parts, 2 * rows_q // parts
    )
    if parts == 1:
        g_send = [g_send[0][k * 2 * quarter : (k + 1) * 2 * quarter] for k in range(n_d)]

    packed_far, qkv_far, x_rows, g_send = tie(packed_far, qkv_far, x_rows, g_send)
    g_pieces = swap_chunks(g_send, "dp")
    packed = jnp.where(
        me_s == 0,
        jnp.concatenate([packed, packed_far], axis=1),
        jnp.concatenate([packed_far, packed], axis=1),
    )
    gain_one = packed[:1].astype(F32)
    gain_two = packed[1:2].astype(F32)
    router = packed[2 : 2 + n_e]
    table = packed[2 + n_e].reshape(2, half)[:, : heads * (n_b // 2)]
    table = table.reshape(2, heads, n_b // 2).transpose(1, 0, 2).reshape(heads, n_b)

    inputs = tokens.astype(F32)
    normed_one, inv_one, projected, qkv_full = first_norm(scalar(me_s), tokens, gain_one, qkv_own, qkv_far)
    span = 2 * length
    onehot = (
        jnp.pad(buckets, (0, span - buckets.shape[0]), constant_values=-1)[None, :]
        == jnp.arange(n_b, dtype=jnp.int32)[:, None]
    )
    rel = jnp.pad(contract(table, onehot.astype(BF16), 1, 0), ((0, 8 - heads), (0, 0)))
    doc_row = segment_ids.reshape(1, length)
    attended, lse, *att_slots = attend_fwd(
        projected, rel, doc_row, place_row, heads, n_t, rows_q
    )
    attended, att_slots, g_pieces, w_far = tie(attended, att_slots, g_pieces, w_far)
    weights = (w_own, w_other, w_far, partner(w_far, "shard", 1))
    me_ds = jnp.stack([me_d, me_s]).astype(jnp.int32)

    att_rows = swap_chunks(att_slots, "tensor")
    att_ag, *att_rows = tie(attended, *att_rows)
    att_all = lax.all_gather(att_ag, "tensor", axis=0, tiled=False)
    unit_two, inv_two, sent = middle(scalar(me_t), att_rows, out_all, x_rows, gain_two, parts)

    if parts == 1:
        sent = [sent[0][k * quarter : (k + 1) * quarter] for k in range(n_d)]
    arrived = swap_chunks(sent, "dp")
    drop_att = jnp.where(
        (kept == 0)[:, None],
        contract(cotangent[:, :half], out_all[me_t, 0], 1, 1) + contract(cotangent[:, half:], out_all[me_t, 1], 1, 1),
        0.0,
    ).astype(BF16)
    far_first = partner(arrived[0], "tensor", 1) if parts > 1 else None
    drop_att, arrived, far_first = tie(drop_att, arrived, far_first)
    if parts == 1:
        arrived = [jnp.concatenate(arrived, axis=0)]
        g_own = [jnp.concatenate([p[:quarter] for p in g_send], axis=0)]
        g_sides = [
            [jnp.concatenate([p[r * quarter : (r + 1) * quarter] for p in g_pieces], axis=0)] for r in range(2)
        ]
        g_specs = [wholes(g) for g in g_sides]
    else:
        g_own = g_send
        g_sides = [g_pieces, g_pieces]
        at = lambda r: pl.BlockSpec((quarter, width), lambda i: (r, 0))
        g_specs = [[at(r)] * parts for r in range(2)]
    arrived_far = [partner(p, "tensor", 1) for p in arrived[parts > 1 :]]
    if parts > 1:
        arrived_far = [far_first] + arrived_far

    near = expert(me_ds, arrived, g_sides[0], g_specs[0], weights, router, F32)
    near, arrived_far = tie(near, arrived_far)
    far = expert(me_ds, arrived_far, g_sides[1], g_specs[1], weights, router, BF16)
    grad_far = partner(far[0][0], "tensor", 1)
    near, far, att_all = tie(near, far, att_all)
    late = expert_late(scalar(me_s), [near, far], weights)
    grad_far, late = tie(grad_far, late)
    (res_own, res_other, router_part), (near_in, near_out, far_own, others) = late
    res_far = partner(res_other, "tensor", 1)
    others = partner(others, "shard", 1)
    far_part = [(far_own[n] + others[2 + n].astype(F32)).astype(BF16) for n in range(2)]
    back = add_parts(near[0][0], grad_far, parts)
    if parts == 1:
        back = [back[0][k * quarter : (k + 1) * quarter] for k in range(n_d)]
    grad_two = swap_chunks(list(back), "dp")
    if parts == 1:
        grad_two = [jnp.concatenate(grad_two, axis=0)]

    grad_two, far_part = tie(grad_two, far_part)
    far_sum = [partner(v, "tensor", 2) for v in far_part]

    grad_mixed, gain_two_part, grad_att = second_norm_bwd(
        scalar(me_t), grad_two, g_own, g_specs[0], unit_two, inv_two, gain_two, out_all
    )
    grad_att_slots = swap_chunks(list(grad_att), "tensor")
    grad_mixed_ag, res_far, far_sum[0], *grad_att_slots = tie(grad_mixed, res_far, far_sum[0], *grad_att_slots)
    mixed_slots = lax.all_gather(grad_mixed_ag, "tensor", axis=0, tiled=True)
    res = list(add_parts(res_own, res_far, parts))
    if parts == 1:
        res = [res[0][k * quarter : (k + 1) * quarter] for k in range(n_d)]
    res = swap_chunks(res, "dp")

    grad_q, grad_kt, grad_vt, drel = attend_bwd(
        projected, rel, doc_row, lse, place_row, drop_att, grad_att_slots, heads
    )
    grad_q, grad_kt, grad_vt, drel, res, far_sum[1] = tie(grad_q, grad_kt, grad_vt, drel, res, far_sum[1])
    res_slots = lax.all_gather(jnp.concatenate(res, axis=0), "tensor", axis=0, tiled=True)
    grad_proj, gain_one_part, grad_one, sends = first_norm_bwd(
        order, grad_q, grad_kt, grad_vt, qkv_full, tokens, inv_one
    )
    sends, grad_proj = tie(sends, grad_proj)
    got = [partner(v, "tensor", k + 1) for k, v in enumerate(sends)]

    grad_table = jnp.dot(drel[:heads], onehot.astype(F32).T, precision=HIGH)
    small = jnp.concatenate([gain_one_part, gain_two_part, router_part], axis=0)
    n_small = 2 + n_e
    fill = -(n_small + 1) % 8
    total_rows = half + own + -(half + own) % (16 * n_d)
    table_row = grad_table.reshape(heads, 2, n_b // 2).transpose(1, 0, 2).reshape(1, 2, heads * n_b // 2)
    table_row = jnp.pad(table_row, ((0, fill), (0, 0), (0, half - heads * n_b // 2))).reshape(fill + 1, width)
    small = jnp.concatenate([small, table_row], axis=0)
    mixed_tok, total, theirs = weight_pack(
        scalar(me_s), place_abs, cotangent, attended, normed_one, grad_proj, small, [mixed_slots], total_rows
    )
    got, total, theirs, mixed_tok, far_sum = tie(got, total, theirs, mixed_tok, far_sum)
    theirs = partner(theirs, "shard", 1)
    delta = token_delta(order, tokens, inv_one, gain_one, grad_one, got)
    theirs, delta = tie(theirs, delta)
    delta_pieces = gather_pieces(delta, "tensor")
    total, sends = pair_sum(order_d, total, theirs)
    got = [partner(piece, "dp", k + 1) for k, piece in enumerate(sends)]
    grad_inw, grad_outw = grad_sum(near_in, near_out, others, far_sum)
    got, grad_inw, grad_outw = tie(got, grad_inw, grad_outw)
    for piece in got:
        total = total + piece.astype(F32)
    grad_tokens = place_chunks(order, mixed_tok, delta_pieces)
    pieces = gather_pieces(total.astype(BF16), "dp")
    pieces, grad_tokens = tie(pieces, grad_tokens)
    grad_qkv, grad_out, rest = weight_unpack(order_d, pieces, half, own, small.shape[0])
    small = total_over(rest[:n_small], "tensor")
    grad_table = rest[n_small, : heads * n_b // 2].reshape(heads, n_b // 2)

    output = layer_output(place_abs, tokens, att_all, out_all, res_slots)
    return (
        output,
        grad_tokens,
        small[0],
        small[1],
        grad_qkv.reshape(half, 3, own),
        grad_out,
        grad_table,
        small[2:].T,
        grad_inw[None],
        grad_outw[None],
    )


def solution(mesh):
    placed = (
        P(("dp", "shard"), None),
        P(("dp", "shard"), None),
        P(),
        P(("dp", "shard")),
        P(("dp", "shard")),
        P(("dp", "shard")),
        P(("dp", "shard"), None),
        P("shard"),
        P("shard"),
        P("shard", None, "tensor"),
        P("tensor", "shard"),
        P("tensor", "shard"),
        P("shard", None),
        P("dp", "shard", "tensor"),
        P("dp", "tensor", "shard"),
    )
    return jax.shard_map(
        body,
        mesh=mesh,
        in_specs=placed,
        out_specs=(
            P(("dp", "shard"), None),
            P(("dp", "shard"), None),
            P("shard"),
            P("shard"),
            P("shard", None, "tensor"),
            P("tensor", "shard"),
            P("tensor", "shard"),
            P("shard", None),
            P("dp", "shard", "tensor"),
            P("dp", "tensor", "shard"),
        ),
        check_vma=False,
    )
```
